32 devices in a mesh: sub: 8 (over z, x), layer: 4 (over y, core).
Axes of the slice: x: 2, y: 2, z: 4, core: 2. Of those that a mesh axis runs over, the one named last changes fastest.
Arguments:
- local_gap: float32 [8, 4, 1152, 128], P('sub', 'layer'), may hold values from -6 to 6
- route_codes: int32 [8, 4, 1152], P('sub', 'layer'), may hold values from 0 to 1152, as said below
- flexibility: float32 [8, 4, 1152, 1152], P('sub', 'layer'), may hold values from -1 to 3
- dirichlet: float32 [8, 4, 1152, 1152], P('sub', 'layer'), may hold values from -1 to 3
- rigid_modes: float32 [8, 4, 6, 1152], P('sub', 'layer'), may hold values from -6 to 6
- coarse_inverse: float32 [192, 192], P(('sub', 'layer')), may hold values from -1 to 1
- rigid_load: float32 [192, 128], P(('sub', 'layer')), may hold values from -360 to 360
Outputs:
- multipliers: float32 [8, 4, 1152, 128], P('sub', 'layer')
- residual: float32 [8, 4, 1152, 128], P('sub', 'layer')
The draws below stay inside these ranges and needn't reach their ends.
Inputs may be any that keep to these rules, and one draw needn't show every extreme that they name: `route_codes`: row r of subdomain (i, j) carries d * 288 + k when it is the k-th row it shares with neighbour d (0: sub index i - 1, 1: i + 1, 2: layer index j - 1, 3: j + 1); the row of that neighbour carrying e * 288 + k, e the opposite direction, is the same interface row. 4 * 288 marks a row shared with nobody. Neighbouring subdomains share between 144 and 288 rows, some pair exactly 288; there is no neighbour beyond the ends of an axis.
All inputs are finite; a program needn't handle non-finite values.
Results may differ from the reference program's by a relative error of at most 0.00017.
Values sent between devices are 32-bit elements; how exact they have to be, the bound alone decides.
No kernel may reach another device: no remote copies, remote signals or barrier semaphores. Data moves between devices by JAX's collectives and lax.ppermute only.
A program may use at most 128 MiB of HBM per device.

```python
import math
import jax
import jax.numpy as jnp
from jax import lax

NI = 1152
CAP = 288
MODES = 6
RHS = 128
SUBS = 8
LAYERS = 4
COARSE = 192


def permute_rows(row_seed):
    return jax.random.permutation(row_seed, 4 * CAP)


def interface_maps(key):
    across_key = jax.random.fold_in(key, 11)
    upward_key = jax.random.fold_in(key, 12)
    order_key = jax.random.fold_in(key, 13)
    across = jax.random.randint(across_key, (SUBS, LAYERS), CAP // 2, CAP + 1).astype(jnp.int32)
    across = across.at[0, 0].set(CAP)
    upward = jax.random.randint(upward_key, (SUBS, LAYERS), CAP // 2, CAP + 1).astype(jnp.int32)
    sub_index = jnp.arange(SUBS)[:, None]
    layer_index = jnp.arange(LAYERS)[None, :]
    left_count = jnp.where(sub_index > 0, jnp.roll(across, 1, 0), 0)
    right_count = jnp.where(sub_index < SUBS - 1, across, 0)
    lower_count = jnp.where(layer_index > 0, jnp.roll(upward, 1, 1), 0)
    upper_count = jnp.where(layer_index < LAYERS - 1, upward, 0)
    counts = jnp.stack([left_count, right_count, lower_count, upper_count], axis=-1)
    code_values = jnp.arange(4 * CAP, dtype=jnp.int32)
    valid_slot = (code_values % CAP)[None, None, :] < jnp.repeat(counts, CAP, axis=-1)
    slot_codes = jnp.where(valid_slot, code_values[None, None, :], 4 * CAP).astype(jnp.int32)
    device_keys = jax.random.split(order_key, SUBS * LAYERS)
    row_order = jax.vmap(permute_rows)(device_keys).reshape(SUBS, LAYERS, 4 * CAP)
    return (valid_slot, row_order, slot_codes)


def mode_codes(key):
    valid_slot, row_order, slot_codes = interface_maps(key)
    base_shape = (SUBS, LAYERS, CAP, MODES)
    noise_shape = (SUBS, LAYERS, 4 * CAP, MODES)
    across_base = jnp.clip(jax.random.normal(jax.random.fold_in(key, 21), base_shape, jnp.float32), -4.0, 4.0)
    upward_base = jnp.clip(jax.random.normal(jax.random.fold_in(key, 22), base_shape, jnp.float32), -4.0, 4.0)
    own_noise = 0.5 * jnp.clip(jax.random.normal(jax.random.fold_in(key, 23), noise_shape, jnp.float32), -4.0, 4.0)
    shared_base = jnp.concatenate([jnp.roll(across_base, 1, 0), across_base, jnp.roll(upward_base, 1, 1), upward_base], axis=2)
    mode_values = jnp.where(valid_slot[..., None], shared_base + own_noise, 0.0)
    return (row_order, mode_values)


def local_operator(key):
    full_shape = (SUBS, LAYERS, NI, NI)
    normal_draw = jnp.clip(jax.random.normal(jax.random.fold_in(key, 1), full_shape, jnp.float32), -6.0, 6.0)
    diagonal_values = jax.random.uniform(jax.random.fold_in(key, 2), (SUBS, LAYERS, NI), jnp.float32, 1.0, 2.0)
    symmetric = (normal_draw + jnp.swapaxes(normal_draw, 2, 3)) * (0.4 / math.sqrt(2.0 * NI))
    on_diagonal = jnp.arange(NI)[:, None] == jnp.arange(NI)[None, :]
    return symmetric + jnp.where(on_diagonal, diagonal_values[..., None], 0.0)


def draw_route_codes(key, part):
    valid_slot, row_order, slot_codes = interface_maps(key)
    return jnp.take_along_axis(slot_codes, row_order, axis=2).astype(jnp.int32)


def draw_flexibility(key, part):
    return local_operator(jax.random.fold_in(key, 31))


def draw_dirichlet(key, part):
    return local_operator(jax.random.fold_in(key, 41))


def draw_rigid_modes(key, part):
    row_order, mode_values = mode_codes(key)
    placed = jnp.take_along_axis(mode_values, row_order[..., None], axis=2)
    return jnp.transpose(placed, (0, 1, 3, 2))


def draw_coarse_inverse(key, part):
    full_shape = (COARSE, COARSE)
    raw_draw = jnp.clip(jax.random.normal(jax.random.fold_in(key, 51), full_shape, jnp.float32), -4.0, 4.0)
    dense_part = (raw_draw + raw_draw.T) * (0.25 / math.sqrt(2.0 * COARSE))
    row_scales = jax.random.uniform(jax.random.fold_in(key, 52), (COARSE,), jnp.float32, 0.75, 1.25) / (3.0 * CAP)
    root_scales = jnp.sqrt(row_scales)
    on_diagonal = jnp.arange(COARSE)[:, None] == jnp.arange(COARSE)[None, :]
    core = dense_part + jnp.where(on_diagonal, 1.0, 0.0)
    return root_scales[:, None] * root_scales[None, :] * core


def level_of(key, shape, cuts, low, largest):
    level = 1.0
    for position, shards_of in cuts:
        heights = jax.random.uniform(jax.random.fold_in(jax.random.fold_in(key, 6), position), (shards_of,), jnp.float32, low / len(cuts), largest / len(cuts))
        level = level * jnp.repeat(jnp.exp(heights), shape[position] // shards_of).reshape((-1,) + (1,) * (len(shape) - 1 - position))
    return level


def centred(key, dims, deviation, bound, shards=(), kind=jnp.bfloat16):
    drawn = jax.random.normal(key, dims, jnp.float32) * deviation
    if len(shards) > 0:
        drawn = level_of(key, dims, shards, -0.22, 0.18) * drawn
    return jnp.clip(drawn, min=-bound, max=bound).astype(kind)


def setup_inputs(seed: int = 0) -> dict:
    splits = jax.random.split(jax.random.key(seed), 8)
    return {
        "local_gap": centred(splits[0], (SUBS, LAYERS, NI, RHS), 1.0, 6.0, ((0, 8), (1, 4)), jnp.float32),
        "route_codes": draw_route_codes(jax.random.fold_in(splits[7], 71), 0),
        "flexibility": draw_flexibility(jax.random.fold_in(splits[7], 71), 0),
        "dirichlet": draw_dirichlet(jax.random.fold_in(splits[7], 71), 0),
        "rigid_modes": draw_rigid_modes(jax.random.fold_in(splits[7], 71), 0),
        "coarse_inverse": draw_coarse_inverse(jax.random.fold_in(splits[7], 71), 0),
        "rigid_load": centred(splits[6], (COARSE, RHS), 60.0, 360.0, ((0, 32),), jnp.float32),
    }


exact_mode = lax.Precision.HIGHEST
theta_mid = 4.25
delta_half = 3.75

def interface_jump(values, route_codes):
    live_rows = route_codes < 4 * CAP
    heading = jnp.minimum(route_codes // CAP, 3)
    slot_index = route_codes % CAP
    sub_index = jnp.arange(SUBS, dtype=jnp.int32)[:, None, None]
    layer_index = jnp.arange(LAYERS, dtype=jnp.int32)[None, :, None]
    row_index = jnp.arange(NI, dtype=jnp.int32)
    sub_step = jnp.where(heading == 0, -1, jnp.where(heading == 1, 1, 0)).astype(jnp.int32)
    layer_step = jnp.where(heading == 2, -1, jnp.where(heading == 3, 1, 0)).astype(jnp.int32)
    partner_sub = jnp.clip(sub_index + sub_step, 0, SUBS - 1).astype(jnp.int32)
    partner_layer = jnp.clip(layer_index + layer_step, 0, LAYERS - 1).astype(jnp.int32)
    opposite = heading + 1 - 2 * (heading % 2)
    row_table = jnp.zeros((SUBS, LAYERS, 4 * CAP + 1), jnp.int32)
    row_table = row_table.at[sub_index, layer_index, route_codes].set(jnp.broadcast_to(row_index, route_codes.shape).astype(jnp.int32))
    partner_row = row_table[partner_sub, partner_layer, (opposite * CAP + slot_index).astype(jnp.int32)]
    received = values[partner_sub, partner_layer, partner_row]
    return jnp.where(live_rows[..., None], values - received, 0.0)

def correction(coefficients, rigid_modes, route_codes):
    shaped = coefficients.reshape(SUBS, LAYERS, MODES, -1)
    traces = jnp.einsum('slkn,slkr->slnr', rigid_modes, shaped, precision=exact_mode)
    return interface_jump(traces, route_codes)

def project(values, rigid_modes, coarse_inverse, route_codes):
    components = jnp.einsum('slkn,slnr->slkr', rigid_modes, values, precision=exact_mode).reshape(COARSE, -1)
    coefficients = jnp.dot(coarse_inverse.astype(jnp.float32), components.astype(jnp.float32), precision=exact_mode, preferred_element_type=jnp.float32)
    return values - correction(coefficients, rigid_modes, route_codes)

def apply_local(matrix, values):
    return jnp.einsum('slij,sljr->slir', matrix, values, precision=exact_mode)

def reference(local_gap, route_codes, flexibility, dirichlet, rigid_modes, coarse_inverse, rigid_load):
    sigma_ratio = theta_mid / delta_half

    def operator(values):
        return project(interface_jump(apply_local(flexibility, values), route_codes), rigid_modes, coarse_inverse, route_codes)

    def precond(values):
        return project(0.5 * interface_jump(apply_local(dirichlet, values), route_codes), rigid_modes, coarse_inverse, route_codes)
    gap_jump = interface_jump(local_gap, route_codes)
    start = correction(jnp.dot(coarse_inverse.astype(jnp.float32), rigid_load.astype(jnp.float32), precision=exact_mode, preferred_element_type=jnp.float32), rigid_modes, route_codes)
    residual = project(gap_jump - interface_jump(apply_local(flexibility, start), route_codes), rigid_modes, coarse_inverse, route_codes)
    step_value = precond(residual) / theta_mid
    damping = delta_half / theta_mid
    multipliers = start + step_value
    residual = residual - operator(step_value)
    damping_next = 1.0 / (2.0 * sigma_ratio - damping)
    step_value = damping_next * damping * step_value + 2.0 * damping_next / delta_half * precond(residual)
    multipliers = multipliers + step_value
    residual = residual - operator(step_value)
    return (multipliers, residual)
```

```python
import functools

import jax
import jax.numpy as jnp
from jax import lax
from jax.experimental import pallas as pl
from jax.experimental.pallas import tpu as pltpu
from jax.sharding import PartitionSpec as P

theta_mid = 4.25
delta_half = 3.75
sigma_ratio = theta_mid / delta_half
damping = delta_half / theta_mid
damping_next = 1.0 / (2.0 * sigma_ratio - damping)
keep_step = damping_next * damping
new_step = 2.0 * damping_next / delta_half

GROUP = 32
PAD = 8
SIDES = 4


def exact(a, b, contract=((1,), (0,))):
    return lax.dot_general(
        a,
        b,
        (contract, ((), ())),
        precision=lax.Precision.HIGHEST,
        preferred_element_type=jnp.float32,
    )


def one_pass(a, b):
    return jnp.dot(a, b, preferred_element_type=jnp.float32)


def two_pieces(x):
    high = x.astype(jnp.bfloat16)
    low = (x - high.astype(jnp.float32)).astype(jnp.bfloat16)
    return high, low


def slot_by_row(codes_row, start, rows):
    slots = lax.broadcasted_iota(jnp.int32, (rows, codes_row.shape[1]), 0) + start
    return jnp.where(slots == codes_row, 1.0, 0.0).astype(jnp.bfloat16)


def row_by_slot(codes_lanes, slots):
    rows, lanes = codes_lanes.shape
    lane = lax.broadcasted_iota(jnp.int32, (rows, lanes), 1)
    parts = [
        jnp.where(lane + first == codes_lanes, 1.0, 0.0).astype(jnp.bfloat16)
        for first in range(0, slots, lanes)
    ]
    return jnp.concatenate(parts, axis=1)


def fill_pieces(pieces, start, x):
    high, low = two_pieces(x)
    cols = x.shape[1]
    pieces[pl.ds(start, x.shape[0]), 0:cols] = high
    pieces[pl.ds(start, x.shape[0]), cols : 2 * cols] = low


def to_rows(codes_lanes, slot_pieces, write):
    total = slot_pieces.shape[0]
    chunk = total // SIDES
    for c in range(SIDES):
        pick = row_by_slot(codes_lanes[c * chunk : (c + 1) * chunk, :], total)
        write(c * chunk, one_pass(pick, slot_pieces[...]))


def halves(x):
    cols = x.shape[1] // 2
    return x[:, :cols] + x[:, cols:]


def apply_local(matrix, codes_row, codes_lanes, slot_pieces, row_pieces, out_pieces, write):
    total = slot_pieces.shape[0]
    chunk = total // SIDES
    cols = slot_pieces.shape[1] // 2

    def keep(start, rows):
        row_pieces[start : start + chunk, :] = rows.astype(jnp.bfloat16)

    to_rows(codes_lanes, slot_pieces, keep)
    for c in range(SIDES):
        high, low = two_pieces(matrix[c * chunk : (c + 1) * chunk, :])
        product = halves(one_pass(high, row_pieces[...])) + one_pass(low, row_pieces[:, :cols])
        fill_pieces(out_pieces, c * chunk, product)
    for side in range(SIDES):
        pick = slot_by_row(codes_row[...], side * chunk, chunk)
        write(side, halves(one_pass(pick, out_pieces[...])))


def copies(ref, block):
    rows = block.shape[0]
    for q in range(ref.shape[0] // rows):
        ref[q * rows : (q + 1) * rows, :] = block


def in_slots(x, codes_row, side, cap):
    high = x.astype(jnp.bfloat16)
    rest = x - high.astype(jnp.float32)
    middle = rest.astype(jnp.bfloat16)
    low = (rest - middle.astype(jnp.float32)).astype(jnp.bfloat16)
    pick = slot_by_row(codes_row, side * cap, cap)
    cols = x.shape[1]
    moved = one_pass(pick, jnp.concatenate([high, middle, low], axis=1))
    return moved[:, :cols] + moved[:, cols : 2 * cols] + moved[:, 2 * cols :]


def modes_kernel(mode_count, codes_lanes, modes, inverse, load, *outs):
    total = codes_lanes.shape[0]
    cap = total // SIDES
    x = jnp.concatenate(
        [modes[...], jnp.zeros((PAD - mode_count, total), jnp.float32)], axis=0
    )
    high = x.astype(jnp.bfloat16).astype(jnp.float32)
    middle = (x - high).astype(jnp.bfloat16).astype(jnp.float32)
    low = x - high - middle
    pieces = jnp.concatenate([high, middle, low, jnp.zeros_like(low)], axis=0).astype(jnp.bfloat16)
    pick = row_by_slot(codes_lanes[...], total)
    moved = one_pass(pieces, pick)
    moved = moved[0:PAD] + moved[PAD : 2 * PAD] + moved[2 * PAD : 3 * PAD]
    for side in range(SIDES):
        outs[side][...] = moved[:, side * cap : (side + 1) * cap]
    coarse = inverse.shape[1]
    padded = coarse // mode_count * PAD
    old = lax.broadcasted_iota(jnp.int32, (coarse, padded), 0)
    new = lax.broadcasted_iota(jnp.int32, (coarse, padded), 1)
    spread = jnp.where((old // mode_count) * PAD + old % mode_count == new, 1.0, 0.0)
    blank = jnp.zeros((PAD - mode_count, coarse), jnp.float32)
    wide = exact(jnp.concatenate([inverse[...], blank], axis=0), spread)
    blank = jnp.zeros((PAD - mode_count, load.shape[1]), jnp.float32)
    loads = jnp.concatenate([load[...], blank], axis=0)
    copies(outs[SIDES], jnp.concatenate([wide, loads], axis=1))


def gap_kernel(codes_row, gap, out):
    cap = gap.shape[0] // SIDES
    for side in range(SIDES):
        out[side * cap : (side + 1) * cap, :] = in_slots(gap[...], codes_row[...], side, cap)


def around(place, layers):
    return [place, place - layers, place + layers, place - 1, place + 1]


def mode_blocks(mode_count, own, partner):
    cap = own[0].shape[1]
    rows = []
    for side in range(SIDES):
        column = [own[side][...]]
        for other in range(SIDES):
            if other == side:
                column.append(-partner[side][...])
            else:
                column.append(jnp.zeros((PAD, cap), jnp.float32))
        rows.append(jnp.concatenate(column, axis=0))
    return rows


def lane_spread(mode_count, copies_wanted):
    shape = (PAD * (SIDES + 1), 4 * GROUP)
    old = lax.broadcasted_iota(jnp.int32, shape, 0)
    new = lax.broadcasted_iota(jnp.int32, shape, 1)
    spot = (old // PAD) * mode_count + old % PAD
    match = (spot == new % GROUP) & (old % PAD < mode_count) & (new < GROUP * copies_wanted)
    return jnp.where(match, 1.0, 0.0)


def start_kernel(mode_count, layers, gap_slots, flex, codes_row, codes_lanes, *refs):
    own, partner = refs[0:4], refs[4:8]
    gathered, place_ref = refs[8], refs[9]
    outs = refs[10:14]
    start_out, modes_out, inverse_out = refs[14:17]
    slot_pieces, row_pieces, out_pieces = refs[17:20]
    total = codes_lanes.shape[0]
    cap = total // SIDES
    wide = gathered.shape[0]
    place = place_ref[0]
    lanes = 4 * GROUP
    spread_all = lane_spread(mode_count, 4)
    for n, centre in enumerate(around(place, layers)):
        rows = []
        for near in around(centre, layers):
            first = jnp.clip(near, 0, wide // PAD - 1) * PAD
            rows.append(gathered[pl.ds(pl.multiple_of(first, PAD), PAD), 0:wide])
        table = jnp.concatenate(rows, axis=0)
        inverse_out[n * lanes : (n + 1) * lanes, :] = exact(spread_all, table, ((0,), (0,)))
    coefficients = exact(inverse_out[0:lanes, :], gathered[:, wide:])
    spread = lane_spread(mode_count, 1)
    for side, block in enumerate(mode_blocks(mode_count, own, partner)):
        rows = slice(side * cap, (side + 1) * cap)
        placed = exact(block, spread, ((0,), (0,)))
        modes_out[rows, :] = placed
        start = exact(placed, coefficients)
        start_out[rows, :] = start
        fill_pieces(slot_pieces, side * cap, start)

    def write(side, block):
        outs[side][...] = gap_slots[side * cap : (side + 1) * cap, :] - block

    apply_local(flex, codes_row, codes_lanes, slot_pieces, row_pieces, out_pieces, write)


def operators_kernel(mode_count, flex, schur, codes_row, codes_lanes, *refs):
    own, partner = refs[0:4], refs[4:8]
    outs = refs[8:12]
    slot_pieces, row_pieces, out_pieces = refs[12:15]
    total = codes_lanes.shape[0]
    cap = total // SIDES
    half = cap // 2
    spread = lane_spread(mode_count, 4)
    for side, block in enumerate(mode_blocks(mode_count, own, partner)):
        fill_pieces(slot_pieces, side * cap, exact(block, spread, ((0,), (0,))))
    group = lax.broadcasted_iota(jnp.int32, (half, 4 * GROUP), 1) // GROUP

    def write_schur(side, block):
        outs[side][...] = jnp.where(group == 0, block[:half], block[half:])

    def write_flex(side, block):
        mine = jnp.where(group == 2, block[:half], block[half:])
        outs[side][...] = jnp.where(group < 2, outs[side][...], mine)

    apply_local(schur, codes_row, codes_lanes, slot_pieces, row_pieces, out_pieces, write_schur)
    apply_local(flex, codes_row, codes_lanes, slot_pieces, row_pieces, out_pieces, write_flex)


def components_of(own, blocks):
    total = exact(own[0][...], blocks[0])
    for side in range(1, SIDES):
        total = total + exact(own[side][...], blocks[side])
    return total


def grouped(slab, first):
    group = lax.broadcasted_iota(jnp.int32, slab.shape, 1) // GROUP
    upper = jnp.where(group == first, slab, 0.0)
    lower = jnp.where(group == first + 1, slab, 0.0)
    return jnp.concatenate([upper, lower], axis=0)


def lagged(side, first, mine, theirs, coefficients):
    lanes = 4 * GROUP
    left = jnp.concatenate([grouped(mine[...], first), grouped(theirs[...], first)], axis=1)
    right = jnp.concatenate(
        [
            coefficients[0:lanes],
            -coefficients[(side + 1) * lanes : (side + 2) * lanes],
        ],
        axis=0,
    )
    return exact(left, right)


def first_kernel(schur, codes_row, codes_lanes, *refs):
    received, sent, own, slabs = refs[0:4], refs[4:8], refs[8:12], refs[12:16]
    outs = refs[16:20]
    gap_out, parts_out = refs[20:22]
    slot_pieces, row_pieces, out_pieces = refs[22:25]
    cap = own[0].shape[1]
    blocks = []
    for side in range(SIDES):
        block = sent[side][...] - received[side][...]
        gap_out[side * cap : (side + 1) * cap, :] = block
        fill_pieces(slot_pieces, side * cap, block)
        blocks.append(block)
        outs[side][cap:, :] = slabs[side][...]
    copies(parts_out, components_of(own, blocks))

    def write(side, block):
        outs[side][0:cap, :] = block

    apply_local(schur, codes_row, codes_lanes, slot_pieces, row_pieces, out_pieces, write)


def stage_kernel(stage, flags, matrix, codes_row, codes_lanes, *refs):
    refs = list(refs)

    def take(count):
        taken = refs[:count]
        del refs[:count]
        return taken

    received, sent, own = take(4), take(4), take(4)
    mine, theirs = (sent, received) if stage == 2 else (take(4), take(4))
    gathered, inverse_rows, modes = take(3)
    states_in = take(flags["states_in"])
    outs = take(4) if matrix is not None else []
    states_out = take(flags["states_out"])
    (parts_out,) = take(1)
    slot_pieces, row_pieces, out_pieces = take(3)
    cap = own[0].shape[1]
    lanes = 4 * GROUP
    coefficients = exact(inverse_rows[...], gathered[...])
    blocks = []
    for side in range(SIDES):
        rows = slice(side * cap, (side + 1) * cap)
        jump = sent[side][0:cap, :] - received[side][0:cap, :]
        tail = pl.ds(cap, cap // 2) if stage == 2 else slice(None)
        first = 0 if stage in (2, 4) else 2
        behind = lagged(side, first, mine[side].at[tail], theirs[side].at[tail], coefficients)
        direct = exact(modes[rows, :], coefficients[0:lanes])
        if stage == 2:
            (gap,) = states_in
            block = 0.5 * (jump - behind)
            nextin = block
            states_out[0][rows, :] = block
            states_out[1][rows, :] = gap[rows, :] - direct
        elif stage == 3:
            precond, residual = states_in
            block = (jump - behind) / theta_mid
            nextin = residual[rows, :] - block
            states_out[0][rows, :] = nextin
            states_out[1][rows, :] = (precond[rows, :] - direct) / theta_mid
        elif stage == 4:
            residual, step = states_in
            block = 0.5 * (jump + behind)
            nextin = keep_step * step[rows, :] + new_step * block
            states_out[0][rows, :] = residual[rows, :] + direct
            states_out[1][rows, :] = nextin
        else:
            residual, raw_step, start, step = states_in
            block = jump - new_step * behind
            states_out[0][rows, :] = residual[rows, :] - block
            nextin = raw_step[rows, :] - new_step * direct + start[rows, :] + step[rows, :]
        fill_pieces(slot_pieces, side * cap, nextin)
        blocks.append(block)
    copies(parts_out, components_of(own, blocks))
    if matrix is not None:

        def write(side, block):
            outs[side][...] = block

        apply_local(matrix, codes_row, codes_lanes, slot_pieces, row_pieces, out_pieces, write)
    else:

        def keep(begin, rows):
            states_out[1][begin : begin + cap, :] = halves(rows)

        to_rows(codes_lanes, slot_pieces, keep)


def last_kernel(codes_lanes, residual, modes, gathered, inverse_rows, out, slot_pieces):
    cap = residual.shape[0] // SIDES
    lanes = 4 * GROUP
    coefficients = exact(inverse_rows[0:lanes, :], gathered[...])
    fill_pieces(slot_pieces, 0, residual[...] + exact(modes[...], coefficients))

    def keep(begin, rows):
        out[begin : begin + cap, :] = halves(rows)

    to_rows(codes_lanes, slot_pieces, keep)


def call(kernel, name, outs, inputs, scratch=(), smem=()):
    vmem = pl.BlockSpec(memory_space=pltpu.VMEM)
    scalar = pl.BlockSpec(memory_space=pltpu.SMEM)
    return pl.pallas_call(
        kernel,
        name=name,
        out_shape=[jax.ShapeDtypeStruct(shape, jnp.float32) for shape in outs],
        in_specs=[scalar if n in smem else vmem for n in range(len(inputs))],
        out_specs=[vmem] * len(outs),
        scratch_shapes=list(scratch),
        compiler_params=pltpu.CompilerParams(vmem_limit_bytes=56 * 1024 * 1024),
    )(*inputs)


def exchange(blocks):
    received = []
    for side in range(SIDES):
        axis = "sub" if side < 2 else "layer"
        count = lax.axis_size(axis)
        if side % 2 == 0:
            pairs = [(i, i + 1) for i in range(count - 1)]
        else:
            pairs = [(i + 1, i) for i in range(count - 1)]
        received.append(lax.ppermute(blocks[side + 1 - 2 * (side % 2)], axis, pairs))
    return received


def everywhere(stacked):
    return lax.all_to_all(stacked, ("sub", "layer"), split_axis=0, concat_axis=0, tiled=True)


def per_device(
    local_gap, route_codes, flexibility, dirichlet, rigid_modes, coarse_inverse, rigid_load
):
    gap_local = local_gap[0, 0]
    flex = flexibility[0, 0]
    schur = dirichlet[0, 0]
    modes = rigid_modes[0, 0]
    mode_count, total = modes.shape
    cap = total // SIDES
    cols = gap_local.shape[1]
    codes_row = route_codes[0]
    codes_lanes = jnp.broadcast_to(route_codes[0, 0][:, None], (total, 128))
    layers = lax.axis_size("layer")
    devices = lax.axis_size("sub") * layers
    wide = devices * PAD
    place = (lax.axis_index("sub") * layers + lax.axis_index("layer")).astype(jnp.int32)[None]
    pieces = pltpu.VMEM((total, 2 * cols), jnp.bfloat16)
    scratch = [pieces] * 3
    block = [(cap, cols)] * SIDES
    whole = (total, cols)
    parts = (wide, cols)

    *own, inverse_load = call(
        functools.partial(modes_kernel, mode_count),
        "modes_to_slots",
        [(PAD, cap)] * SIDES + [(wide, wide + cols)],
        [codes_lanes, modes, coarse_inverse, rigid_load],
    )
    partner = exchange(own)
    gathered = everywhere(inverse_load)
    (gap_slots,) = call(gap_kernel, "gap_to_slots", [whole], [codes_row, gap_local])
    shown = call(
        functools.partial(start_kernel, mode_count, layers),
        "start",
        block + [whole, (total, 4 * GROUP), (5 * 4 * GROUP, wide)],
        [gap_slots, flex, codes_row, codes_lanes, *own, *partner, gathered, place],
        scratch,
        smem=(13,),
    )
    sent, (start, slot_modes, inverse_rows) = shown[:4], shown[4:]
    received = exchange(sent)
    slabs = call(
        functools.partial(operators_kernel, mode_count),
        "operators_on_modes",
        [(cap // 2, 4 * GROUP)] * SIDES,
        [flex, schur, codes_row, codes_lanes, *own, *partner],
        scratch,
    )
    shown = call(
        first_kernel,
        "stage_1",
        [(cap + cap // 2, cols)] * SIDES + [whole, parts],
        [schur, codes_row, codes_lanes, *received, *sent, *own, *slabs],
        scratch,
    )
    sent, (gap_jump, components) = shown[:4], shown[4:]
    slab_sent = sent

    def stage(number, matrix, states_in, states_out, sent, received, extra, components):
        kernel = functools.partial(
            stage_kernel, number, {"states_in": len(states_in), "states_out": states_out}
        )
        inputs = [codes_row, codes_lanes, *received, *sent, *own, *extra]
        inputs += [components, inverse_rows, slot_modes, *states_in]
        outs = [whole] * states_out + [parts]
        if matrix is None:
            kernel = functools.partial(kernel, None)
        else:
            inputs, outs = [matrix] + inputs, block + outs
        return call(kernel, "stage_%d" % number, outs, inputs, scratch)

    received = exchange(sent)
    slab_received = received
    components = everywhere(components)
    shown = stage(2, flex, [gap_jump], 2, sent, received, [], components)
    sent, (precond, residual, components) = shown[:4], shown[4:]
    extra = [x[cap:] for x in slab_sent] + [x[cap:] for x in slab_received]

    received = exchange(sent)
    components = everywhere(components)
    shown = stage(3, schur, [precond, residual], 2, sent, received, extra, components)
    sent, (residual, step, components) = shown[:4], shown[4:]

    received = exchange(sent)
    components = everywhere(components)
    shown = stage(4, flex, [residual, step], 2, sent, received, extra, components)
    sent, (residual, raw_step, components) = shown[:4], shown[4:]

    received = exchange(sent)
    components = everywhere(components)
    shown = stage(5, None, [residual, raw_step, start, step], 2, sent, received, extra, components)
    residual, multipliers, components = shown

    components = everywhere(components)
    (residual,) = call(
        last_kernel,
        "residual_to_rows",
        [whole],
        [codes_lanes, residual, slot_modes, components, inverse_rows],
        [pieces],
    )
    return (multipliers[None, None], residual[None, None])


def solution(mesh):
    placed = (
        P("sub", "layer", None, None),
        P("sub", "layer", None),
        P("sub", "layer", None, None),
        P("sub", "layer", None, None),
        P("sub", "layer", None, None),
        P(("sub", "layer"), None),
        P(("sub", "layer"), None),
    )
    return jax.shard_map(
        per_device,
        mesh=mesh,
        in_specs=placed,
        out_specs=(P("sub", "layer", None, None), P("sub", "layer", None, None)),
        check_vma=False,
    )
```

```python
import functools

import jax
import jax.numpy as jnp
from jax import lax
from jax.experimental import pallas as pl
from jax.experimental.pallas import tpu as pltpu
from jax.sharding import PartitionSpec as P

theta_mid = 4.25
delta_half = 3.75
sigma_ratio = theta_mid / delta_half
damping = delta_half / theta_mid
damping_next = 1.0 / (2.0 * sigma_ratio - damping)
keep_step = damping_next * damping
new_step = 2.0 * damping_next / delta_half

GROUP = 32
PAD = 8
SIDES = 4


def exact(a, b, contract=((1,), (0,))):
    return lax.dot_general(
        a,
        b,
        (contract, ((), ())),
        precision=lax.Precision.HIGHEST,
        preferred_element_type=jnp.float32,
    )


def one_pass(a, b):
    return jnp.dot(a, b, preferred_element_type=jnp.float32)


def two_pieces(x):
    high = x.astype(jnp.bfloat16)
    low = (x - high.astype(jnp.float32)).astype(jnp.bfloat16)
    return high, low


def slot_by_row(codes_row, start, rows):
    slots = lax.broadcasted_iota(jnp.int32, (rows, codes_row.shape[1]), 0) + start
    return jnp.where(slots == codes_row, 1.0, 0.0).astype(jnp.bfloat16)


def row_by_slot(codes_lanes, slots):
    rows, lanes = codes_lanes.shape
    lane = lax.broadcasted_iota(jnp.int32, (rows, lanes), 1)
    parts = [
        jnp.where(lane + first == codes_lanes, 1.0, 0.0).astype(jnp.bfloat16)
        for first in range(0, slots, lanes)
    ]
    return jnp.concatenate(parts, axis=1)


def fill_pieces(pieces, start, x):
    high, low = two_pieces(x)
    cols = x.shape[1]
    pieces[pl.ds(start, x.shape[0]), 0:cols] = high
    pieces[pl.ds(start, x.shape[0]), cols : 2 * cols] = low


def to_rows(codes_lanes, slot_pieces, write):
    total = slot_pieces.shape[0]
    chunk = total // SIDES
    for c in range(SIDES):
        pick = row_by_slot(codes_lanes[c * chunk : (c + 1) * chunk, :], total)
        write(c * chunk, one_pass(pick, slot_pieces[...]))


def halves(x):
    cols = x.shape[1] // 2
    return x[:, :cols] + x[:, cols:]


def apply_local(matrix, codes_row, codes_lanes, slot_pieces, row_pieces, out_pieces, write, less=None):
    total = slot_pieces.shape[0]
    chunk = total // SIDES

    def keep(start, rows):
        row_pieces[start : start + chunk, :] = rows.astype(jnp.bfloat16)

    to_rows(codes_lanes, slot_pieces, keep)
    apply_rows(matrix, codes_row, row_pieces, out_pieces, write, less)


def apply_rows(matrix, codes_row, row_pieces, out_pieces, write, less=None):
    total = row_pieces.shape[0]
    chunk = total // SIDES
    cols = row_pieces.shape[1] // 2
    for c in range(SIDES):
        high, low = two_pieces(matrix[c * chunk : (c + 1) * chunk, :])
        product = halves(one_pass(high, row_pieces[...])) + one_pass(low, row_pieces[:, :cols])
        if less is not None:
            product = less[c * chunk : (c + 1) * chunk, :] - product
        fill_pieces(out_pieces, c * chunk, product)
    for side in range(SIDES):
        pick = slot_by_row(codes_row[...], side * chunk, chunk)
        write(side, halves(one_pass(pick, out_pieces[...])))


def three_pass(a, b):
    a_high, a_low = two_pieces(a)
    b_high, b_low = two_pieces(b)
    both = jnp.concatenate([b_high, b_low], axis=1)
    return halves(one_pass(a_high, both)) + one_pass(a_low, b_high)


def modes_kernel(mode_count, codes_row, modes, inverse, load, *outs):
    total = codes_row.shape[1]
    cap = total // SIDES
    codes = jnp.broadcast_to(codes_row[...], (128, total)).astype(jnp.float32)
    codes_lanes = jnp.transpose(codes).astype(jnp.int32)
    x = jnp.concatenate(
        [modes[...], jnp.zeros((PAD - mode_count, total), jnp.float32)], axis=0
    )
    high = x.astype(jnp.bfloat16).astype(jnp.float32)
    middle = (x - high).astype(jnp.bfloat16).astype(jnp.float32)
    low = x - high - middle
    pieces = jnp.concatenate([high, middle, low, jnp.zeros_like(low)], axis=0).astype(jnp.bfloat16)
    moved = one_pass(pieces, row_by_slot(codes_lanes, total))
    upper, lower = moved[0:PAD], moved[PAD : 2 * PAD]
    moved = upper + lower + moved[2 * PAD : 3 * PAD]
    for side in range(SIDES):
        outs[side][...] = moved[:, side * cap : (side + 1) * cap]
    coarse = inverse.shape[1]
    padded = coarse // mode_count * PAD
    old = lax.broadcasted_iota(jnp.int32, (coarse, padded), 0)
    new = lax.broadcasted_iota(jnp.int32, (coarse, padded), 1)
    spread = jnp.where((old // mode_count) * PAD + old % mode_count == new, 1.0, 0.0)
    blank = jnp.zeros((PAD - mode_count, coarse), jnp.float32)
    wide = exact(jnp.concatenate([inverse[...], blank], axis=0), spread)
    blank = jnp.zeros((PAD - mode_count, load.shape[1]), jnp.float32)
    loads = jnp.concatenate([load[...], blank], axis=0)
    outs[SIDES][...] = jnp.concatenate([wide, loads], axis=1)
    outs[SIDES + 1][...] = codes_lanes
    outs[SIDES + 2][...] = jnp.concatenate([upper, lower], axis=0)


def around(place, layers):
    return [place, place - layers, place + layers, place - 1, place + 1]


def mode_blocks(own, partner):
    cap = own[0].shape[1]
    rows = []
    for side in range(SIDES):
        column = [own[side][...]]
        for other in range(SIDES):
            if other == side:
                column.append(-partner[side][...])
            else:
                column.append(jnp.zeros((PAD, cap), jnp.float32))
        rows.append(jnp.concatenate(column, axis=0))
    return rows


def lane_spread(mode_count, lanes):
    shape = (PAD * (SIDES + 1), lanes)
    old = lax.broadcasted_iota(jnp.int32, shape, 0)
    new = lax.broadcasted_iota(jnp.int32, shape, 1)
    spot = (old // PAD) * mode_count + old % PAD
    match = (spot == new % GROUP) & (old % PAD < mode_count)
    return jnp.where(match, 1.0, 0.0)


def operators_kernel(mode_count, flex, schur, codes_row, codes_lanes, *refs):
    own, partner = refs[0:4], refs[4:8]
    outs = refs[8:12]
    modes_out = refs[12]
    slot_pieces, row_pieces, out_pieces = refs[13:16]
    total = codes_lanes.shape[0]
    cap = total // SIDES
    half = cap // 2
    lanes = 4 * GROUP
    spread = lane_spread(mode_count, lanes)
    for side, block in enumerate(mode_blocks(own, partner)):
        placed = exact(block, spread, ((0,), (0,)))
        first = lax.broadcasted_iota(jnp.int32, placed.shape, 1) < GROUP
        modes_out[side * cap : (side + 1) * cap, :] = jnp.where(first, placed, 0.0)
        fill_pieces(slot_pieces, side * cap, placed)
    group = lax.broadcasted_iota(jnp.int32, (half, lanes), 1) // GROUP

    def write_schur(side, block):
        outs[side][...] = jnp.where(group == 0, block[:half], block[half:])

    def write_flex(side, block):
        mine = jnp.where(group == 2, block[:half], block[half:])
        outs[side][...] = jnp.where(group < 2, outs[side][...], mine)

    apply_local(schur, codes_row, codes_lanes, slot_pieces, row_pieces, out_pieces, write_schur)
    apply_rows(flex, codes_row, row_pieces, out_pieces, write_flex)


def start_kernel(mode_count, layers, flex, gap, codes_row, codes_lanes, *refs):
    slabs = refs[0:4]
    gathered, modes, place_ref = refs[4:7]
    outs = refs[7:11]
    start_out, inverse_out = refs[11:13]
    slot_pieces, row_pieces, out_pieces = refs[13:16]
    cap = codes_lanes.shape[0] // SIDES
    wide = gathered.shape[0]
    place = place_ref[0]
    spread = lane_spread(mode_count, GROUP)
    for n, centre in enumerate(around(place, layers)):
        rows = []
        for near in around(centre, layers):
            first = jnp.clip(near, 0, wide // PAD - 1) * PAD
            rows.append(gathered[pl.ds(pl.multiple_of(first, PAD), PAD), 0:wide])
        table = jnp.concatenate(rows, axis=0)
        inverse_out[n * GROUP : (n + 1) * GROUP, :] = exact(spread, table, ((0,), (0,)))
    coefficients = repeated(exact(inverse_out[0:GROUP, :], gathered[:, wide:]))
    start = three_pass(modes[...], coefficients)
    start_out[...] = start
    fill_pieces(slot_pieces, 0, start)

    def write(side, block):
        outs[side][0:cap, :] = block
        outs[side][cap:, :] = slabs[side][...]

    apply_local(flex, codes_row, codes_lanes, slot_pieces, row_pieces, out_pieces, write, gap)


def repeated(x):
    return jnp.concatenate([x] * 4, axis=0)


def components_of(own_pieces, block_pieces):
    both = one_pass(own_pieces[...].astype(jnp.bfloat16), block_pieces[...])
    cols = both.shape[1] // 2
    return halves(both[0:PAD]) + both[PAD:, :cols]


def grouped(slab, first):
    group = lax.broadcasted_iota(jnp.int32, slab.shape, 1) // GROUP
    upper = jnp.where(group == first, slab, 0.0)
    lower = jnp.where(group == first + 1, slab, 0.0)
    return jnp.concatenate([upper, lower], axis=0)


def lagged(side, first, mine, theirs, coefficients):
    left = jnp.concatenate([grouped(mine[...], first), grouped(theirs[...], first)], axis=1)
    near = coefficients[(side + 1) * GROUP : (side + 2) * GROUP]
    return three_pass(left, jnp.concatenate([repeated(coefficients[0:GROUP]), repeated(-near)], axis=0))


def first_kernel(schur, codes_row, codes_lanes, *refs):
    received, sent, own = refs[0:4], refs[4:8], refs[8]
    outs = refs[9:13]
    gap_out, parts_out = refs[13:15]
    slot_pieces, row_pieces, out_pieces = refs[15:18]
    cap = codes_lanes.shape[0] // SIDES
    for side in range(SIDES):
        block = sent[side][0:cap, :] - received[side][0:cap, :]
        gap_out[side * cap : (side + 1) * cap, :] = block
        fill_pieces(slot_pieces, side * cap, block)
    parts_out[...] = components_of(own, slot_pieces)

    def write(side, block):
        outs[side][...] = block

    apply_local(schur, codes_row, codes_lanes, slot_pieces, row_pieces, out_pieces, write)


def stage_kernel(stage, counts, matrix, codes_row, codes_lanes, *refs):
    refs = list(refs)

    def take(count):
        taken = refs[:count]
        del refs[:count]
        return taken

    received, sent, mine, theirs = take(4), take(4), take(4), take(4)
    own, gathered, inverse_rows, modes = take(4)
    states_in = take(counts[0])
    outs = take(4) if stage < 5 else []
    states_out = take(counts[1])
    (parts_out,) = take(1)
    slot_pieces, row_pieces, out_pieces = take(3)
    total = codes_lanes.shape[0]
    cap = total // SIDES
    coefficients = exact(inverse_rows[...], gathered[...])
    direct_all = three_pass(modes[...], repeated(coefficients[0:GROUP]))
    tail = pl.ds(cap, cap // 2)
    for side in range(SIDES):
        rows = slice(side * cap, (side + 1) * cap)
        jump = sent[side][...] - received[side][...]
        first = 0 if stage in (2, 4) else 2
        behind = lagged(side, first, mine[side].at[tail], theirs[side].at[tail], coefficients)
        direct = direct_all[rows, :]
        nextin = None
        if stage == 2:
            (gap,) = states_in
            block = 0.5 * (jump - behind)
            nextin = block
            states_out[0][rows, :] = block
            states_out[1][rows, :] = gap[rows, :] - direct
        elif stage == 3:
            precond, residual = states_in
            block = (jump - behind) / theta_mid
            nextin = residual[rows, :] - block
            states_out[0][rows, :] = nextin
            states_out[1][rows, :] = (precond[rows, :] - direct) / theta_mid
        elif stage == 4:
            residual, step = states_in
            block = 0.5 * (jump + behind)
            nextin = keep_step * step[rows, :] + new_step * block
            states_out[0][rows, :] = residual[rows, :] + direct
            states_out[1][rows, :] = nextin
        else:
            residual, raw_step, start, step = states_in
            block = jump - new_step * behind
            states_out[0][rows, :] = residual[rows, :] - block
            second = raw_step[rows, :] - new_step * direct
            states_out[1][rows, :] = second + start[rows, :] + step[rows, :]
        if nextin is not None:
            fill_pieces(slot_pieces, side * cap, nextin)
        fill_pieces(out_pieces, side * cap, block)
    parts_out[...] = components_of(own, out_pieces)
    if stage < 5:

        def write(side, block):
            outs[side][...] = block

        apply_local(matrix, codes_row, codes_lanes, slot_pieces, row_pieces, out_pieces, write)


def rows_kernel(codes_lanes, residual, multipliers, modes, residual_out, multipliers_out, modes_out, pieces):
    total = residual.shape[0]
    cap = total // SIDES
    for n, source in enumerate((residual, multipliers, modes)):
        high, low = two_pieces(source[...])
        pieces[:, 256 * n : 256 * n + 128] = high
        pieces[:, 256 * n + 128 : 256 * (n + 1)] = low

    def keep(begin, rows):
        for n, target in enumerate((residual_out, multipliers_out, modes_out)):
            target[begin : begin + cap, :] = halves(rows[:, 256 * n : 256 * (n + 1)])

    to_rows(codes_lanes, pieces, keep)


def last_kernel(residual, modes, gathered, inverse_rows, out):
    coefficients = repeated(exact(inverse_rows[0:GROUP, :], gathered[...]))
    out[...] = residual[...] + three_pass(modes[...], coefficients)


def call(kernel, name, outs, inputs, scratch=(), smem=(), extra=0):
    vmem = pl.BlockSpec(memory_space=pltpu.VMEM)
    scalar = pl.BlockSpec(memory_space=pltpu.SMEM)
    return pl.pallas_call(
        kernel,
        name=name,
        out_shape=[jax.ShapeDtypeStruct(shape, jnp.float32) if isinstance(shape, tuple) else shape for shape in outs],
        in_specs=[scalar if n in smem else vmem for n in range(len(inputs))],
        out_specs=[vmem] * len(outs),
        scratch_shapes=list(scratch),
        compiler_params=pltpu.CompilerParams(vmem_limit_bytes=28 * 1024 * 1024 + extra),
    )(*inputs)


def exchange(blocks):
    received = []
    for side in range(SIDES):
        axis = "sub" if side < 2 else "layer"
        count = lax.axis_size(axis)
        if side % 2 == 0:
            pairs = [(i, i + 1) for i in range(count - 1)]
        else:
            pairs = [(i + 1, i) for i in range(count - 1)]
        received.append(lax.ppermute(blocks[side + 1 - 2 * (side % 2)], axis, pairs))
    return received


def everywhere(block):
    return lax.all_gather(block, ("sub", "layer"), axis=0, tiled=True)


def per_device(
    local_gap, route_codes, flexibility, dirichlet, rigid_modes, coarse_inverse, rigid_load
):
    gap = local_gap[0, 0]
    flex = flexibility[0, 0]
    schur = dirichlet[0, 0]
    modes = rigid_modes[0, 0]
    mode_count, total = modes.shape
    cap = total // SIDES
    cols = gap.shape[1]
    codes_row = route_codes[0]
    layers = lax.axis_size("layer")
    wide = lax.axis_size("sub") * layers * PAD
    place = (lax.axis_index("sub") * layers + lax.axis_index("layer")).astype(jnp.int32)[None]
    pieces = pltpu.VMEM((total, 2 * cols), jnp.bfloat16)
    scratch = [pieces] * 3
    block = [(cap, cols)] * SIDES
    whole = (total, cols)
    parts = (PAD, cols)
    table = 8 * wide * (wide + cols)

    shown = call(
        functools.partial(modes_kernel, mode_count),
        "modes_to_slots",
        [(PAD, cap)] * SIDES
        + [(PAD, wide + cols), jax.ShapeDtypeStruct((total, 128), jnp.int32), (2 * PAD, total)],
        [codes_row, modes, coarse_inverse, rigid_load],
        extra=table,
    )
    own, (inverse_load, codes_lanes, own_pieces) = shown[:4], shown[4:]
    gathered = everywhere(inverse_load)
    partner = exchange(own)
    shown = call(
        functools.partial(operators_kernel, mode_count),
        "operators_on_modes",
        [(cap // 2, 4 * GROUP)] * SIDES + [(total, 4 * GROUP)],
        [flex, schur, codes_row, codes_lanes, *own, *partner],
        scratch,
    )
    slabs, slot_modes = shown[:4], shown[4]
    shown = call(
        functools.partial(start_kernel, mode_count, layers),
        "start",
        [(cap + cap // 2, cols)] * SIDES + [whole, (5 * GROUP, wide)],
        [flex, gap, codes_row, codes_lanes, *slabs, gathered, slot_modes, place],
        scratch,
        smem=(10,),
        extra=table,
    )
    sent, (start, inverse_rows) = shown[:4], shown[4:]
    received = exchange(sent)
    slab_sent, slab_received = sent, received
    shown = call(
        first_kernel,
        "stage_1",
        block + [whole, parts],
        [schur, codes_row, codes_lanes, *received, *sent, own_pieces],
        scratch,
    )
    sent, (gap_jump, components) = shown[:4], shown[4:]

    def stage(number, matrix, states_in, sent, components):
        gathered = everywhere(components)
        received = exchange(sent)
        inputs = [codes_row, codes_lanes, *received, *sent, *slab_sent, *slab_received]
        inputs += [own_pieces, gathered, inverse_rows, slot_modes, *states_in]
        outs = [whole] * 2 + [parts]
        kernel = functools.partial(stage_kernel, number, (len(states_in), 2))
        if matrix is None:
            kernel = functools.partial(kernel, None)
        else:
            inputs, outs = [matrix] + inputs, block + outs
        return call(kernel, "stage_%d" % number, outs, inputs, scratch)

    shown = stage(2, flex, [gap_jump], sent, components)
    sent, (precond, residual, components) = shown[:4], shown[4:]
    shown = stage(3, schur, [precond, residual], sent, components)
    sent, (residual, step, components) = shown[:4], shown[4:]
    shown = stage(4, flex, [residual, step], sent, components)
    sent, (residual, raw_step, components) = shown[:4], shown[4:]
    shown = stage(5, None, [residual, raw_step, start, step], sent, components)
    residual, multipliers, components = shown

    gathered = everywhere(components)
    residual, multipliers, row_modes = call(
        rows_kernel,
        "slots_to_rows",
        [whole, whole, (total, 4 * GROUP)],
        [codes_lanes, residual, multipliers, slot_modes],
        [pltpu.VMEM((total, 768), jnp.bfloat16)],
    )
    (residual,) = call(
        last_kernel, "residual", [whole], [residual, row_modes, gathered, inverse_rows]
    )
    return (multipliers[None, None], residual[None, None])


def solution(mesh):
    placed = (
        P("sub", "layer", None, None),
        P("sub", "layer", None),
        P("sub", "layer", None, None),
        P("sub", "layer", None, None),
        P("sub", "layer", None, None),
        P(("sub", "layer"), None),
        P(("sub", "layer"), None),
    )
    return jax.shard_map(
        per_device,
        mesh=mesh,
        in_specs=placed,
        out_specs=(P("sub", "layer", None, None), P("sub", "layer", None, None)),
        check_vma=False,
    )
```

```python
import functools

import jax
import jax.numpy as jnp
from jax import lax
from jax.experimental import pallas as pl
from jax.experimental.pallas import tpu as pltpu
from jax.sharding import PartitionSpec as P

theta_mid = 4.25
delta_half = 3.75
sigma_ratio = theta_mid / delta_half
damping = delta_half / theta_mid
damping_next = 1.0 / (2.0 * sigma_ratio - damping)
keep_step = damping_next * damping
new_step = 2.0 * damping_next / delta_half

GROUP = 32
PAD = 8
SIDES = 4


def exact(a, b, contract=((1,), (0,))):
    return lax.dot_general(
        a,
        b,
        (contract, ((), ())),
        precision=lax.Precision.HIGHEST,
        preferred_element_type=jnp.float32,
    )


def one_pass(a, b):
    return jnp.dot(a, b, preferred_element_type=jnp.float32)


def two_pieces(x):
    high = x.astype(jnp.bfloat16)
    low = (x - high.astype(jnp.float32)).astype(jnp.bfloat16)
    return high, low


def slot_by_row(codes_row, start, rows):
    slots = lax.broadcasted_iota(jnp.int32, (rows, codes_row.shape[1]), 0) + start
    return jnp.where(slots == codes_row, 1.0, 0.0).astype(jnp.bfloat16)


def row_by_slot(codes_lanes, slots):
    rows, lanes = codes_lanes.shape
    lane = lax.broadcasted_iota(jnp.int32, (rows, lanes), 1)
    parts = [
        jnp.where(lane + first == codes_lanes, 1.0, 0.0).astype(jnp.bfloat16)
        for first in range(0, slots, lanes)
    ]
    return jnp.concatenate(parts, axis=1)


def fill_pieces(pieces, start, x):
    high, low = two_pieces(x)
    cols = x.shape[1]
    pieces[pl.ds(start, x.shape[0]), 0:cols] = high
    pieces[pl.ds(start, x.shape[0]), cols : 2 * cols] = low


def to_rows(codes_lanes, slot_pieces, write):
    total = slot_pieces.shape[0]
    chunk = total // SIDES
    for c in range(SIDES):
        pick = row_by_slot(codes_lanes[c * chunk : (c + 1) * chunk, :], total)
        write(c * chunk, one_pass(pick, slot_pieces[...]))


def halves(x):
    cols = x.shape[1] // 2
    return x[:, :cols] + x[:, cols:]


def apply_local(matrix, codes_row, codes_lanes, slot_pieces, row_pieces, out_pieces, write, less=None):
    total = slot_pieces.shape[0]
    chunk = total // SIDES

    def keep(start, rows):
        row_pieces[start : start + chunk, :] = rows.astype(jnp.bfloat16)

    to_rows(codes_lanes, slot_pieces, keep)
    apply_rows(matrix, codes_row, row_pieces, out_pieces, write, less)


def apply_rows(matrix, codes_row, row_pieces, out_pieces, write, less=None):
    total = row_pieces.shape[0]
    chunk = total // SIDES
    cols = row_pieces.shape[1] // 2
    for c in range(SIDES):
        high, low = two_pieces(matrix[c * chunk : (c + 1) * chunk, :])
        product = halves(one_pass(high, row_pieces[...])) + one_pass(low, row_pieces[:, :cols])
        if less is not None:
            product = less[c * chunk : (c + 1) * chunk, :] - product
        fill_pieces(out_pieces, c * chunk, product)
    for side in range(SIDES):
        pick = slot_by_row(codes_row[...], side * chunk, chunk)
        write(side, halves(one_pass(pick, out_pieces[...])))


def three_pass(a, b):
    a_high, a_low = two_pieces(a)
    b_high, b_low = two_pieces(b)
    both = jnp.concatenate([b_high, b_low], axis=1)
    return halves(one_pass(a_high, both)) + one_pass(a_low, b_high)


def copies(ref, block):
    rows = block.shape[0]
    for q in range(ref.shape[0] // rows):
        ref[q * rows : (q + 1) * rows, :] = block


def modes_kernel(mode_count, codes_row, modes, inverse, load, place, *outs):
    total = codes_row.shape[1]
    cap = total // SIDES
    codes = codes_row[...]
    heading = codes // cap
    even = jnp.where(heading < 2, 1 - lax.rem(place[0], 2), 1 - lax.rem(place[1], 2))
    turn = jnp.where(heading < SIDES, even * (1 - 2 * (heading % 2)), 0)
    codes = codes + turn * cap
    outs[SIDES + 3][...] = codes
    codes = jnp.broadcast_to(codes, (128, total)).astype(jnp.float32)
    codes_lanes = jnp.transpose(codes).astype(jnp.int32)
    x = jnp.concatenate(
        [modes[...], jnp.zeros((PAD - mode_count, total), jnp.float32)], axis=0
    )
    high = x.astype(jnp.bfloat16).astype(jnp.float32)
    middle = (x - high).astype(jnp.bfloat16).astype(jnp.float32)
    low = x - high - middle
    pieces = jnp.concatenate([high, middle, low, jnp.zeros_like(low)], axis=0).astype(jnp.bfloat16)
    moved = one_pass(pieces, row_by_slot(codes_lanes, total))
    upper, lower = moved[0:PAD], moved[PAD : 2 * PAD]
    moved = upper + lower + moved[2 * PAD : 3 * PAD]
    for side in range(SIDES):
        outs[side][...] = moved[:, side * cap : (side + 1) * cap]
    coarse = inverse.shape[1]
    padded = coarse // mode_count * PAD
    old = lax.broadcasted_iota(jnp.int32, (coarse, padded), 0)
    new = lax.broadcasted_iota(jnp.int32, (coarse, padded), 1)
    spread = jnp.where((old // mode_count) * PAD + old % mode_count == new, 1.0, 0.0)
    blank = jnp.zeros((PAD - mode_count, coarse), jnp.float32)
    wide = exact(jnp.concatenate([inverse[...], blank], axis=0), spread)
    blank = jnp.zeros((PAD - mode_count, load.shape[1]), jnp.float32)
    loads = jnp.concatenate([load[...], blank], axis=0)
    copies(outs[SIDES], jnp.concatenate([wide, loads], axis=1))
    outs[SIDES + 1][...] = codes_lanes
    outs[SIDES + 2][...] = jnp.concatenate([upper, lower], axis=0)


def around(i, j):
    right, up = 1 - 2 * (i % 2), 1 - 2 * (j % 2)
    return [(i, j), (i + right, j), (i - right, j), (i, j + up), (i, j - up)]


def mode_blocks(own, partner):
    cap = own[0].shape[1]
    rows = []
    for side in range(SIDES):
        column = [own[side][...]]
        for other in range(SIDES):
            if other == side:
                column.append(-partner[side][...])
            else:
                column.append(jnp.zeros((PAD, cap), jnp.float32))
        rows.append(jnp.concatenate(column, axis=0))
    return rows


def lane_spread(mode_count, lanes):
    shape = (PAD * (SIDES + 1), lanes)
    old = lax.broadcasted_iota(jnp.int32, shape, 0)
    new = lax.broadcasted_iota(jnp.int32, shape, 1)
    spot = (old // PAD) * mode_count + old % PAD
    match = (spot == new % GROUP) & (old % PAD < mode_count)
    return jnp.where(match, 1.0, 0.0)


def operators_kernel(mode_count, flex, schur, codes_row, codes_lanes, *refs):
    own, partner = refs[0:4], refs[4:8]
    outs = refs[8:12]
    modes_out = refs[12]
    slot_pieces, row_pieces, out_pieces = refs[13:16]
    total = codes_lanes.shape[0]
    cap = total // SIDES
    half = cap // 2
    lanes = 4 * GROUP
    spread = lane_spread(mode_count, lanes)
    for side, block in enumerate(mode_blocks(own, partner)):
        placed = exact(block, spread, ((0,), (0,)))
        first = lax.broadcasted_iota(jnp.int32, placed.shape, 1) < GROUP
        modes_out[side * cap : (side + 1) * cap, :] = jnp.where(first, placed, 0.0)
        fill_pieces(slot_pieces, side * cap, placed)
    group = lax.broadcasted_iota(jnp.int32, (half, lanes), 1) // GROUP

    def write_schur(side, block):
        outs[side][...] = jnp.where(group == 0, block[:half], block[half:])

    def write_flex(side, block):
        mine = jnp.where(group == 2, block[:half], block[half:])
        outs[side][...] = jnp.where(group < 2, outs[side][...], mine)

    apply_local(schur, codes_row, codes_lanes, slot_pieces, row_pieces, out_pieces, write_schur)
    apply_rows(flex, codes_row, row_pieces, out_pieces, write_flex)


def start_kernel(mode_count, layers, flex, gap, codes_row, codes_lanes, *refs):
    slabs = refs[0:4]
    gathered, modes, place_ref = refs[4:7]
    outs = refs[7:11]
    start_out, inverse_out = refs[11:13]
    slot_pieces, row_pieces, out_pieces = refs[13:16]
    cap = codes_lanes.shape[0] // SIDES
    wide = gathered.shape[0]
    spread = lane_spread(mode_count, GROUP)
    for n, centre in enumerate(around(place_ref[0], place_ref[1])):
        rows = []
        for i, j in around(*centre):
            first = jnp.clip(i * layers + j, 0, wide // PAD - 1) * PAD
            rows.append(gathered[pl.ds(pl.multiple_of(first, PAD), PAD), 0:wide])
        table = jnp.concatenate(rows, axis=0)
        inverse_out[n * GROUP : (n + 1) * GROUP, :] = exact(spread, table, ((0,), (0,)))
    coefficients = repeated(exact(inverse_out[0:GROUP, :], gathered[:, wide:]))
    start = three_pass(modes[...], coefficients)
    start_out[...] = start
    fill_pieces(slot_pieces, 0, start)

    def write(side, block):
        outs[side][0:cap, :] = block
        outs[side][cap:, :] = slabs[side][...]

    apply_local(flex, codes_row, codes_lanes, slot_pieces, row_pieces, out_pieces, write, gap)


def repeated(x):
    return jnp.concatenate([x] * 4, axis=0)


def components_of(own_pieces, block_pieces):
    both = one_pass(own_pieces[...].astype(jnp.bfloat16), block_pieces[...])
    cols = both.shape[1] // 2
    return halves(both[0:PAD]) + both[PAD:, :cols]


def grouped(slab, first):
    group = lax.broadcasted_iota(jnp.int32, slab.shape, 1) // GROUP
    upper = jnp.where(group == first, slab, 0.0)
    lower = jnp.where(group == first + 1, slab, 0.0)
    return jnp.concatenate([upper, lower], axis=0)


def lagged(side, first, mine, theirs, coefficients):
    left = jnp.concatenate([grouped(mine[...], first), grouped(theirs[...], first)], axis=1)
    near = coefficients[(side + 1) * GROUP : (side + 2) * GROUP]
    return three_pass(left, jnp.concatenate([repeated(coefficients[0:GROUP]), repeated(-near)], axis=0))


def first_kernel(schur, codes_row, codes_lanes, *refs):
    received, sent, own = refs[0:4], refs[4:8], refs[8]
    outs = refs[9:13]
    gap_out, parts_out = refs[13:15]
    slot_pieces, row_pieces, out_pieces = refs[15:18]
    cap = codes_lanes.shape[0] // SIDES
    for side in range(SIDES):
        block = sent[side][0:cap, :] - received[side][0:cap, :]
        gap_out[side * cap : (side + 1) * cap, :] = block
        fill_pieces(slot_pieces, side * cap, block)
    copies(parts_out, components_of(own, slot_pieces))

    def write(side, block):
        outs[side][...] = block

    apply_local(schur, codes_row, codes_lanes, slot_pieces, row_pieces, out_pieces, write)


def stage_kernel(stage, counts, matrix, codes_row, codes_lanes, *refs):
    refs = list(refs)

    def take(count):
        taken = refs[:count]
        del refs[:count]
        return taken

    received, sent, mine, theirs = take(4), take(4), take(4), take(4)
    own, gathered, inverse_rows, modes = take(4)
    states_in = take(counts[0])
    outs = take(4) if stage < 5 else []
    states_out = take(counts[1])
    (parts_out,) = take(1)
    slot_pieces, row_pieces, out_pieces = take(3)
    total = codes_lanes.shape[0]
    cap = total // SIDES
    coefficients = exact(inverse_rows[...], gathered[...])
    direct_all = three_pass(modes[...], repeated(coefficients[0:GROUP]))
    tail = pl.ds(cap, cap // 2)
    for side in range(SIDES):
        rows = slice(side * cap, (side + 1) * cap)
        jump = sent[side][...] - received[side][...]
        first = 0 if stage in (2, 4) else 2
        behind = lagged(side, first, mine[side].at[tail], theirs[side].at[tail], coefficients)
        direct = direct_all[rows, :]
        nextin = None
        if stage == 2:
            (gap,) = states_in
            block = 0.5 * (jump - behind)
            nextin = block
            states_out[0][rows, :] = block
            states_out[1][rows, :] = gap[rows, :] - direct
        elif stage == 3:
            precond, residual = states_in
            block = (jump - behind) / theta_mid
            nextin = residual[rows, :] - block
            states_out[0][rows, :] = nextin
            states_out[1][rows, :] = (precond[rows, :] - direct) / theta_mid
        elif stage == 4:
            residual, step = states_in
            block = 0.5 * (jump + behind)
            nextin = keep_step * step[rows, :] + new_step * block
            states_out[0][rows, :] = residual[rows, :] + direct
            states_out[1][rows, :] = nextin
        else:
            residual, raw_step, start, step = states_in
            block = jump - new_step * behind
            states_out[0][rows, :] = residual[rows, :] - block
            second = raw_step[rows, :] - new_step * direct
            states_out[1][rows, :] = second + start[rows, :] + step[rows, :]
        if nextin is not None:
            fill_pieces(slot_pieces, side * cap, nextin)
        fill_pieces(out_pieces, side * cap, block)
    copies(parts_out, components_of(own, out_pieces))
    if stage < 5:

        def write(side, block):
            outs[side][...] = block

        apply_local(matrix, codes_row, codes_lanes, slot_pieces, row_pieces, out_pieces, write)


def rows_kernel(codes_lanes, residual, multipliers, modes, residual_out, multipliers_out, modes_out, pieces):
    total = residual.shape[0]
    cap = total // SIDES
    for n, source in enumerate((residual, multipliers, modes)):
        high, low = two_pieces(source[...])
        pieces[:, 256 * n : 256 * n + 128] = high
        pieces[:, 256 * n + 128 : 256 * (n + 1)] = low

    def keep(begin, rows):
        for n, target in enumerate((residual_out, multipliers_out, modes_out)):
            target[begin : begin + cap, :] = halves(rows[:, 256 * n : 256 * (n + 1)])

    to_rows(codes_lanes, pieces, keep)


def last_kernel(residual, modes, gathered, inverse_rows, out):
    coefficients = repeated(exact(inverse_rows[0:GROUP, :], gathered[...]))
    out[...] = residual[...] + three_pass(modes[...], coefficients)


def call(kernel, name, outs, inputs, scratch=(), smem=(), extra=0):
    vmem = pl.BlockSpec(memory_space=pltpu.VMEM)
    scalar = pl.BlockSpec(memory_space=pltpu.SMEM)
    return pl.pallas_call(
        kernel,
        name=name,
        out_shape=[jax.ShapeDtypeStruct(shape, jnp.float32) if isinstance(shape, tuple) else shape for shape in outs],
        in_specs=[scalar if n in smem else vmem for n in range(len(inputs))],
        out_specs=[vmem] * len(outs),
        scratch_shapes=list(scratch),
        compiler_params=pltpu.CompilerParams(vmem_limit_bytes=28 * 1024 * 1024 + extra),
    )(*inputs)


def exchange(blocks):
    received = []
    for side, block in enumerate(blocks):
        axis = "sub" if side < 2 else "layer"
        pairs = []
        for i in range(side % 2, lax.axis_size(axis) - 1, 2):
            pairs += [(i, i + 1), (i + 1, i)]
        received.append(lax.ppermute(block, axis, pairs))
    return received


def everywhere(stacked):
    return lax.all_to_all(stacked, ("sub", "layer"), split_axis=0, concat_axis=0, tiled=True)


def per_device(
    local_gap, route_codes, flexibility, dirichlet, rigid_modes, coarse_inverse, rigid_load
):
    gap = local_gap[0, 0]
    flex = flexibility[0, 0]
    schur = dirichlet[0, 0]
    modes = rigid_modes[0, 0]
    mode_count, total = modes.shape
    cap = total // SIDES
    cols = gap.shape[1]
    layers = lax.axis_size("layer")
    wide = lax.axis_size("sub") * layers * PAD
    place = jnp.stack([lax.axis_index("sub"), lax.axis_index("layer")]).astype(jnp.int32)
    pieces = pltpu.VMEM((total, 2 * cols), jnp.bfloat16)
    scratch = [pieces] * 3
    block = [(cap, cols)] * SIDES
    whole = (total, cols)
    parts = (wide, cols)
    table = 8 * wide * (wide + cols)

    shown = call(
        functools.partial(modes_kernel, mode_count),
        "modes_to_slots",
        [(PAD, cap)] * SIDES
        + [(wide, wide + cols), jax.ShapeDtypeStruct((total, 128), jnp.int32), (2 * PAD, total)]
        + [jax.ShapeDtypeStruct((1, total), jnp.int32)],
        [route_codes[0], modes, coarse_inverse, rigid_load, place],
        smem=(4,),
        extra=table,
    )
    own, (inverse_load, codes_lanes, own_pieces, codes_row) = shown[:4], shown[4:]
    gathered = everywhere(inverse_load)
    partner = exchange(own)
    shown = call(
        functools.partial(operators_kernel, mode_count),
        "operators_on_modes",
        [(cap // 2, 4 * GROUP)] * SIDES + [(total, 4 * GROUP)],
        [flex, schur, codes_row, codes_lanes, *own, *partner],
        scratch,
    )
    slabs, slot_modes = shown[:4], shown[4]
    shown = call(
        functools.partial(start_kernel, mode_count, layers),
        "start",
        [(cap + cap // 2, cols)] * SIDES + [whole, (5 * GROUP, wide)],
        [flex, gap, codes_row, codes_lanes, *slabs, gathered, slot_modes, place],
        scratch,
        smem=(10,),
        extra=table,
    )
    sent, (start, inverse_rows) = shown[:4], shown[4:]
    received = exchange(sent)
    slab_sent, slab_received = sent, received
    shown = call(
        first_kernel,
        "stage_1",
        block + [whole, parts],
        [schur, codes_row, codes_lanes, *received, *sent, own_pieces],
        scratch,
    )
    sent, (gap_jump, components) = shown[:4], shown[4:]

    def stage(number, matrix, states_in, sent, components):
        gathered = everywhere(components)
        received = exchange(sent)
        inputs = [codes_row, codes_lanes, *received, *sent, *slab_sent, *slab_received]
        inputs += [own_pieces, gathered, inverse_rows, slot_modes, *states_in]
        outs = [whole] * 2 + [parts]
        kernel = functools.partial(stage_kernel, number, (len(states_in), 2))
        if matrix is None:
            kernel = functools.partial(kernel, None)
        else:
            inputs, outs = [matrix] + inputs, block + outs
        return call(kernel, "stage_%d" % number, outs, inputs, scratch)

    shown = stage(2, flex, [gap_jump], sent, components)
    sent, (precond, residual, components) = shown[:4], shown[4:]
    shown = stage(3, schur, [precond, residual], sent, components)
    sent, (residual, step, components) = shown[:4], shown[4:]
    shown = stage(4, flex, [residual, step], sent, components)
    sent, (residual, raw_step, components) = shown[:4], shown[4:]
    shown = stage(5, None, [residual, raw_step, start, step], sent, components)
    residual, multipliers, components = shown

    gathered = everywhere(components)
    residual, multipliers, row_modes = call(
        rows_kernel,
        "slots_to_rows",
        [whole, whole, (total, 4 * GROUP)],
        [codes_lanes, residual, multipliers, slot_modes],
        [pltpu.VMEM((total, 768), jnp.bfloat16)],
    )
    (residual,) = call(
        last_kernel, "residual", [whole], [residual, row_modes, gathered, inverse_rows]
    )
    return (multipliers[None, None], residual[None, None])


def solution(mesh):
    placed = (
        P("sub", "layer", None, None),
        P("sub", "layer", None),
        P("sub", "layer", None, None),
        P("sub", "layer", None, None),
        P("sub", "layer", None, None),
        P(("sub", "layer"), None),
        P(("sub", "layer"), None),
    )
    return jax.shard_map(
        per_device,
        mesh=mesh,
        in_specs=placed,
        out_specs=(P("sub", "layer", None, None), P("sub", "layer", None, None)),
        check_vma=False,
    )
```

```python
import functools

import jax
import jax.numpy as jnp
from jax import lax
from jax.experimental import pallas as pl
from jax.experimental.pallas import tpu as pltpu
from jax.sharding import PartitionSpec as P

theta_mid = 4.25
delta_half = 3.75
sigma_ratio = theta_mid / delta_half
damping = delta_half / theta_mid
damping_next = 1.0 / (2.0 * sigma_ratio - damping)
keep_step = damping_next * damping
new_step = 2.0 * damping_next / delta_half

GROUP = 32
PAD = 8
SIDES = 4


def exact(a, b, contract=((1,), (0,))):
    return lax.dot_general(
        a,
        b,
        (contract, ((), ())),
        precision=lax.Precision.HIGHEST,
        preferred_element_type=jnp.float32,
    )


def one_pass(a, b):
    return jnp.dot(a, b, preferred_element_type=jnp.float32)


def two_pieces(x):
    high = x.astype(jnp.bfloat16)
    low = (x - high.astype(jnp.float32)).astype(jnp.bfloat16)
    return high, low


def slot_by_row(codes_row, start, rows):
    slots = lax.broadcasted_iota(jnp.int32, (rows, codes_row.shape[1]), 0) + start
    return jnp.where(slots == codes_row, 1.0, 0.0).astype(jnp.bfloat16)


def row_by_slot(codes_lanes, slots):
    rows, lanes = codes_lanes.shape
    lane = lax.broadcasted_iota(jnp.int32, (rows, lanes), 1)
    parts = [
        jnp.where(lane + first == codes_lanes, 1.0, 0.0).astype(jnp.bfloat16)
        for first in range(0, slots, lanes)
    ]
    return jnp.concatenate(parts, axis=1)


def fill_pieces(pieces, start, x):
    high, low = two_pieces(x)
    cols = x.shape[1]
    pieces[pl.ds(start, x.shape[0]), 0:cols] = high
    pieces[pl.ds(start, x.shape[0]), cols : 2 * cols] = low


def to_rows(codes_lanes, slot_pieces, write):
    total = slot_pieces.shape[0]
    chunk = total // SIDES
    for c in range(SIDES):
        pick = row_by_slot(codes_lanes[c * chunk : (c + 1) * chunk, :], total)
        write(c * chunk, one_pass(pick, slot_pieces[...]))


def halves(x):
    cols = x.shape[1] // 2
    return x[:, :cols] + x[:, cols:]


def apply_local(matrix, codes_row, codes_lanes, slot_pieces, row_pieces, out_pieces, write, less=None):
    total = slot_pieces.shape[0]
    chunk = total // SIDES

    def keep(start, rows):
        row_pieces[start : start + chunk, :] = rows.astype(jnp.bfloat16)

    to_rows(codes_lanes, slot_pieces, keep)
    apply_rows(matrix, codes_row, row_pieces, out_pieces, write, less)


def apply_rows(matrix, codes_row, row_pieces, out_pieces, write, less=None):
    total = row_pieces.shape[0]
    chunk = total // SIDES
    cols = row_pieces.shape[1] // 2
    for c in range(SIDES):
        high, low = two_pieces(matrix[c * chunk : (c + 1) * chunk, :])
        product = halves(one_pass(high, row_pieces[...])) + one_pass(low, row_pieces[:, :cols])
        if less is not None:
            product = less[c * chunk : (c + 1) * chunk, :] - product
        fill_pieces(out_pieces, c * chunk, product)
    for side in range(SIDES):
        pick = slot_by_row(codes_row[...], side * chunk, chunk)
        write(side, halves(one_pass(pick, out_pieces[...])))


def three_pass(a, b):
    a_high, a_low = two_pieces(a)
    b_high, b_low = two_pieces(b)
    both = jnp.concatenate([b_high, b_low], axis=1)
    return halves(one_pass(a_high, both)) + one_pass(a_low, b_high)


def copies(ref, block):
    rows = block.shape[0]
    for q in range(ref.shape[0] // rows):
        ref[q * rows : (q + 1) * rows, :] = block


def modes_kernel(mode_count, codes_row, modes, inverse, load, place, *outs):
    total = codes_row.shape[1]
    cap = total // SIDES
    codes = codes_row[...]
    heading = codes // cap
    even = jnp.where(heading < 2, 1 - lax.rem(place[0], 2), 1 - lax.rem(place[1], 2))
    turn = jnp.where(heading < SIDES, even * (1 - 2 * (heading % 2)), 0)
    codes = codes + turn * cap
    outs[SIDES + 3][...] = codes
    codes = jnp.broadcast_to(codes, (128, total)).astype(jnp.float32)
    codes_lanes = jnp.transpose(codes).astype(jnp.int32)
    x = jnp.concatenate(
        [modes[...], jnp.zeros((PAD - mode_count, total), jnp.float32)], axis=0
    )
    high = x.astype(jnp.bfloat16).astype(jnp.float32)
    middle = (x - high).astype(jnp.bfloat16).astype(jnp.float32)
    low = x - high - middle
    pieces = jnp.concatenate([high, middle, low, jnp.zeros_like(low)], axis=0).astype(jnp.bfloat16)
    moved = one_pass(pieces, row_by_slot(codes_lanes, total))
    upper, lower = moved[0:PAD], moved[PAD : 2 * PAD]
    moved = upper + lower + moved[2 * PAD : 3 * PAD]
    for side in range(SIDES):
        outs[side][...] = moved[:, side * cap : (side + 1) * cap]
    coarse = inverse.shape[1]
    padded = coarse // mode_count * PAD
    old = lax.broadcasted_iota(jnp.int32, (coarse, padded), 0)
    new = lax.broadcasted_iota(jnp.int32, (coarse, padded), 1)
    spread = jnp.where((old // mode_count) * PAD + old % mode_count == new, 1.0, 0.0)
    blank = jnp.zeros((PAD - mode_count, coarse), jnp.float32)
    wide = exact(jnp.concatenate([inverse[...], blank], axis=0), spread)
    blank = jnp.zeros((PAD - mode_count, load.shape[1]), jnp.float32)
    loads = jnp.concatenate([load[...], blank], axis=0)
    copies(outs[SIDES], jnp.concatenate([wide, loads], axis=1))
    outs[SIDES + 1][...] = codes_lanes
    outs[SIDES + 2][...] = jnp.concatenate([upper, lower], axis=0)


def around(i, j):
    right, up = 1 - 2 * (i % 2), 1 - 2 * (j % 2)
    return [(i, j), (i + right, j), (i - right, j), (i, j + up), (i, j - up)]


def mode_blocks(own, partner):
    cap = own[0].shape[1]
    rows = []
    for side in range(SIDES):
        column = [own[side][...]]
        for other in range(SIDES):
            if other == side:
                column.append(-partner[side][...])
            else:
                column.append(jnp.zeros((PAD, cap), jnp.float32))
        rows.append(jnp.concatenate(column, axis=0))
    return rows


def lane_spread(mode_count, lanes):
    shape = (PAD * (SIDES + 1), lanes)
    old = lax.broadcasted_iota(jnp.int32, shape, 0)
    new = lax.broadcasted_iota(jnp.int32, shape, 1)
    spot = (old // PAD) * mode_count + old % PAD
    match = (spot == new % GROUP) & (old % PAD < mode_count)
    return jnp.where(match, 1.0, 0.0)


def operators_kernel(mode_count, flex, schur, codes_row, codes_lanes, *refs):
    own, partner = refs[0:4], refs[4:8]
    outs = refs[8:12]
    modes_out = refs[12]
    slot_pieces, row_pieces, out_pieces = refs[13:16]
    total = codes_lanes.shape[0]
    cap = total // SIDES
    half = cap // 2
    lanes = 4 * GROUP
    spread = lane_spread(mode_count, lanes)
    for side, block in enumerate(mode_blocks(own, partner)):
        placed = exact(block, spread, ((0,), (0,)))
        first = lax.broadcasted_iota(jnp.int32, placed.shape, 1) < GROUP
        modes_out[side * cap : (side + 1) * cap, :] = jnp.where(first, placed, 0.0)
        fill_pieces(slot_pieces, side * cap, placed)
    group = lax.broadcasted_iota(jnp.int32, (half, lanes), 1) // GROUP

    def write_schur(side, block):
        outs[side][...] = jnp.where(group == 0, block[:half], block[half:])

    def write_flex(side, block):
        mine = jnp.where(group == 2, block[:half], block[half:])
        outs[side][...] = jnp.where(group < 2, outs[side][...], mine)

    apply_local(schur, codes_row, codes_lanes, slot_pieces, row_pieces, out_pieces, write_schur)
    apply_rows(flex, codes_row, row_pieces, out_pieces, write_flex)


def start_kernel(mode_count, layers, flex, gap, codes_row, codes_lanes, *refs):
    slabs = refs[0:4]
    gathered, modes, place_ref = refs[4:7]
    outs = refs[7:11]
    start_out, inverse_out = refs[11:13]
    slot_pieces, row_pieces, out_pieces = refs[13:16]
    cap = codes_lanes.shape[0] // SIDES
    wide = gathered.shape[0]
    spread = lane_spread(mode_count, GROUP)
    for n, centre in enumerate(around(place_ref[0], place_ref[1])):
        rows = []
        for i, j in around(*centre):
            first = jnp.clip(i * layers + j, 0, wide // PAD - 1) * PAD
            rows.append(gathered[pl.ds(pl.multiple_of(first, PAD), PAD), 0:wide])
        table = jnp.concatenate(rows, axis=0)
        inverse_out[n * GROUP : (n + 1) * GROUP, :] = exact(spread, table, ((0,), (0,)))
    coefficients = repeated(exact(inverse_out[0:GROUP, :], gathered[:, wide:]))
    start = three_pass(modes[...], coefficients)
    start_out[...] = start
    fill_pieces(slot_pieces, 0, start)

    def write(side, block):
        outs[side][0:cap, :] = block
        outs[side][cap:, :] = slabs[side][...]

    apply_local(flex, codes_row, codes_lanes, slot_pieces, row_pieces, out_pieces, write, gap)


def repeated(x):
    return jnp.concatenate([x] * 4, axis=0)


def components_of(own_pieces, block_pieces):
    both = one_pass(own_pieces[...].astype(jnp.bfloat16), block_pieces[...])
    cols = both.shape[1] // 2
    return halves(both[0:PAD]) + both[PAD:, :cols]


def grouped(slab, first):
    group = lax.broadcasted_iota(jnp.int32, slab.shape, 1) // GROUP
    upper = jnp.where(group == first, slab, 0.0)
    lower = jnp.where(group == first + 1, slab, 0.0)
    return jnp.concatenate([upper, lower], axis=0)


def lagged(side, first, mine, theirs, coefficients):
    left = jnp.concatenate([grouped(mine[...], first), grouped(theirs[...], first)], axis=1)
    near = coefficients[(side + 1) * GROUP : (side + 2) * GROUP]
    return three_pass(left, jnp.concatenate([repeated(coefficients[0:GROUP]), repeated(-near)], axis=0))


def first_kernel(schur, codes_row, codes_lanes, *refs):
    received, sent, own = refs[0:4], refs[4:8], refs[8]
    outs = refs[9:13]
    gap_out, parts_out = refs[13:15]
    slot_pieces, row_pieces, out_pieces = refs[15:18]
    cap = codes_lanes.shape[0] // SIDES
    for side in range(SIDES):
        block = sent[side][0:cap, :] - received[side][0:cap, :]
        gap_out[side * cap : (side + 1) * cap, :] = block
        fill_pieces(slot_pieces, side * cap, block)
    copies(parts_out, components_of(own, slot_pieces))

    def write(side, block):
        outs[side][...] = block

    apply_local(schur, codes_row, codes_lanes, slot_pieces, row_pieces, out_pieces, write)


def stage_kernel(stage, counts, matrix, codes_row, codes_lanes, *refs):
    refs = list(refs)

    def take(count):
        taken = refs[:count]
        del refs[:count]
        return taken

    received, sent, mine, theirs = take(4), take(4), take(4), take(4)
    own, gathered, inverse_rows, modes = take(4)
    states_in = take(counts[0])
    outs = take(4) if stage < 5 else []
    states_out = take(counts[1])
    (parts_out,) = take(1)
    slot_pieces, row_pieces, out_pieces = take(3)
    total = codes_lanes.shape[0]
    cap = total // SIDES
    coefficients = exact(inverse_rows[...], gathered[...])
    direct_all = three_pass(modes[...], repeated(coefficients[0:GROUP]))
    tail = pl.ds(cap, cap // 2)
    for side in range(SIDES):
        rows = slice(side * cap, (side + 1) * cap)
        jump = sent[side][...] - received[side][...]
        first = 0 if stage in (2, 4) else 2
        behind = lagged(side, first, mine[side].at[tail], theirs[side].at[tail], coefficients)
        direct = direct_all[rows, :]
        nextin = None
        if stage == 2:
            (gap,) = states_in
            block = 0.5 * (jump - behind)
            nextin = block
            states_out[0][rows, :] = block
            states_out[1][rows, :] = gap[rows, :] - direct
        elif stage == 3:
            precond, residual = states_in
            block = (jump - behind) / theta_mid
            nextin = residual[rows, :] - block
            states_out[0][rows, :] = nextin
            states_out[1][rows, :] = (precond[rows, :] - direct) / theta_mid
        elif stage == 4:
            residual, step = states_in
            block = 0.5 * (jump + behind)
            nextin = keep_step * step[rows, :] + new_step * block
            states_out[0][rows, :] = residual[rows, :] + direct
            states_out[1][rows, :] = nextin
        else:
            residual, raw_step, start, step = states_in
            block = jump - new_step * behind
            states_out[0][rows, :] = residual[rows, :] - block
            second = raw_step[rows, :] - new_step * direct
            states_out[1][rows, :] = second + start[rows, :] + step[rows, :]
        if nextin is not None:
            fill_pieces(slot_pieces, side * cap, nextin)
        fill_pieces(out_pieces, side * cap, block)
    copies(parts_out, components_of(own, out_pieces))
    if stage < 5:

        def write(side, block):
            outs[side][...] = block

        apply_local(matrix, codes_row, codes_lanes, slot_pieces, row_pieces, out_pieces, write)


def rows_kernel(codes_lanes, residual, multipliers, modes, residual_out, multipliers_out, modes_out, pieces):
    total = residual.shape[0]
    cap = total // SIDES
    for n, source in enumerate((residual, multipliers, modes)):
        high, low = two_pieces(source[...])
        pieces[:, 256 * n : 256 * n + 128] = high
        pieces[:, 256 * n + 128 : 256 * (n + 1)] = low

    def keep(begin, rows):
        for n, target in enumerate((residual_out, multipliers_out, modes_out)):
            target[begin : begin + cap, :] = halves(rows[:, 256 * n : 256 * (n + 1)])

    to_rows(codes_lanes, pieces, keep)


def last_kernel(residual, modes, gathered, inverse_rows, out):
    coefficients = repeated(exact(inverse_rows[0:GROUP, :], gathered[...]))
    out[...] = residual[...] + three_pass(modes[...], coefficients)


def call(kernel, name, outs, inputs, scratch=(), smem=(), extra=0):
    vmem = pl.BlockSpec(memory_space=pltpu.VMEM)
    scalar = pl.BlockSpec(memory_space=pltpu.SMEM)
    return pl.pallas_call(
        kernel,
        name=name,
        out_shape=[jax.ShapeDtypeStruct(shape, jnp.float32) if isinstance(shape, tuple) else shape for shape in outs],
        in_specs=[scalar if n in smem else vmem for n in range(len(inputs))],
        out_specs=[vmem] * len(outs),
        scratch_shapes=list(scratch),
        compiler_params=pltpu.CompilerParams(vmem_limit_bytes=28 * 1024 * 1024 + extra),
    )(*inputs)


def exchange(blocks):
    received = []
    for side, block in enumerate(blocks):
        axis = "sub" if side < 2 else "layer"
        pairs = []
        for i in range(side % 2, lax.axis_size(axis) - 1, 2):
            pairs += [(i, i + 1), (i + 1, i)]
        received.append(lax.ppermute(block, axis, pairs))
    return received


def everywhere(stacked):
    own = lax.axis_index("sub") * lax.axis_size("layer") + lax.axis_index("layer")
    rows = lax.broadcasted_iota(jnp.int32, stacked.shape, 0) // PAD
    return lax.psum(jnp.where(rows == own, stacked, 0.0), ("sub", "layer"))


def per_device(
    local_gap, route_codes, flexibility, dirichlet, rigid_modes, coarse_inverse, rigid_load
):
    gap = local_gap[0, 0]
    flex = flexibility[0, 0]
    schur = dirichlet[0, 0]
    modes = rigid_modes[0, 0]
    mode_count, total = modes.shape
    cap = total // SIDES
    cols = gap.shape[1]
    layers = lax.axis_size("layer")
    wide = lax.axis_size("sub") * layers * PAD
    place = jnp.stack([lax.axis_index("sub"), lax.axis_index("layer")]).astype(jnp.int32)
    pieces = pltpu.VMEM((total, 2 * cols), jnp.bfloat16)
    scratch = [pieces] * 3
    block = [(cap, cols)] * SIDES
    whole = (total, cols)
    parts = (wide, cols)
    table = 8 * wide * (wide + cols)

    shown = call(
        functools.partial(modes_kernel, mode_count),
        "modes_to_slots",
        [(PAD, cap)] * SIDES
        + [(wide, wide + cols), jax.ShapeDtypeStruct((total, 128), jnp.int32), (2 * PAD, total)]
        + [jax.ShapeDtypeStruct((1, total), jnp.int32)],
        [route_codes[0], modes, coarse_inverse, rigid_load, place],
        smem=(4,),
        extra=table,
    )
    own, (inverse_load, codes_lanes, own_pieces, codes_row) = shown[:4], shown[4:]
    gathered = everywhere(inverse_load)
    partner = exchange(own)
    shown = call(
        functools.partial(operators_kernel, mode_count),
        "operators_on_modes",
        [(cap // 2, 4 * GROUP)] * SIDES + [(total, 4 * GROUP)],
        [flex, schur, codes_row, codes_lanes, *own, *partner],
        scratch,
    )
    slabs, slot_modes = shown[:4], shown[4]
    shown = call(
        functools.partial(start_kernel, mode_count, layers),
        "start",
        [(cap + cap // 2, cols)] * SIDES + [whole, (5 * GROUP, wide)],
        [flex, gap, codes_row, codes_lanes, *slabs, gathered, slot_modes, place],
        scratch,
        smem=(10,),
        extra=table,
    )
    sent, (start, inverse_rows) = shown[:4], shown[4:]
    received = exchange(sent)
    slab_sent, slab_received = sent, received
    shown = call(
        first_kernel,
        "stage_1",
        block + [whole, parts],
        [schur, codes_row, codes_lanes, *received, *sent, own_pieces],
        scratch,
    )
    sent, (gap_jump, components) = shown[:4], shown[4:]

    def stage(number, matrix, states_in, sent, components):
        gathered = everywhere(components)
        received = exchange(sent)
        inputs = [codes_row, codes_lanes, *received, *sent, *slab_sent, *slab_received]
        inputs += [own_pieces, gathered, inverse_rows, slot_modes, *states_in]
        outs = [whole] * 2 + [parts]
        kernel = functools.partial(stage_kernel, number, (len(states_in), 2))
        if matrix is None:
            kernel = functools.partial(kernel, None)
        else:
            inputs, outs = [matrix] + inputs, block + outs
        return call(kernel, "stage_%d" % number, outs, inputs, scratch)

    shown = stage(2, flex, [gap_jump], sent, components)
    sent, (precond, residual, components) = shown[:4], shown[4:]
    shown = stage(3, schur, [precond, residual], sent, components)
    sent, (residual, step, components) = shown[:4], shown[4:]
    shown = stage(4, flex, [residual, step], sent, components)
    sent, (residual, raw_step, components) = shown[:4], shown[4:]
    shown = stage(5, None, [residual, raw_step, start, step], sent, components)
    residual, multipliers, components = shown

    gathered = everywhere(components)
    residual, multipliers, row_modes = call(
        rows_kernel,
        "slots_to_rows",
        [whole, whole, (total, 4 * GROUP)],
        [codes_lanes, residual, multipliers, slot_modes],
        [pltpu.VMEM((total, 768), jnp.bfloat16)],
    )
    (residual,) = call(
        last_kernel, "residual", [whole], [residual, row_modes, gathered, inverse_rows]
    )
    return (multipliers[None, None], residual[None, None])


def solution(mesh):
    placed = (
        P("sub", "layer", None, None),
        P("sub", "layer", None),
        P("sub", "layer", None, None),
        P("sub", "layer", None, None),
        P("sub", "layer", None, None),
        P(("sub", "layer"), None),
        P(("sub", "layer"), None),
    )
    return jax.shard_map(
        per_device,
        mesh=mesh,
        in_specs=placed,
        out_specs=(P("sub", "layer", None, None), P("sub", "layer", None, None)),
        check_vma=False,
    )
```

```python
import functools

import jax
import jax.numpy as jnp
from jax import lax
from jax.experimental import pallas as pl
from jax.experimental.pallas import tpu as pltpu
from jax.sharding import PartitionSpec as P

theta_mid = 4.25
delta_half = 3.75
sigma_ratio = theta_mid / delta_half
damping = delta_half / theta_mid
damping_next = 1.0 / (2.0 * sigma_ratio - damping)
keep_step = damping_next * damping
new_step = 2.0 * damping_next / delta_half

GROUP = 32
PAD = 8
SIDES = 4


def exact(a, b, contract=((1,), (0,))):
    return lax.dot_general(
        a,
        b,
        (contract, ((), ())),
        precision=lax.Precision.HIGHEST,
        preferred_element_type=jnp.float32,
    )


def one_pass(a, b):
    return jnp.dot(a, b, preferred_element_type=jnp.float32)


def two_pieces(x):
    high = x.astype(jnp.bfloat16)
    low = (x - high.astype(jnp.float32)).astype(jnp.bfloat16)
    return high, low


def slot_by_row(codes_row, start, rows):
    slots = lax.broadcasted_iota(jnp.int32, (rows, codes_row.shape[1]), 0) + start
    return jnp.where(slots == codes_row, 1.0, 0.0).astype(jnp.bfloat16)


def row_by_slot(codes_lanes, slots):
    rows, lanes = codes_lanes.shape
    lane = lax.broadcasted_iota(jnp.int32, (rows, lanes), 1)
    parts = [
        jnp.where(lane + first == codes_lanes, 1.0, 0.0).astype(jnp.bfloat16)
        for first in range(0, slots, lanes)
    ]
    return jnp.concatenate(parts, axis=1)


def fill_pieces(pieces, start, x):
    high, low = two_pieces(x)
    cols = x.shape[1]
    pieces[pl.ds(start, x.shape[0]), 0:cols] = high
    pieces[pl.ds(start, x.shape[0]), cols : 2 * cols] = low


def to_rows(codes_lanes, slot_pieces, write):
    total = slot_pieces.shape[0]
    chunk = total // SIDES
    for c in range(SIDES):
        pick = row_by_slot(codes_lanes[c * chunk : (c + 1) * chunk, :], total)
        write(c * chunk, one_pass(pick, slot_pieces[...]))


def halves(x):
    cols = x.shape[1] // 2
    return x[:, :cols] + x[:, cols:]


def apply_local(matrix, codes_row, codes_lanes, slot_pieces, row_pieces, out_pieces, write, less=None):
    total = slot_pieces.shape[0]
    chunk = total // SIDES

    def keep(start, rows):
        row_pieces[start : start + chunk, :] = rows.astype(jnp.bfloat16)

    to_rows(codes_lanes, slot_pieces, keep)
    apply_rows(matrix, codes_row, row_pieces, out_pieces, write, less)


def apply_rows(matrix, codes_row, row_pieces, out_pieces, write, less=None):
    total = row_pieces.shape[0]
    chunk = total // SIDES
    cols = row_pieces.shape[1] // 2
    for c in range(SIDES):
        high, low = two_pieces(matrix[c * chunk : (c + 1) * chunk, :])
        product = halves(one_pass(high, row_pieces[...])) + one_pass(low, row_pieces[:, :cols])
        if less is not None:
            product = less[c * chunk : (c + 1) * chunk, :] - product
        fill_pieces(out_pieces, c * chunk, product)
    for side in range(SIDES):
        pick = slot_by_row(codes_row[...], side * chunk, chunk)
        write(side, halves(one_pass(pick, out_pieces[...])))


def three_pass(a, b):
    a_high, a_low = two_pieces(a)
    b_high, b_low = two_pieces(b)
    both = jnp.concatenate([b_high, b_low], axis=1)
    return halves(one_pass(a_high, both)) + one_pass(a_low, b_high)


def turned(x, bits):
    flipped = 0
    for b in range(bits):
        flipped = flipped | (((x >> b) & 1) << (bits - 1 - b))
    return flipped


def in_order(gathered, columns, here, table):
    count = table.shape[0] // PAD
    bits = count.bit_length() - 1
    for q in range(count):
        first = pl.multiple_of((here ^ turned(q, bits)) * PAD, PAD)
        table[pl.ds(first, PAD), :] = gathered[q * PAD : (q + 1) * PAD, columns]


def modes_kernel(mode_count, codes_row, modes, inverse, load, place, *outs):
    total = codes_row.shape[1]
    cap = total // SIDES
    codes = codes_row[...]
    heading = codes // cap
    even = jnp.where(heading < 2, 1 - lax.rem(place[0], 2), 1 - lax.rem(place[1], 2))
    turn = jnp.where(heading < SIDES, even * (1 - 2 * (heading % 2)), 0)
    codes = codes + turn * cap
    outs[SIDES + 3][...] = codes
    codes = jnp.broadcast_to(codes, (128, total)).astype(jnp.float32)
    codes_lanes = jnp.transpose(codes).astype(jnp.int32)
    x = jnp.concatenate(
        [modes[...], jnp.zeros((PAD - mode_count, total), jnp.float32)], axis=0
    )
    high = x.astype(jnp.bfloat16).astype(jnp.float32)
    middle = (x - high).astype(jnp.bfloat16).astype(jnp.float32)
    low = x - high - middle
    pieces = jnp.concatenate([high, middle, low, jnp.zeros_like(low)], axis=0).astype(jnp.bfloat16)
    moved = one_pass(pieces, row_by_slot(codes_lanes, total))
    upper, lower = moved[0:PAD], moved[PAD : 2 * PAD]
    moved = upper + lower + moved[2 * PAD : 3 * PAD]
    for side in range(SIDES):
        outs[side][...] = moved[:, side * cap : (side + 1) * cap]
    coarse = inverse.shape[1]
    padded = coarse // mode_count * PAD
    old = lax.broadcasted_iota(jnp.int32, (coarse, padded), 0)
    new = lax.broadcasted_iota(jnp.int32, (coarse, padded), 1)
    spread = jnp.where((old // mode_count) * PAD + old % mode_count == new, 1.0, 0.0)
    blank = jnp.zeros((PAD - mode_count, coarse), jnp.float32)
    wide = exact(jnp.concatenate([inverse[...], blank], axis=0), spread)
    blank = jnp.zeros((PAD - mode_count, load.shape[1]), jnp.float32)
    loads = jnp.concatenate([load[...], blank], axis=0)
    outs[SIDES][...] = jnp.concatenate([wide, loads], axis=1)
    outs[SIDES + 1][...] = codes_lanes
    outs[SIDES + 2][...] = jnp.concatenate([upper, lower], axis=0)


def around(i, j):
    right, up = 1 - 2 * (i % 2), 1 - 2 * (j % 2)
    return [(i, j), (i + right, j), (i - right, j), (i, j + up), (i, j - up)]


def mode_blocks(own, partner):
    cap = own[0].shape[1]
    rows = []
    for side in range(SIDES):
        column = [own[side][...]]
        for other in range(SIDES):
            if other == side:
                column.append(-partner[side][...])
            else:
                column.append(jnp.zeros((PAD, cap), jnp.float32))
        rows.append(jnp.concatenate(column, axis=0))
    return rows


def lane_spread(mode_count, lanes):
    shape = (PAD * (SIDES + 1), lanes)
    old = lax.broadcasted_iota(jnp.int32, shape, 0)
    new = lax.broadcasted_iota(jnp.int32, shape, 1)
    spot = (old // PAD) * mode_count + old % PAD
    match = (spot == new % GROUP) & (old % PAD < mode_count)
    return jnp.where(match, 1.0, 0.0)


def operators_kernel(mode_count, flex, schur, codes_row, codes_lanes, *refs):
    own, partner = refs[0:4], refs[4:8]
    outs = refs[8:12]
    modes_out = refs[12]
    slot_pieces, row_pieces, out_pieces = refs[13:16]
    total = codes_lanes.shape[0]
    cap = total // SIDES
    half = cap // 2
    lanes = 4 * GROUP
    spread = lane_spread(mode_count, lanes)
    for side, block in enumerate(mode_blocks(own, partner)):
        placed = exact(block, spread, ((0,), (0,)))
        first = lax.broadcasted_iota(jnp.int32, placed.shape, 1) < GROUP
        modes_out[side * cap : (side + 1) * cap, :] = jnp.where(first, placed, 0.0)
        fill_pieces(slot_pieces, side * cap, placed)
    group = lax.broadcasted_iota(jnp.int32, (half, lanes), 1) // GROUP

    def write_schur(side, block):
        outs[side][...] = jnp.where(group == 0, block[:half], block[half:])

    def write_flex(side, block):
        mine = jnp.where(group == 2, block[:half], block[half:])
        outs[side][...] = jnp.where(group < 2, outs[side][...], mine)

    apply_local(schur, codes_row, codes_lanes, slot_pieces, row_pieces, out_pieces, write_schur)
    apply_rows(flex, codes_row, row_pieces, out_pieces, write_flex)


def start_kernel(mode_count, layers, flex, gap, codes_row, codes_lanes, *refs):
    slabs = refs[0:4]
    gathered, modes, place_ref = refs[4:7]
    outs = refs[7:11]
    start_out, inverse_out = refs[11:13]
    slot_pieces, row_pieces, out_pieces, table = refs[13:17]
    cap = codes_lanes.shape[0] // SIDES
    wide = gathered.shape[0]
    devices = wide // PAD
    bits = devices.bit_length() - 1
    here = place_ref[0] * layers + place_ref[1]
    spread = lane_spread(mode_count, GROUP)
    for n, centre in enumerate(around(place_ref[0], place_ref[1])):
        rows = []
        for i, j in around(*centre):
            near = jnp.clip(i * layers + j, 0, devices - 1)
            first = turned(here ^ near, bits) * PAD
            rows.append(gathered[pl.ds(pl.multiple_of(first, PAD), PAD), 0:wide])
        rows = jnp.concatenate(rows, axis=0)
        inverse_out[n * GROUP : (n + 1) * GROUP, :] = exact(spread, rows, ((0,), (0,)))
    in_order(gathered, slice(wide, None), here, table)
    coefficients = repeated(exact(inverse_out[0:GROUP, :], table[...]))
    start = three_pass(modes[...], coefficients)
    start_out[...] = start
    fill_pieces(slot_pieces, 0, start)

    def write(side, block):
        outs[side][0:cap, :] = block
        outs[side][cap:, :] = slabs[side][...]

    apply_local(flex, codes_row, codes_lanes, slot_pieces, row_pieces, out_pieces, write, gap)


def repeated(x):
    return jnp.concatenate([x] * 4, axis=0)


def components_of(own_pieces, block_pieces):
    both = one_pass(own_pieces[...].astype(jnp.bfloat16), block_pieces[...])
    cols = both.shape[1] // 2
    return halves(both[0:PAD]) + both[PAD:, :cols]


def grouped(slab, first):
    group = lax.broadcasted_iota(jnp.int32, slab.shape, 1) // GROUP
    upper = jnp.where(group == first, slab, 0.0)
    lower = jnp.where(group == first + 1, slab, 0.0)
    return jnp.concatenate([upper, lower], axis=0)


def lagged(side, first, mine, theirs, coefficients):
    left = jnp.concatenate([grouped(mine[...], first), grouped(theirs[...], first)], axis=1)
    near = coefficients[(side + 1) * GROUP : (side + 2) * GROUP]
    return three_pass(left, jnp.concatenate([repeated(coefficients[0:GROUP]), repeated(-near)], axis=0))


def first_kernel(schur, codes_row, codes_lanes, *refs):
    received, sent, own = refs[0:4], refs[4:8], refs[8]
    outs = refs[9:13]
    gap_out, parts_out = refs[13:15]
    slot_pieces, row_pieces, out_pieces = refs[15:18]
    cap = codes_lanes.shape[0] // SIDES
    for side in range(SIDES):
        block = sent[side][0:cap, :] - received[side][0:cap, :]
        gap_out[side * cap : (side + 1) * cap, :] = block
        fill_pieces(slot_pieces, side * cap, block)
    parts_out[...] = components_of(own, slot_pieces)

    def write(side, block):
        outs[side][...] = block

    apply_local(schur, codes_row, codes_lanes, slot_pieces, row_pieces, out_pieces, write)


def stage_kernel(stage, layers, counts, matrix, codes_row, codes_lanes, place_ref, *refs):
    refs = list(refs)

    def take(count):
        taken = refs[:count]
        del refs[:count]
        return taken

    received, sent, mine, theirs = take(4), take(4), take(4), take(4)
    own, gathered, inverse_rows, modes = take(4)
    states_in = take(counts[0])
    outs = take(4) if stage < 5 else []
    states_out = take(counts[1])
    (parts_out,) = take(1)
    slot_pieces, row_pieces, out_pieces, table = take(4)
    total = codes_lanes.shape[0]
    cap = total // SIDES
    in_order(gathered, slice(None), place_ref[0] * layers + place_ref[1], table)
    coefficients = exact(inverse_rows[...], table[...])
    direct_all = three_pass(modes[...], repeated(coefficients[0:GROUP]))
    tail = pl.ds(cap, cap // 2)
    for side in range(SIDES):
        rows = slice(side * cap, (side + 1) * cap)
        jump = sent[side][...] - received[side][...]
        first = 0 if stage in (2, 4) else 2
        behind = lagged(side, first, mine[side].at[tail], theirs[side].at[tail], coefficients)
        direct = direct_all[rows, :]
        nextin = None
        if stage == 2:
            (gap,) = states_in
            block = 0.5 * (jump - behind)
            nextin = block
            states_out[0][rows, :] = block
            states_out[1][rows, :] = gap[rows, :] - direct
        elif stage == 3:
            precond, residual = states_in
            block = (jump - behind) / theta_mid
            nextin = residual[rows, :] - block
            states_out[0][rows, :] = nextin
            states_out[1][rows, :] = (precond[rows, :] - direct) / theta_mid
        elif stage == 4:
            residual, step = states_in
            block = 0.5 * (jump + behind)
            nextin = keep_step * step[rows, :] + new_step * block
            states_out[0][rows, :] = residual[rows, :] + direct
            states_out[1][rows, :] = nextin
        else:
            residual, raw_step, start, step = states_in
            block = jump - new_step * behind
            states_out[0][rows, :] = residual[rows, :] - block
            second = raw_step[rows, :] - new_step * direct
            states_out[1][rows, :] = second + start[rows, :] + step[rows, :]
        if nextin is not None:
            fill_pieces(slot_pieces, side * cap, nextin)
        fill_pieces(out_pieces, side * cap, block)
    parts_out[...] = components_of(own, out_pieces)
    if stage < 5:

        def write(side, block):
            outs[side][...] = block

        apply_local(matrix, codes_row, codes_lanes, slot_pieces, row_pieces, out_pieces, write)


def rows_kernel(codes_lanes, residual, multipliers, modes, residual_out, multipliers_out, modes_out, pieces):
    total = residual.shape[0]
    cap = total // SIDES
    for n, source in enumerate((residual, multipliers, modes)):
        high, low = two_pieces(source[...])
        pieces[:, 256 * n : 256 * n + 128] = high
        pieces[:, 256 * n + 128 : 256 * (n + 1)] = low

    def keep(begin, rows):
        for n, target in enumerate((residual_out, multipliers_out, modes_out)):
            target[begin : begin + cap, :] = halves(rows[:, 256 * n : 256 * (n + 1)])

    to_rows(codes_lanes, pieces, keep)


def last_kernel(layers, residual, modes, gathered, inverse_rows, place_ref, out, table):
    in_order(gathered, slice(None), place_ref[0] * layers + place_ref[1], table)
    coefficients = repeated(exact(inverse_rows[0:GROUP, :], table[...]))
    out[...] = residual[...] + three_pass(modes[...], coefficients)


def call(kernel, name, outs, inputs, scratch=(), smem=(), extra=0):
    vmem = pl.BlockSpec(memory_space=pltpu.VMEM)
    scalar = pl.BlockSpec(memory_space=pltpu.SMEM)
    return pl.pallas_call(
        kernel,
        name=name,
        out_shape=[jax.ShapeDtypeStruct(shape, jnp.float32) if isinstance(shape, tuple) else shape for shape in outs],
        in_specs=[scalar if n in smem else vmem for n in range(len(inputs))],
        out_specs=[vmem] * len(outs),
        scratch_shapes=list(scratch),
        compiler_params=pltpu.CompilerParams(vmem_limit_bytes=28 * 1024 * 1024 + extra),
    )(*inputs)


def exchange(blocks):
    received = []
    for side, block in enumerate(blocks):
        axis = "sub" if side < 2 else "layer"
        pairs = []
        for i in range(side % 2, lax.axis_size(axis) - 1, 2):
            pairs += [(i, i + 1), (i + 1, i)]
        received.append(lax.ppermute(block, axis, pairs))
    return received


def everywhere(block):
    for axis in ("sub", "layer"):
        count = lax.axis_size(axis)
        step = count // 2
        while step > 0:
            other = lax.ppermute(block, axis, [(i, i ^ step) for i in range(count)])
            block = jnp.concatenate([block, other], axis=0)
            step //= 2
    return block


def per_device(
    local_gap, route_codes, flexibility, dirichlet, rigid_modes, coarse_inverse, rigid_load
):
    gap = local_gap[0, 0]
    flex = flexibility[0, 0]
    schur = dirichlet[0, 0]
    modes = rigid_modes[0, 0]
    mode_count, total = modes.shape
    cap = total // SIDES
    cols = gap.shape[1]
    layers = lax.axis_size("layer")
    wide = lax.axis_size("sub") * layers * PAD
    place = jnp.stack([lax.axis_index("sub"), lax.axis_index("layer")]).astype(jnp.int32)
    pieces = pltpu.VMEM((total, 2 * cols), jnp.bfloat16)
    scratch = [pieces] * 3
    block = [(cap, cols)] * SIDES
    whole = (total, cols)
    parts = (PAD, cols)
    ordered = pltpu.VMEM((wide, cols), jnp.float32)
    table = 8 * wide * (wide + cols)

    shown = call(
        functools.partial(modes_kernel, mode_count),
        "modes_to_slots",
        [(PAD, cap)] * SIDES
        + [(PAD, wide + cols), jax.ShapeDtypeStruct((total, 128), jnp.int32), (2 * PAD, total)]
        + [jax.ShapeDtypeStruct((1, total), jnp.int32)],
        [route_codes[0], modes, coarse_inverse, rigid_load, place],
        smem=(4,),
        extra=table,
    )
    own, (inverse_load, codes_lanes, own_pieces, codes_row) = shown[:4], shown[4:]
    gathered = everywhere(inverse_load)
    partner = exchange(own)
    shown = call(
        functools.partial(operators_kernel, mode_count),
        "operators_on_modes",
        [(cap // 2, 4 * GROUP)] * SIDES + [(total, 4 * GROUP)],
        [flex, schur, codes_row, codes_lanes, *own, *partner],
        scratch,
    )
    slabs, slot_modes = shown[:4], shown[4]
    shown = call(
        functools.partial(start_kernel, mode_count, layers),
        "start",
        [(cap + cap // 2, cols)] * SIDES + [whole, (5 * GROUP, wide)],
        [flex, gap, codes_row, codes_lanes, *slabs, gathered, slot_modes, place],
        scratch + [ordered],
        smem=(10,),
        extra=table,
    )
    sent, (start, inverse_rows) = shown[:4], shown[4:]
    received = exchange(sent)
    slab_sent, slab_received = sent, received
    shown = call(
        first_kernel,
        "stage_1",
        block + [whole, parts],
        [schur, codes_row, codes_lanes, *received, *sent, own_pieces],
        scratch,
    )
    sent, (gap_jump, components) = shown[:4], shown[4:]

    def stage(number, matrix, states_in, sent, components):
        gathered = everywhere(components)
        received = exchange(sent)
        inputs = [codes_row, codes_lanes, place, *received, *sent, *slab_sent, *slab_received]
        inputs += [own_pieces, gathered, inverse_rows, slot_modes, *states_in]
        outs = [whole] * 2 + [parts]
        kernel = functools.partial(stage_kernel, number, layers, (len(states_in), 2))
        if matrix is None:
            kernel = functools.partial(kernel, None)
        else:
            inputs, outs = [matrix] + inputs, block + outs
        scalar = (2,) if matrix is None else (3,)
        return call(kernel, "stage_%d" % number, outs, inputs, scratch + [ordered], smem=scalar)

    shown = stage(2, flex, [gap_jump], sent, components)
    sent, (precond, residual, components) = shown[:4], shown[4:]
    shown = stage(3, schur, [precond, residual], sent, components)
    sent, (residual, step, components) = shown[:4], shown[4:]
    shown = stage(4, flex, [residual, step], sent, components)
    sent, (residual, raw_step, components) = shown[:4], shown[4:]
    shown = stage(5, None, [residual, raw_step, start, step], sent, components)
    residual, multipliers, components = shown

    gathered = everywhere(components)
    residual, multipliers, row_modes = call(
        rows_kernel,
        "slots_to_rows",
        [whole, whole, (total, 4 * GROUP)],
        [codes_lanes, residual, multipliers, slot_modes],
        [pltpu.VMEM((total, 768), jnp.bfloat16)],
    )
    (residual,) = call(
        functools.partial(last_kernel, layers),
        "residual",
        [whole],
        [residual, row_modes, gathered, inverse_rows, place],
        [ordered],
        smem=(4,),
    )
    return (multipliers[None, None], residual[None, None])


def solution(mesh):
    placed = (
        P("sub", "layer", None, None),
        P("sub", "layer", None),
        P("sub", "layer", None, None),
        P("sub", "layer", None, None),
        P("sub", "layer", None, None),
        P(("sub", "layer"), None),
        P(("sub", "layer"), None),
    )
    return jax.shard_map(
        per_device,
        mesh=mesh,
        in_specs=placed,
        out_specs=(P("sub", "layer", None, None), P("sub", "layer", None, None)),
        check_vma=False,
    )
```

```python
import functools

import jax
import jax.numpy as jnp
from jax import lax
from jax.experimental import pallas as pl
from jax.experimental.pallas import tpu as pltpu
from jax.sharding import PartitionSpec as P

theta_mid = 4.25
delta_half = 3.75
sigma_ratio = theta_mid / delta_half
damping = delta_half / theta_mid
damping_next = 1.0 / (2.0 * sigma_ratio - damping)
keep_step = damping_next * damping
new_step = 2.0 * damping_next / delta_half

GROUP = 32
PAD = 8
SIDES = 4


def exact(a, b, contract=((1,), (0,))):
    return lax.dot_general(
        a,
        b,
        (contract, ((), ())),
        precision=lax.Precision.HIGHEST,
        preferred_element_type=jnp.float32,
    )


def one_pass(a, b):
    return jnp.dot(a, b, preferred_element_type=jnp.float32)


def two_pieces(x):
    high = x.astype(jnp.bfloat16)
    low = (x - high.astype(jnp.float32)).astype(jnp.bfloat16)
    return high, low


def slot_by_row(codes_row, start, rows):
    slots = lax.broadcasted_iota(jnp.int32, (rows, codes_row.shape[1]), 0) + start
    return jnp.where(slots == codes_row, 1.0, 0.0).astype(jnp.bfloat16)


def row_by_slot(codes_lanes, slots):
    rows, lanes = codes_lanes.shape
    lane = lax.broadcasted_iota(jnp.int32, (rows, lanes), 1)
    parts = [
        jnp.where(lane + first == codes_lanes, 1.0, 0.0).astype(jnp.bfloat16)
        for first in range(0, slots, lanes)
    ]
    return jnp.concatenate(parts, axis=1)


def fill_pieces(pieces, start, x):
    high, low = two_pieces(x)
    cols = x.shape[1]
    pieces[pl.ds(start, x.shape[0]), 0:cols] = high
    pieces[pl.ds(start, x.shape[0]), cols : 2 * cols] = low


def to_rows(codes_lanes, slot_pieces, write):
    total = slot_pieces.shape[0]
    chunk = total // SIDES
    for c in range(SIDES):
        pick = row_by_slot(codes_lanes[c * chunk : (c + 1) * chunk, :], total)
        write(c * chunk, one_pass(pick, slot_pieces[...]))


def halves(x):
    cols = x.shape[1] // 2
    return x[:, :cols] + x[:, cols:]


def fetch(matrix, held, arrived):
    chunk = held.shape[0] // SIDES
    pieces = []
    for c in range(SIDES):
        rows = pl.ds(c * chunk, chunk)
        pieces.append(pltpu.make_async_copy(matrix.at[rows], held.at[rows], arrived.at[c]))
        pieces[c].start()
    return pieces, held


def apply_local(fetched, codes_row, codes_lanes, slot_pieces, row_pieces, out_pieces, write, less=None):
    total = slot_pieces.shape[0]
    chunk = total // SIDES

    def keep(start, rows):
        row_pieces[start : start + chunk, :] = rows.astype(jnp.bfloat16)

    to_rows(codes_lanes, slot_pieces, keep)
    apply_rows(fetched, codes_row, row_pieces, out_pieces, write, less)


def apply_rows(fetched, codes_row, row_pieces, out_pieces, write, less=None):
    coming, matrix = fetched
    total = row_pieces.shape[0]
    chunk = total // SIDES
    cols = row_pieces.shape[1] // 2
    for c in range(SIDES):
        coming[c].wait()
        high, low = two_pieces(matrix[c * chunk : (c + 1) * chunk, :])
        product = halves(one_pass(high, row_pieces[...])) + one_pass(low, row_pieces[:, :cols])
        if less is not None:
            product = less[c * chunk : (c + 1) * chunk, :] - product
        fill_pieces(out_pieces, c * chunk, product)
    for side in range(SIDES):
        pick = slot_by_row(codes_row[...], side * chunk, chunk)
        write(side, halves(one_pass(pick, out_pieces[...])))


def three_pass(a, b):
    a_high, a_low = two_pieces(a)
    b_high, b_low = two_pieces(b)
    both = jnp.concatenate([b_high, b_low], axis=1)
    return halves(one_pass(a_high, both)) + one_pass(a_low, b_high)


def copies(ref, block):
    rows = block.shape[0]
    for q in range(ref.shape[0] // rows):
        ref[q * rows : (q + 1) * rows, :] = block


def modes_kernel(mode_count, codes_row, modes, inverse, load, place, *outs):
    total = codes_row.shape[1]
    cap = total // SIDES
    codes = codes_row[...]
    heading = codes // cap
    even = jnp.where(heading < 2, 1 - lax.rem(place[0], 2), 1 - lax.rem(place[1], 2))
    turn = jnp.where(heading < SIDES, even * (1 - 2 * (heading % 2)), 0)
    codes = codes + turn * cap
    outs[SIDES + 3][...] = codes
    codes = jnp.broadcast_to(codes, (128, total)).astype(jnp.float32)
    codes_lanes = jnp.transpose(codes).astype(jnp.int32)
    x = jnp.concatenate(
        [modes[...], jnp.zeros((PAD - mode_count, total), jnp.float32)], axis=0
    )
    high = x.astype(jnp.bfloat16).astype(jnp.float32)
    middle = (x - high).astype(jnp.bfloat16).astype(jnp.float32)
    low = x - high - middle
    pieces = jnp.concatenate([high, middle, low, jnp.zeros_like(low)], axis=0).astype(jnp.bfloat16)
    moved = one_pass(pieces, row_by_slot(codes_lanes, total))
    upper, lower = moved[0:PAD], moved[PAD : 2 * PAD]
    moved = upper + lower + moved[2 * PAD : 3 * PAD]
    for side in range(SIDES):
        outs[side][...] = moved[:, side * cap : (side + 1) * cap]
    coarse = inverse.shape[1]
    padded = coarse // mode_count * PAD
    old = lax.broadcasted_iota(jnp.int32, (coarse, padded), 0)
    new = lax.broadcasted_iota(jnp.int32, (coarse, padded), 1)
    spread = jnp.where((old // mode_count) * PAD + old % mode_count == new, 1.0, 0.0)
    blank = jnp.zeros((PAD - mode_count, coarse), jnp.float32)
    wide = exact(jnp.concatenate([inverse[...], blank], axis=0), spread)
    blank = jnp.zeros((PAD - mode_count, load.shape[1]), jnp.float32)
    loads = jnp.concatenate([load[...], blank], axis=0)
    copies(outs[SIDES], jnp.concatenate([wide, loads], axis=1))
    outs[SIDES + 1][...] = codes_lanes
    outs[SIDES + 2][...] = jnp.concatenate([upper, lower], axis=0)


def around(i, j):
    right, up = 1 - 2 * (i % 2), 1 - 2 * (j % 2)
    return [(i, j), (i + right, j), (i - right, j), (i, j + up), (i, j - up)]


def mode_blocks(own, partner):
    cap = own[0].shape[1]
    rows = []
    for side in range(SIDES):
        column = [own[side][...]]
        for other in range(SIDES):
            if other == side:
                column.append(-partner[side][...])
            else:
                column.append(jnp.zeros((PAD, cap), jnp.float32))
        rows.append(jnp.concatenate(column, axis=0))
    return rows


def lane_spread(mode_count, lanes):
    shape = (PAD * (SIDES + 1), lanes)
    old = lax.broadcasted_iota(jnp.int32, shape, 0)
    new = lax.broadcasted_iota(jnp.int32, shape, 1)
    spot = (old // PAD) * mode_count + old % PAD
    match = (spot == new % GROUP) & (old % PAD < mode_count)
    return jnp.where(match, 1.0, 0.0)


def operators_kernel(mode_count, flex, schur, codes_row, codes_lanes, *refs):
    own, partner = refs[0:4], refs[4:8]
    outs = refs[8:12]
    modes_out = refs[12]
    slot_pieces, row_pieces, out_pieces = refs[13:16]
    schur = fetch(schur, refs[16], refs[17])
    flex = fetch(flex, refs[18], refs[19])
    total = codes_lanes.shape[0]
    cap = total // SIDES
    half = cap // 2
    lanes = 4 * GROUP
    spread = lane_spread(mode_count, lanes)
    for side, block in enumerate(mode_blocks(own, partner)):
        placed = exact(block, spread, ((0,), (0,)))
        first = lax.broadcasted_iota(jnp.int32, placed.shape, 1) < GROUP
        modes_out[side * cap : (side + 1) * cap, :] = jnp.where(first, placed, 0.0)
        fill_pieces(slot_pieces, side * cap, placed)
    group = lax.broadcasted_iota(jnp.int32, (half, lanes), 1) // GROUP

    def write_schur(side, block):
        outs[side][...] = jnp.where(group == 0, block[:half], block[half:])

    def write_flex(side, block):
        mine = jnp.where(group == 2, block[:half], block[half:])
        outs[side][...] = jnp.where(group < 2, outs[side][...], mine)

    apply_local(schur, codes_row, codes_lanes, slot_pieces, row_pieces, out_pieces, write_schur)
    apply_rows(flex, codes_row, row_pieces, out_pieces, write_flex)


def start_kernel(mode_count, layers, flex, gap, codes_row, codes_lanes, *refs):
    slabs = refs[0:4]
    gathered, modes, place_ref = refs[4:7]
    outs = refs[7:11]
    start_out, inverse_out = refs[11:13]
    slot_pieces, row_pieces, out_pieces = refs[13:16]
    flex = fetch(flex, refs[16], refs[17])
    cap = codes_lanes.shape[0] // SIDES
    wide = gathered.shape[0]
    spread = lane_spread(mode_count, GROUP)
    for n, centre in enumerate(around(place_ref[0], place_ref[1])):
        rows = []
        for i, j in around(*centre):
            first = jnp.clip(i * layers + j, 0, wide // PAD - 1) * PAD
            rows.append(gathered[pl.ds(pl.multiple_of(first, PAD), PAD), 0:wide])
        table = jnp.concatenate(rows, axis=0)
        inverse_out[n * GROUP : (n + 1) * GROUP, :] = exact(spread, table, ((0,), (0,)))
    coefficients = repeated(exact(inverse_out[0:GROUP, :], gathered[:, wide:]))
    start = three_pass(modes[...], coefficients)
    start_out[...] = start
    fill_pieces(slot_pieces, 0, start)

    def write(side, block):
        outs[side][0:cap, :] = block
        outs[side][cap:, :] = slabs[side][...]

    apply_local(flex, codes_row, codes_lanes, slot_pieces, row_pieces, out_pieces, write, gap)


def repeated(x):
    return jnp.concatenate([x] * 4, axis=0)


def components_of(own_pieces, block_pieces):
    both = one_pass(own_pieces[...].astype(jnp.bfloat16), block_pieces[...])
    cols = both.shape[1] // 2
    return halves(both[0:PAD]) + both[PAD:, :cols]


def grouped(slab, first):
    group = lax.broadcasted_iota(jnp.int32, slab.shape, 1) // GROUP
    upper = jnp.where(group == first, slab, 0.0)
    lower = jnp.where(group == first + 1, slab, 0.0)
    return jnp.concatenate([upper, lower], axis=0)


def lagged(side, first, mine, theirs, coefficients):
    left = jnp.concatenate([grouped(mine[...], first), grouped(theirs[...], first)], axis=1)
    near = coefficients[(side + 1) * GROUP : (side + 2) * GROUP]
    return three_pass(left, jnp.concatenate([repeated(coefficients[0:GROUP]), repeated(-near)], axis=0))


def first_kernel(schur, codes_row, codes_lanes, *refs):
    received, sent, own = refs[0:4], refs[4:8], refs[8]
    outs = refs[9:13]
    gap_out, parts_out = refs[13:15]
    slot_pieces, row_pieces, out_pieces = refs[15:18]
    schur = fetch(schur, refs[18], refs[19])
    cap = codes_lanes.shape[0] // SIDES
    for side in range(SIDES):
        block = sent[side][0:cap, :] - received[side][0:cap, :]
        gap_out[side * cap : (side + 1) * cap, :] = block
        fill_pieces(slot_pieces, side * cap, block)
    copies(parts_out, components_of(own, slot_pieces))

    def write(side, block):
        outs[side][...] = block

    apply_local(schur, codes_row, codes_lanes, slot_pieces, row_pieces, out_pieces, write)


def stage_kernel(stage, counts, matrix, codes_row, codes_lanes, *refs):
    refs = list(refs)

    def take(count):
        taken = refs[:count]
        del refs[:count]
        return taken

    received, sent, mine, theirs = take(4), take(4), take(4), take(4)
    own, gathered, inverse_rows, modes = take(4)
    states_in = take(counts[0])
    outs = take(4) if stage < 5 else []
    states_out = take(counts[1])
    (parts_out,) = take(1)
    slot_pieces, row_pieces, out_pieces = take(3)
    if stage < 5:
        matrix = fetch(matrix, *take(2))
    total = codes_lanes.shape[0]
    cap = total // SIDES
    coefficients = exact(inverse_rows[...], gathered[...])
    direct_all = three_pass(modes[...], repeated(coefficients[0:GROUP]))
    tail = pl.ds(cap, cap // 2)
    for side in range(SIDES):
        rows = slice(side * cap, (side + 1) * cap)
        jump = sent[side][...] - received[side][...]
        first = 0 if stage in (2, 4) else 2
        behind = lagged(side, first, mine[side].at[tail], theirs[side].at[tail], coefficients)
        direct = direct_all[rows, :]
        nextin = None
        if stage == 2:
            (gap,) = states_in
            block = 0.5 * (jump - behind)
            nextin = block
            states_out[0][rows, :] = block
            states_out[1][rows, :] = gap[rows, :] - direct
        elif stage == 3:
            precond, residual = states_in
            block = (jump - behind) / theta_mid
            nextin = residual[rows, :] - block
            states_out[0][rows, :] = nextin
            states_out[1][rows, :] = (precond[rows, :] - direct) / theta_mid
        elif stage == 4:
            residual, step = states_in
            block = 0.5 * (jump + behind)
            nextin = keep_step * step[rows, :] + new_step * block
            states_out[0][rows, :] = residual[rows, :] + direct
            states_out[1][rows, :] = nextin
        else:
            residual, raw_step, start, step = states_in
            block = jump - new_step * behind
            states_out[0][rows, :] = residual[rows, :] - block
            second = raw_step[rows, :] - new_step * direct
            states_out[1][rows, :] = second + start[rows, :] + step[rows, :]
        if nextin is not None:
            fill_pieces(slot_pieces, side * cap, nextin)
        fill_pieces(out_pieces, side * cap, block)
    copies(parts_out, components_of(own, out_pieces))
    if stage < 5:

        def write(side, block):
            outs[side][...] = block

        apply_local(matrix, codes_row, codes_lanes, slot_pieces, row_pieces, out_pieces, write)


def rows_kernel(codes_lanes, residual, multipliers, modes, residual_out, multipliers_out, modes_out, pieces):
    total = residual.shape[0]
    cap = total // SIDES
    for n, source in enumerate((residual, multipliers, modes)):
        high, low = two_pieces(source[...])
        pieces[:, 256 * n : 256 * n + 128] = high
        pieces[:, 256 * n + 128 : 256 * (n + 1)] = low

    def keep(begin, rows):
        for n, target in enumerate((residual_out, multipliers_out, modes_out)):
            target[begin : begin + cap, :] = halves(rows[:, 256 * n : 256 * (n + 1)])

    to_rows(codes_lanes, pieces, keep)


def last_kernel(residual, modes, gathered, inverse_rows, out):
    coefficients = repeated(exact(inverse_rows[0:GROUP, :], gathered[...]))
    out[...] = residual[...] + three_pass(modes[...], coefficients)


def call(kernel, name, outs, inputs, scratch=(), smem=(), left=()):
    spaces = [pltpu.VMEM] * len(inputs)
    for n in smem:
        spaces[n] = pltpu.SMEM
    for n in left:
        spaces[n] = pl.ANY
    shapes = []
    for shape in outs:
        shapes.append(jax.ShapeDtypeStruct(shape, jnp.float32) if isinstance(shape, tuple) else shape)
    return pl.pallas_call(
        kernel,
        name=name,
        out_shape=shapes,
        in_specs=[pl.BlockSpec(memory_space=space) for space in spaces],
        out_specs=[pl.BlockSpec(memory_space=pltpu.VMEM)] * len(outs),
        scratch_shapes=list(scratch),
        compiler_params=pltpu.CompilerParams(vmem_limit_bytes=58 * 1024 * 1024),
    )(*inputs)


def exchange(blocks):
    received = []
    for side, block in enumerate(blocks):
        axis = "sub" if side < 2 else "layer"
        pairs = []
        for i in range(side % 2, lax.axis_size(axis) - 1, 2):
            pairs += [(i, i + 1), (i + 1, i)]
        received.append(lax.ppermute(block, axis, pairs))
    return received


def everywhere(stacked):
    return lax.all_to_all(stacked, ("sub", "layer"), split_axis=0, concat_axis=0, tiled=True)


def per_device(
    local_gap, route_codes, flexibility, dirichlet, rigid_modes, coarse_inverse, rigid_load
):
    gap = local_gap[0, 0]
    flex = flexibility[0, 0]
    schur = dirichlet[0, 0]
    modes = rigid_modes[0, 0]
    mode_count, total = modes.shape
    cap = total // SIDES
    cols = gap.shape[1]
    layers = lax.axis_size("layer")
    wide = lax.axis_size("sub") * layers * PAD
    place = jnp.stack([lax.axis_index("sub"), lax.axis_index("layer")]).astype(jnp.int32)
    pieces = pltpu.VMEM((total, 2 * cols), jnp.bfloat16)
    scratch = [pieces] * 3
    block = [(cap, cols)] * SIDES
    whole = (total, cols)
    parts = (wide, cols)
    brought = [pltpu.VMEM((total, total), jnp.float32), pltpu.SemaphoreType.DMA((SIDES,))]

    shown = call(
        functools.partial(modes_kernel, mode_count),
        "modes_to_slots",
        [(PAD, cap)] * SIDES
        + [(wide, wide + cols), jax.ShapeDtypeStruct((total, 128), jnp.int32), (2 * PAD, total)]
        + [jax.ShapeDtypeStruct((1, total), jnp.int32)],
        [route_codes[0], modes, coarse_inverse, rigid_load, place],
        smem=(4,),
    )
    own, (inverse_load, codes_lanes, own_pieces, codes_row) = shown[:4], shown[4:]
    gathered = everywhere(inverse_load)
    partner = exchange(own)
    shown = call(
        functools.partial(operators_kernel, mode_count),
        "operators_on_modes",
        [(cap // 2, 4 * GROUP)] * SIDES + [(total, 4 * GROUP)],
        [flex, schur, codes_row, codes_lanes, *own, *partner],
        scratch + brought * 2,
        left=(0, 1),
    )
    slabs, slot_modes = shown[:4], shown[4]
    shown = call(
        functools.partial(start_kernel, mode_count, layers),
        "start",
        [(cap + cap // 2, cols)] * SIDES + [whole, (5 * GROUP, wide)],
        [flex, gap, codes_row, codes_lanes, *slabs, gathered, slot_modes, place],
        scratch + brought,
        smem=(10,),
        left=(0,),
    )
    sent, (start, inverse_rows) = shown[:4], shown[4:]
    received = exchange(sent)
    slab_sent, slab_received = sent, received
    shown = call(
        first_kernel,
        "stage_1",
        block + [whole, parts],
        [schur, codes_row, codes_lanes, *received, *sent, own_pieces],
        scratch + brought,
        left=(0,),
    )
    sent, (gap_jump, components) = shown[:4], shown[4:]

    def stage(number, matrix, states_in, sent, components):
        gathered = everywhere(components)
        received = exchange(sent)
        inputs = [codes_row, codes_lanes, *received, *sent, *slab_sent, *slab_received]
        inputs += [own_pieces, gathered, inverse_rows, slot_modes, *states_in]
        outs = [whole] * 2 + [parts]
        kernel = functools.partial(stage_kernel, number, (len(states_in), 2))
        name = "stage_%d" % number
        if matrix is None:
            return call(functools.partial(kernel, None), name, outs, inputs, scratch)
        return call(kernel, name, block + outs, [matrix] + inputs, scratch + brought, left=(0,))

    shown = stage(2, flex, [gap_jump], sent, components)
    sent, (precond, residual, components) = shown[:4], shown[4:]
    shown = stage(3, schur, [precond, residual], sent, components)
    sent, (residual, step, components) = shown[:4], shown[4:]
    shown = stage(4, flex, [residual, step], sent, components)
    sent, (residual, raw_step, components) = shown[:4], shown[4:]
    shown = stage(5, None, [residual, raw_step, start, step], sent, components)
    residual, multipliers, components = shown

    gathered = everywhere(components)
    residual, multipliers, row_modes = call(
        rows_kernel,
        "slots_to_rows",
        [whole, whole, (total, 4 * GROUP)],
        [codes_lanes, residual, multipliers, slot_modes],
        [pltpu.VMEM((total, 768), jnp.bfloat16)],
    )
    (residual,) = call(
        last_kernel, "residual", [whole], [residual, row_modes, gathered, inverse_rows]
    )
    return (multipliers[None, None], residual[None, None])


def solution(mesh):
    placed = (
        P("sub", "layer", None, None),
        P("sub", "layer", None),
        P("sub", "layer", None, None),
        P("sub", "layer", None, None),
        P("sub", "layer", None, None),
        P(("sub", "layer"), None),
        P(("sub", "layer"), None),
    )
    return jax.shard_map(
        per_device,
        mesh=mesh,
        in_specs=placed,
        out_specs=(P("sub", "layer", None, None), P("sub", "layer", None, None)),
        check_vma=False,
    )
```

```python
import functools

import jax
import jax.numpy as jnp
from jax import lax
from jax.experimental import pallas as pl
from jax.experimental.pallas import tpu as pltpu
from jax.sharding import PartitionSpec as P

theta_mid = 4.25
delta_half = 3.75
sigma_ratio = theta_mid / delta_half
damping = delta_half / theta_mid
damping_next = 1.0 / (2.0 * sigma_ratio - damping)
keep_step = damping_next * damping
new_step = 2.0 * damping_next / delta_half

GROUP = 32
PAD = 8
SIDES = 4


def exact(a, b, contract=((1,), (0,))):
    return lax.dot_general(
        a,
        b,
        (contract, ((), ())),
        precision=lax.Precision.HIGHEST,
        preferred_element_type=jnp.float32,
    )


def one_pass(a, b):
    return jnp.dot(a, b, preferred_element_type=jnp.float32)


def two_pieces(x):
    high = x.astype(jnp.bfloat16)
    low = (x - high.astype(jnp.float32)).astype(jnp.bfloat16)
    return high, low


def slot_by_row(codes_row, start, rows):
    slots = lax.broadcasted_iota(jnp.int32, (rows, codes_row.shape[1]), 0) + start
    return jnp.where(slots == codes_row, 1.0, 0.0).astype(jnp.bfloat16)


def row_by_slot(codes_lanes, slots):
    rows, lanes = codes_lanes.shape
    lane = lax.broadcasted_iota(jnp.int32, (rows, lanes), 1)
    parts = [
        jnp.where(lane + first == codes_lanes, 1.0, 0.0).astype(jnp.bfloat16)
        for first in range(0, slots, lanes)
    ]
    return jnp.concatenate(parts, axis=1)


def fill_pieces(pieces, start, x):
    high, low = two_pieces(x)
    cols = x.shape[1]
    pieces[pl.ds(start, x.shape[0]), 0:cols] = high
    pieces[pl.ds(start, x.shape[0]), cols : 2 * cols] = low


def to_rows(codes_lanes, slot_pieces, write):
    total = slot_pieces.shape[0]
    chunk = total // SIDES
    for c in range(SIDES):
        pick = row_by_slot(codes_lanes[c * chunk : (c + 1) * chunk, :], total)
        write(c * chunk, one_pass(pick, slot_pieces[...]))


def halves(x):
    cols = x.shape[1] // 2
    return x[:, :cols] + x[:, cols:]


def apply_local(matrix, codes_row, codes_lanes, slot_pieces, row_pieces, out_pieces, write, less=None):
    total = slot_pieces.shape[0]
    chunk = total // SIDES

    def keep(start, rows):
        row_pieces[start : start + chunk, :] = rows.astype(jnp.bfloat16)

    to_rows(codes_lanes, slot_pieces, keep)
    apply_rows(matrix, codes_row, row_pieces, out_pieces, write, less)


def apply_rows(matrix, codes_row, row_pieces, out_pieces, write, less=None):
    total = row_pieces.shape[0]
    chunk = total // SIDES
    cols = row_pieces.shape[1] // 2
    for c in range(SIDES):
        high, low = two_pieces(matrix[c * chunk : (c + 1) * chunk, :])
        product = halves(one_pass(high, row_pieces[...])) + one_pass(low, row_pieces[:, :cols])
        if less is not None:
            product = less[c * chunk : (c + 1) * chunk, :] - product
        fill_pieces(out_pieces, c * chunk, product)
    for side in range(SIDES):
        pick = slot_by_row(codes_row[...], side * chunk, chunk)
        write(side, halves(one_pass(pick, out_pieces[...])))


def three_pass(a, b):
    a_high, a_low = two_pieces(a)
    b_high, b_low = two_pieces(b)
    both = jnp.concatenate([b_high, b_low], axis=1)
    return halves(one_pass(a_high, both)) + one_pass(a_low, b_high)


def copies(ref, block):
    rows = block.shape[0]
    for q in range(ref.shape[0] // rows):
        ref[q * rows : (q + 1) * rows, :] = block


def modes_kernel(mode_count, place, codes_row, modes, inverse, load, *outs):
    total = codes_row.shape[1]
    cap = total // SIDES
    codes = codes_row[...]
    heading = codes // cap
    even = jnp.where(heading < 2, 1 - lax.rem(place[0], 2), 1 - lax.rem(place[1], 2))
    turn = jnp.where(heading < SIDES, even * (1 - 2 * (heading % 2)), 0)
    codes = codes + turn * cap
    outs[SIDES + 3][...] = codes
    codes = jnp.broadcast_to(codes, (128, total)).astype(jnp.float32)
    codes_lanes = jnp.transpose(codes).astype(jnp.int32)
    x = jnp.concatenate(
        [modes[...], jnp.zeros((PAD - mode_count, total), jnp.float32)], axis=0
    )
    high = x.astype(jnp.bfloat16).astype(jnp.float32)
    middle = (x - high).astype(jnp.bfloat16).astype(jnp.float32)
    low = x - high - middle
    pieces = jnp.concatenate([high, middle, low, jnp.zeros_like(low)], axis=0).astype(jnp.bfloat16)
    moved = one_pass(pieces, row_by_slot(codes_lanes, total))
    upper, lower = moved[0:PAD], moved[PAD : 2 * PAD]
    moved = upper + lower + moved[2 * PAD : 3 * PAD]
    for side in range(SIDES):
        outs[side][...] = moved[:, side * cap : (side + 1) * cap]
    coarse = inverse.shape[1]
    padded = coarse // mode_count * PAD
    old = lax.broadcasted_iota(jnp.int32, (coarse, padded), 0)
    new = lax.broadcasted_iota(jnp.int32, (coarse, padded), 1)
    spread = jnp.where((old // mode_count) * PAD + old % mode_count == new, 1.0, 0.0)
    blank = jnp.zeros((PAD - mode_count, coarse), jnp.float32)
    wide = exact(jnp.concatenate([inverse[...], blank], axis=0), spread)
    blank = jnp.zeros((PAD - mode_count, load.shape[1]), jnp.float32)
    loads = jnp.concatenate([load[...], blank], axis=0)
    copies(outs[SIDES], jnp.concatenate([wide, loads], axis=1))
    outs[SIDES + 1][...] = codes_lanes
    outs[SIDES + 2][...] = jnp.concatenate([upper, lower], axis=0)


def around(i, j):
    right, up = 1 - 2 * (i % 2), 1 - 2 * (j % 2)
    return [(i, j), (i + right, j), (i - right, j), (i, j + up), (i, j - up)]


def mode_blocks(own, partner):
    cap = own[0].shape[1]
    rows = []
    for side in range(SIDES):
        column = [own[side][...]]
        for other in range(SIDES):
            if other == side:
                column.append(-partner[side][...])
            else:
                column.append(jnp.zeros((PAD, cap), jnp.float32))
        rows.append(jnp.concatenate(column, axis=0))
    return rows


def lane_spread(mode_count, lanes):
    shape = (PAD * (SIDES + 1), lanes)
    old = lax.broadcasted_iota(jnp.int32, shape, 0)
    new = lax.broadcasted_iota(jnp.int32, shape, 1)
    spot = (old // PAD) * mode_count + old % PAD
    match = (spot == new % GROUP) & (old % PAD < mode_count)
    return jnp.where(match, 1.0, 0.0)


def place_modes_kernel(mode_count, *refs):
    own, partner, out = refs[0:4], refs[4:8], refs[8]
    cap = own[0].shape[1]
    spread = lane_spread(mode_count, 4 * GROUP)
    for side, block in enumerate(mode_blocks(own, partner)):
        out[side * cap : (side + 1) * cap, :] = exact(block, spread, ((0,), (0,)))


def operator_kernel(modes, matrix, codes_row, codes_lanes, *refs):
    outs = refs[0:4]
    slot_pieces, row_pieces, out_pieces = refs[4:7]
    quarter = codes_lanes.shape[0] // SIDES // 4
    group = lax.broadcasted_iota(jnp.int32, (quarter, 4 * GROUP), 1) // GROUP
    fill_pieces(slot_pieces, 0, modes[...])

    def write(side, block):
        packed = block[:quarter]
        for g in range(1, 4):
            packed = jnp.where(group == g, block[g * quarter : (g + 1) * quarter], packed)
        outs[side][...] = packed
        outs[side].send()

    apply_local(matrix, codes_row, codes_lanes, slot_pieces, row_pieces, out_pieces, write)


def start_kernel(layers, mode_count, place_ref, gathered, modes, codes_row, codes_lanes, gap, flex, *refs):
    slabs, outs = refs[0:4], refs[4:8]
    start_out, inverse_out = refs[8:10]
    slot_pieces, row_pieces, out_pieces = refs[10:13]
    cap = codes_lanes.shape[0] // SIDES
    wide = gathered.shape[0]
    spread = lane_spread(mode_count, GROUP)
    for n, centre in enumerate(around(place_ref[0], place_ref[1])):
        rows = []
        for i, j in around(*centre):
            first = jnp.clip(i * layers + j, 0, wide // PAD - 1) * PAD
            rows.append(gathered[pl.ds(pl.multiple_of(first, PAD), PAD), 0:wide])
        picked = exact(spread, jnp.concatenate(rows, axis=0), ((0,), (0,)))
        inverse_out[n * GROUP : (n + 1) * GROUP, :] = picked
        if n == 0:
            coefficients = exact(picked, gathered[:, wide:])
    inverse_out.send()
    start = three_pass(modes[...], once(coefficients))
    start_out[...] = start
    start_out.send()
    fill_pieces(slot_pieces, 0, start)
    for side in range(SIDES):
        outs[side][cap:, :] = slabs[side][...]

    def write(side, block):
        outs[side][0:cap, :] = block
        outs[side].send()

    apply_local(flex, codes_row, codes_lanes, slot_pieces, row_pieces, out_pieces, write, gap)


def once(x):
    return jnp.concatenate([x, jnp.zeros((3 * GROUP, x.shape[1]), x.dtype)], axis=0)


def repeated(x):
    return jnp.concatenate([x] * 4, axis=0)


def components_of(own_pieces, block_pieces):
    both = one_pass(own_pieces[...].astype(jnp.bfloat16), block_pieces[...])
    cols = both.shape[1] // 2
    return halves(both[0:PAD]) + both[PAD:, :cols]


def grouped(slab):
    group = lax.broadcasted_iota(jnp.int32, slab.shape, 1) // GROUP
    return jnp.concatenate([jnp.where(group == g, slab, 0.0) for g in range(4)], axis=0)


def lagged(side, mine, theirs, coefficients):
    left = jnp.concatenate([grouped(mine[...]), grouped(theirs[...])], axis=1)
    near = coefficients[(side + 1) * GROUP : (side + 2) * GROUP]
    return three_pass(left, jnp.concatenate([repeated(coefficients[0:GROUP]), repeated(-near)], axis=0))


def first_kernel(*refs):
    received, sent = refs[0:4], refs[4:8]
    own, codes_row, codes_lanes, schur = refs[8:12]
    slabs, outs = refs[12:16], refs[16:20]
    gap_out, parts_out = refs[20:22]
    slot_pieces, row_pieces, out_pieces = refs[22:25]
    cap = codes_lanes.shape[0] // SIDES
    for side in range(SIDES):
        block = sent[side][...] - received[side][...]
        gap_out[side * cap : (side + 1) * cap, :] = block
        fill_pieces(slot_pieces, side * cap, block)
    gap_out.send()
    copies(parts_out, components_of(own, slot_pieces))
    parts_out.send()
    for side in range(SIDES):
        outs[side][cap:, :] = slabs[side][...]

    def write(side, block):
        outs[side][0:cap, :] = block
        outs[side].send()

    apply_local(schur, codes_row, codes_lanes, slot_pieces, row_pieces, out_pieces, write)


def stage_kernel(stage, counts, *refs):
    refs = list(refs)

    def take(count):
        taken = refs[:count]
        del refs[:count]
        return taken

    gathered, inverse_rows = take(2)
    mine, theirs, received, sent = take(4), take(4), take(4), take(4)
    modes, own, codes_row, codes_lanes = take(4)
    states_in = take(counts[0])
    matrix = take(1)[0] if stage < 5 else None
    outs = take(4) if stage < 5 else []
    states_out = take(counts[1])
    (parts_out,) = take(1)
    slot_pieces, row_pieces, out_pieces = take(3)
    total = codes_lanes.shape[0]
    cap = total // SIDES
    coefficients = exact(inverse_rows[...], gathered[...])
    direct_all = three_pass(modes[...], once(coefficients[0:GROUP]))
    for side in range(SIDES):
        rows = slice(side * cap, (side + 1) * cap)
        behind = lagged(side, mine[side], theirs[side], coefficients)
        jump = sent[side][...] - received[side][...]
        direct = direct_all[rows, :]
        nextin = None
        if stage == 2:
            (gap,) = states_in
            block = 0.5 * (jump - behind)
            nextin = block
            states_out[0][rows, :] = block
            states_out[1][rows, :] = gap[rows, :] - direct
        elif stage == 3:
            precond, residual = states_in
            block = (jump - behind) / theta_mid
            nextin = residual[rows, :] - block
            states_out[0][rows, :] = nextin
            states_out[1][rows, :] = (precond[rows, :] - direct) / theta_mid
        elif stage == 4:
            residual, step = states_in
            block = 0.5 * (jump + behind)
            nextin = keep_step * step[rows, :] + new_step * block
            states_out[0][rows, :] = residual[rows, :] + direct
            states_out[1][rows, :] = nextin
        else:
            residual, raw_step, start, step = states_in
            block = jump - new_step * behind
            states_out[0][rows, :] = residual[rows, :] - block
            second = raw_step[rows, :] - new_step * direct
            states_out[1][rows, :] = second + start[rows, :] + step[rows, :]
        if nextin is not None:
            fill_pieces(slot_pieces, side * cap, nextin)
        fill_pieces(out_pieces, side * cap, block)
    copies(parts_out, components_of(own, out_pieces))
    for out in (parts_out, *states_out):
        out.send()
    if stage < 5:

        def write(side, block):
            outs[side][...] = block
            outs[side].send()

        apply_local(matrix, codes_row, codes_lanes, slot_pieces, row_pieces, out_pieces, write)


def rows_kernel(codes_lanes, residual, multipliers, modes, residual_out, multipliers_out, modes_out, pieces):
    total, cols = residual.shape
    cap = total // SIDES
    for n, source in enumerate((residual, multipliers, modes)):
        high, low = two_pieces(source[...])
        pieces[:, 2 * n * cols : (2 * n + 1) * cols] = high
        pieces[:, (2 * n + 1) * cols : (2 * n + 2) * cols] = low

    def keep(begin, rows):
        for n, target in enumerate((residual_out, multipliers_out, modes_out)):
            target[begin : begin + cap, :] = halves(rows[:, 2 * n * cols : (2 * n + 2) * cols])

    to_rows(codes_lanes, pieces, keep)


def last_kernel(gathered, inverse_rows, modes, residual, out):
    coefficients = once(exact(inverse_rows[0:GROUP, :], gathered[...]))
    out[...] = residual[...] + three_pass(modes[...], coefficients)


class Incoming:
    def __init__(self, source, first, held, arrived):
        self.held = held
        self.shape = held.shape
        source = source.at[pl.ds(first, held.shape[0])]
        self.copy = pltpu.make_async_copy(source, held, arrived)
        self.copy.start()
        self.here = False

    def wait(self):
        if not self.here:
            self.copy.wait()
            self.here = True

    def __getitem__(self, index):
        self.wait()
        return self.held[index]


class Outgoing:
    def __init__(self, target, held, left):
        self.held = held
        self.shape = held.shape
        self.copy = pltpu.make_async_copy(held, target, left)
        self.sent = False

    def __setitem__(self, index, value):
        self.held[index] = value

    def send(self):
        if not self.sent:
            self.copy.start()
            self.sent = True


def call(kernel, name, outs, inputs, scratch=(), smem=None, parts=None):
    parts = parts or {}
    shapes = []
    for shape in outs:
        shapes.append(jax.ShapeDtypeStruct(shape, jnp.float32) if isinstance(shape, tuple) else shape)
    holds, firsts = [], []
    for n, x in enumerate(inputs):
        first, count = parts.get(n, (0, x.shape[0]))
        firsts.append(first)
        holds.append(pltpu.VMEM((count,) + x.shape[1:], x.dtype))
    holds += [pltpu.VMEM(x.shape, x.dtype) for x in shapes]
    fixed = [] if smem is None else [smem]

    def body(*refs):
        refs = list(refs)
        given, refs = refs[: len(fixed)], refs[len(fixed) :]
        sources, refs = refs[: len(inputs)], refs[len(inputs) :]
        targets, refs = refs[: len(outs)], refs[len(outs) :]
        held, refs = refs[: len(holds)], refs[len(holds) :]
        arrived, left, own = refs[0], refs[1], refs[2:]
        coming = [
            Incoming(source, firsts[n], held[n], arrived.at[n]) for n, source in enumerate(sources)
        ]
        going = [
            Outgoing(target, held[len(inputs) + n], left.at[n]) for n, target in enumerate(targets)
        ]
        kernel(*given, *coming, *going, *own)
        for x in coming:
            x.wait()
        for x in going:
            x.send()
        for x in going:
            x.copy.wait()

    anywhere = pl.BlockSpec(memory_space=pl.ANY)
    return pl.pallas_call(
        body,
        name=name,
        out_shape=shapes,
        in_specs=[pl.BlockSpec(memory_space=pltpu.SMEM)] * len(fixed) + [anywhere] * len(inputs),
        out_specs=[anywhere] * len(outs),
        scratch_shapes=holds
        + [pltpu.SemaphoreType.DMA((len(inputs),)), pltpu.SemaphoreType.DMA((len(outs),))]
        + list(scratch),
        compiler_params=pltpu.CompilerParams(vmem_limit_bytes=58 * 1024 * 1024),
    )(*fixed, *inputs)


def exchange(blocks):
    received = []
    for side, block in enumerate(blocks):
        axis = "sub" if side < 2 else "layer"
        pairs = []
        for i in range(side % 2, lax.axis_size(axis) - 1, 2):
            pairs += [(i, i + 1), (i + 1, i)]
        received.append(lax.ppermute(block, axis, pairs))
    return received


def everywhere(stacked):
    return lax.all_to_all(stacked, ("sub", "layer"), split_axis=0, concat_axis=0, tiled=True)


def per_device(
    local_gap, route_codes, flexibility, dirichlet, rigid_modes, coarse_inverse, rigid_load
):
    gap = local_gap[0, 0]
    flex = flexibility[0, 0]
    schur = dirichlet[0, 0]
    modes = rigid_modes[0, 0]
    mode_count, total = modes.shape
    cap = total // SIDES
    cols = gap.shape[1]
    layers = lax.axis_size("layer")
    wide = lax.axis_size("sub") * layers * PAD
    place = jnp.stack([lax.axis_index("sub"), lax.axis_index("layer")]).astype(jnp.int32)
    pieces = pltpu.VMEM((total, 2 * cols), jnp.bfloat16)
    scratch = [pieces] * 3
    block = [(cap, cols)] * SIDES
    longer = [(cap + cap // 4, cols)] * SIDES
    slab = [(cap // 4, 4 * GROUP)] * SIDES
    whole = (total, cols)
    parts = (wide, cols)
    head, tail = (0, cap), (cap, cap // 4)

    shown = call(
        functools.partial(modes_kernel, mode_count),
        "modes_to_slots",
        [(PAD, cap)] * SIDES
        + [(wide, wide + cols), jax.ShapeDtypeStruct((total, 128), jnp.int32), (2 * PAD, total)]
        + [jax.ShapeDtypeStruct((1, total), jnp.int32)],
        [route_codes[0], modes, coarse_inverse, rigid_load],
        smem=place,
    )
    own, (inverse_load, codes_lanes, own_pieces, codes_row) = shown[:4], shown[4:]
    gathered = everywhere(inverse_load)
    partner = exchange(own)
    (slot_modes,) = call(
        functools.partial(place_modes_kernel, mode_count),
        "place_modes",
        [(total, 4 * GROUP)],
        [*own, *partner],
    )
    slabs = call(
        operator_kernel,
        "dirichlet_on_modes",
        slab,
        [slot_modes, schur, codes_row, codes_lanes],
        scratch,
    )
    shown = call(
        functools.partial(start_kernel, layers, mode_count),
        "start",
        longer + [whole, (5 * GROUP, wide)],
        [gathered, slot_modes, codes_row, codes_lanes, gap, flex, *slabs],
        scratch,
        smem=place,
    )
    sent, (start, inverse_rows) = shown[:4], shown[4:]
    received = exchange(sent)
    schur_slabs = [*sent, *received]
    slabs = call(
        operator_kernel,
        "flexibility_on_modes",
        slab,
        [slot_modes, flex, codes_row, codes_lanes],
        scratch,
    )
    shown = call(
        first_kernel,
        "stage_1",
        longer + [whole, parts],
        [*received, *sent, own_pieces, codes_row, codes_lanes, schur, *slabs],
        scratch,
        parts={n: head for n in range(8)},
    )
    sent, (gap_jump, components) = shown[:4], shown[4:]

    def stage(number, matrix, states_in, sent, received, slabs, components):
        gathered = everywhere(components)
        inputs = [gathered, inverse_rows, *slabs, *received, *sent]
        inputs += [slot_modes, own_pieces, codes_row, codes_lanes, *states_in]
        rows = {n: tail for n in range(2, 10)}
        rows.update({n: head for n in range(10, 18)})
        outs = [whole] * 2 + [parts]
        if matrix is not None:
            inputs, outs = inputs + [matrix], block + outs
        kernel = functools.partial(stage_kernel, number, (len(states_in), 2))
        return call(kernel, "stage_%d" % number, outs, inputs, scratch, parts=rows)

    received = exchange(sent)
    flex_slabs = [*sent, *received]
    shown = stage(2, flex, [gap_jump], sent, received, schur_slabs, components)
    sent, (precond, residual, components) = shown[:4], shown[4:]
    received = exchange(sent)
    shown = stage(3, schur, [precond, residual], sent, received, flex_slabs, components)
    sent, (residual, step, components) = shown[:4], shown[4:]
    received = exchange(sent)
    shown = stage(4, flex, [residual, step], sent, received, schur_slabs, components)
    sent, (residual, raw_step, components) = shown[:4], shown[4:]
    received = exchange(sent)
    states = [residual, raw_step, start, step]
    shown = stage(5, None, states, sent, received, flex_slabs, components)
    residual, multipliers, components = shown

    gathered = everywhere(components)
    residual, multipliers, row_modes = call(
        rows_kernel,
        "slots_to_rows",
        [whole, whole, (total, 4 * GROUP)],
        [codes_lanes, residual, multipliers, slot_modes],
        [pltpu.VMEM((total, 6 * cols), jnp.bfloat16)],
    )
    (residual,) = call(
        last_kernel, "residual", [whole], [gathered, inverse_rows, row_modes, residual]
    )
    return (multipliers[None, None], residual[None, None])


def solution(mesh):
    placed = (
        P("sub", "layer", None, None),
        P("sub", "layer", None),
        P("sub", "layer", None, None),
        P("sub", "layer", None, None),
        P("sub", "layer", None, None),
        P(("sub", "layer"), None),
        P(("sub", "layer"), None),
    )
    return jax.shard_map(
        per_device,
        mesh=mesh,
        in_specs=placed,
        out_specs=(P("sub", "layer", None, None), P("sub", "layer", None, None)),
        check_vma=False,
    )
```

```python
import functools

import jax
import jax.numpy as jnp
from jax import lax
from jax.experimental import pallas as pl
from jax.experimental.pallas import tpu as pltpu
from jax.sharding import PartitionSpec as P

theta_mid = 4.25
delta_half = 3.75
sigma_ratio = theta_mid / delta_half
damping = delta_half / theta_mid
damping_next = 1.0 / (2.0 * sigma_ratio - damping)
keep_step = damping_next * damping
new_step = 2.0 * damping_next / delta_half

GROUP = 32
PAD = 8
SIDES = 4


def exact(a, b, contract=((1,), (0,))):
    return lax.dot_general(
        a,
        b,
        (contract, ((), ())),
        precision=lax.Precision.HIGHEST,
        preferred_element_type=jnp.float32,
    )


def one_pass(a, b):
    return jnp.dot(a, b, preferred_element_type=jnp.float32)


def two_pieces(x):
    high = x.astype(jnp.bfloat16)
    low = (x - high.astype(jnp.float32)).astype(jnp.bfloat16)
    return high, low


def slot_by_row(codes_row, start, rows):
    slots = lax.broadcasted_iota(jnp.int32, (rows, codes_row.shape[1]), 0) + start
    return jnp.where(slots == codes_row, 1.0, 0.0).astype(jnp.bfloat16)


def row_by_slot(codes_lanes, slots):
    rows, lanes = codes_lanes.shape
    lane = lax.broadcasted_iota(jnp.int32, (rows, lanes), 1)
    parts = [
        jnp.where(lane + first == codes_lanes, 1.0, 0.0).astype(jnp.bfloat16)
        for first in range(0, slots, lanes)
    ]
    return jnp.concatenate(parts, axis=1)


def fill_pieces(pieces, start, x):
    high, low = two_pieces(x)
    cols = x.shape[1]
    pieces[pl.ds(start, x.shape[0]), 0:cols] = high
    pieces[pl.ds(start, x.shape[0]), cols : 2 * cols] = low


def to_rows(codes_lanes, slot_pieces, write):
    total = slot_pieces.shape[0]
    chunk = total // SIDES
    for c in range(SIDES):
        pick = row_by_slot(codes_lanes[c * chunk : (c + 1) * chunk, :], total)
        write(c * chunk, one_pass(pick, slot_pieces[...]))


def halves(x):
    cols = x.shape[1] // 2
    return x[:, :cols] + x[:, cols:]


def fetch(matrix, held, arrived):
    chunk = held.shape[0] // SIDES
    pieces = []
    for c in range(SIDES):
        rows = pl.ds(c * chunk, chunk)
        pieces.append(pltpu.make_async_copy(matrix.at[rows], held.at[rows], arrived.at[c]))
        pieces[c].start()
    return pieces, held


def apply_local(fetched, codes_row, codes_lanes, slot_pieces, row_pieces, out_pieces, write, less=None):
    total = slot_pieces.shape[0]
    chunk = total // SIDES

    def keep(start, rows):
        row_pieces[start : start + chunk, :] = rows.astype(jnp.bfloat16)

    to_rows(codes_lanes, slot_pieces, keep)
    apply_rows(fetched, codes_row, row_pieces, out_pieces, write, less)


def apply_rows(fetched, codes_row, row_pieces, out_pieces, write, less=None):
    coming, matrix = fetched
    total = row_pieces.shape[0]
    chunk = total // SIDES
    cols = row_pieces.shape[1] // 2
    for c in range(SIDES):
        coming[c].wait()
        high, low = two_pieces(matrix[c * chunk : (c + 1) * chunk, :])
        product = halves(one_pass(high, row_pieces[...])) + one_pass(low, row_pieces[:, :cols])
        if less is not None:
            product = less[c * chunk : (c + 1) * chunk, :] - product
        fill_pieces(out_pieces, c * chunk, product)
    for side in range(SIDES):
        pick = slot_by_row(codes_row[...], side * chunk, chunk)
        write(side, halves(one_pass(pick, out_pieces[...])))


def three_pass(a, b):
    a_high, a_low = two_pieces(a)
    b_high, b_low = two_pieces(b)
    both = jnp.concatenate([b_high, b_low], axis=1)
    return halves(one_pass(a_high, both)) + one_pass(a_low, b_high)


def copies(ref, block):
    rows = block.shape[0]
    for q in range(ref.shape[0] // rows):
        ref[q * rows : (q + 1) * rows, :] = block


def modes_kernel(mode_count, codes_row, modes, inverse, load, place, *outs):
    total = codes_row.shape[1]
    cap = total // SIDES
    codes = codes_row[...]
    heading = codes // cap
    even = jnp.where(heading < 2, 1 - lax.rem(place[0], 2), 1 - lax.rem(place[1], 2))
    turn = jnp.where(heading < SIDES, even * (1 - 2 * (heading % 2)), 0)
    codes = codes + turn * cap
    outs[SIDES + 3][...] = codes
    codes = jnp.broadcast_to(codes, (128, total)).astype(jnp.float32)
    codes_lanes = jnp.transpose(codes).astype(jnp.int32)
    x = jnp.concatenate(
        [modes[...], jnp.zeros((PAD - mode_count, total), jnp.float32)], axis=0
    )
    high = x.astype(jnp.bfloat16).astype(jnp.float32)
    middle = (x - high).astype(jnp.bfloat16).astype(jnp.float32)
    low = x - high - middle
    pieces = jnp.concatenate([high, middle, low, jnp.zeros_like(low)], axis=0).astype(jnp.bfloat16)
    moved = one_pass(pieces, row_by_slot(codes_lanes, total))
    upper, lower = moved[0:PAD], moved[PAD : 2 * PAD]
    moved = upper + lower + moved[2 * PAD : 3 * PAD]
    for side in range(SIDES):
        outs[side][...] = moved[:, side * cap : (side + 1) * cap]
    coarse = inverse.shape[1]
    padded = coarse // mode_count * PAD
    old = lax.broadcasted_iota(jnp.int32, (coarse, padded), 0)
    new = lax.broadcasted_iota(jnp.int32, (coarse, padded), 1)
    spread = jnp.where((old // mode_count) * PAD + old % mode_count == new, 1.0, 0.0)
    blank = jnp.zeros((PAD - mode_count, coarse), jnp.float32)
    wide = exact(jnp.concatenate([inverse[...], blank], axis=0), spread)
    blank = jnp.zeros((PAD - mode_count, load.shape[1]), jnp.float32)
    loads = jnp.concatenate([load[...], blank], axis=0)
    copies(outs[SIDES], jnp.concatenate([wide, loads], axis=1))
    outs[SIDES + 1][...] = codes_lanes
    outs[SIDES + 2][...] = jnp.concatenate([upper, lower], axis=0)


def around(i, j):
    right, up = 1 - 2 * (i % 2), 1 - 2 * (j % 2)
    return [(i, j), (i + right, j), (i - right, j), (i, j + up), (i, j - up)]


def mode_blocks(own, partner):
    cap = own[0].shape[1]
    rows = []
    for side in range(SIDES):
        column = [own[side][...]]
        for other in range(SIDES):
            if other == side:
                column.append(-partner[side][...])
            else:
                column.append(jnp.zeros((PAD, cap), jnp.float32))
        rows.append(jnp.concatenate(column, axis=0))
    return rows


def lane_spread(mode_count, lanes):
    shape = (PAD * (SIDES + 1), lanes)
    old = lax.broadcasted_iota(jnp.int32, shape, 0)
    new = lax.broadcasted_iota(jnp.int32, shape, 1)
    spot = (old // PAD) * mode_count + old % PAD
    match = (spot == new % GROUP) & (old % PAD < mode_count)
    return jnp.where(match, 1.0, 0.0)


def operators_kernel(mode_count, flex, schur, codes_row, codes_lanes, *refs):
    own, partner = refs[0:4], refs[4:8]
    outs = refs[8:12]
    modes_out = refs[12]
    slot_pieces, row_pieces, out_pieces = refs[13:16]
    schur = fetch(schur, refs[16], refs[17])
    flex = fetch(flex, refs[18], refs[19])
    total = codes_lanes.shape[0]
    cap = total // SIDES
    half = cap // 2
    lanes = 4 * GROUP
    spread = lane_spread(mode_count, lanes)
    for side, block in enumerate(mode_blocks(own, partner)):
        placed = exact(block, spread, ((0,), (0,)))
        first = lax.broadcasted_iota(jnp.int32, placed.shape, 1) < GROUP
        modes_out[side * cap : (side + 1) * cap, :] = jnp.where(first, placed, 0.0)
        fill_pieces(slot_pieces, side * cap, placed)
    group = lax.broadcasted_iota(jnp.int32, (half, lanes), 1) // GROUP

    def write_schur(side, block):
        outs[side][...] = jnp.where(group == 0, block[:half], block[half:])

    def write_flex(side, block):
        mine = jnp.where(group == 2, block[:half], block[half:])
        outs[side][...] = jnp.where(group < 2, outs[side][...], mine)

    apply_local(schur, codes_row, codes_lanes, slot_pieces, row_pieces, out_pieces, write_schur)
    apply_rows(flex, codes_row, row_pieces, out_pieces, write_flex)


def start_kernel(mode_count, layers, flex, gap, codes_row, codes_lanes, *refs):
    slabs = refs[0:4]
    gathered, modes, place_ref = refs[4:7]
    outs = refs[7:11]
    start_out, inverse_out = refs[11:13]
    slot_pieces, row_pieces, out_pieces = refs[13:16]
    flex = fetch(flex, refs[16], refs[17])
    cap = codes_lanes.shape[0] // SIDES
    wide = gathered.shape[0]
    spread = lane_spread(mode_count, GROUP)
    for n, centre in enumerate(around(place_ref[0], place_ref[1])):
        rows = []
        for i, j in around(*centre):
            first = jnp.clip(i * layers + j, 0, wide // PAD - 1) * PAD
            rows.append(gathered[pl.ds(pl.multiple_of(first, PAD), PAD), 0:wide])
        table = jnp.concatenate(rows, axis=0)
        inverse_out[n * GROUP : (n + 1) * GROUP, :] = exact(spread, table, ((0,), (0,)))
    coefficients = repeated(exact(inverse_out[0:GROUP, :], gathered[:, wide:]))
    start = three_pass(modes[...], coefficients)
    start_out[...] = start
    fill_pieces(slot_pieces, 0, start)

    def write(side, block):
        outs[side][0:cap, :] = block
        outs[side][cap:, :] = slabs[side][...]

    apply_local(flex, codes_row, codes_lanes, slot_pieces, row_pieces, out_pieces, write, gap)


def repeated(x):
    return jnp.concatenate([x] * 4, axis=0)


def components_of(own_pieces, block_pieces):
    both = one_pass(own_pieces[...].astype(jnp.bfloat16), block_pieces[...])
    cols = both.shape[1] // 2
    return halves(both[0:PAD]) + both[PAD:, :cols]


def grouped(slab, first):
    group = lax.broadcasted_iota(jnp.int32, slab.shape, 1) // GROUP
    upper = jnp.where(group == first, slab, 0.0)
    lower = jnp.where(group == first + 1, slab, 0.0)
    return jnp.concatenate([upper, lower], axis=0)


def lagged(side, first, mine, theirs, coefficients):
    left = jnp.concatenate([grouped(mine, first), grouped(theirs, first)], axis=1)
    near = coefficients[(side + 1) * GROUP : (side + 2) * GROUP]
    return three_pass(left, jnp.concatenate([repeated(coefficients[0:GROUP]), repeated(-near)], axis=0))


def first_kernel(schur, codes_row, codes_lanes, *refs):
    received, sent, own = refs[0:4], refs[4:8], refs[8]
    outs = refs[9:13]
    gap_out, parts_out, mine_out, theirs_out = refs[13:17]
    slot_pieces, row_pieces, out_pieces = refs[17:20]
    schur = fetch(schur, refs[20], refs[21])
    half = sent[0].shape[0] - codes_lanes.shape[0] // SIDES
    cap = codes_lanes.shape[0] // SIDES
    for side in range(SIDES):
        block = sent[side][0:cap, :] - received[side][0:cap, :]
        gap_out[side * cap : (side + 1) * cap, :] = block
        fill_pieces(slot_pieces, side * cap, block)
        mine_out[side * half : (side + 1) * half, :] = sent[side][cap:, :]
        theirs_out[side * half : (side + 1) * half, :] = received[side][cap:, :]
    copies(parts_out, components_of(own, slot_pieces))

    def write(side, block):
        outs[side][...] = block

    apply_local(schur, codes_row, codes_lanes, slot_pieces, row_pieces, out_pieces, write)


def jump_kernel(*refs):
    received, sent, out = refs[0:4], refs[4:8], refs[8]
    cap = out.shape[0] // SIDES
    for side in range(SIDES):
        out[side * cap : (side + 1) * cap, :] = sent[side][...] - received[side][...]


def stage_kernel(stage, counts, matrix, codes_row, codes_lanes, *refs):
    refs = list(refs)

    def take(count):
        taken = refs[:count]
        del refs[:count]
        return taken

    jumps, mine, theirs = take(3)
    own, gathered, inverse_rows, modes = take(4)
    states_in = take(counts[0])
    outs = take(4) if stage < 5 else []
    states_out = take(counts[1])
    (parts_out,) = take(1)
    slot_pieces, row_pieces, out_pieces = take(3)
    if stage < 5:
        matrix = fetch(matrix, *take(2))
    total = codes_lanes.shape[0]
    cap = total // SIDES
    coefficients = exact(inverse_rows[...], gathered[...])
    direct_all = three_pass(modes[...], repeated(coefficients[0:GROUP]))
    half = mine.shape[0] // SIDES
    for side in range(SIDES):
        rows = slice(side * cap, (side + 1) * cap)
        jump = jumps[rows, :]
        slab = slice(side * half, (side + 1) * half)
        first = 0 if stage in (2, 4) else 2
        behind = lagged(side, first, mine[slab, :], theirs[slab, :], coefficients)
        direct = direct_all[rows, :]
        nextin = None
        if stage == 2:
            (gap,) = states_in
            block = 0.5 * (jump - behind)
            nextin = block
            states_out[0][rows, :] = block
            states_out[1][rows, :] = gap[rows, :] - direct
        elif stage == 3:
            precond, residual = states_in
            block = (jump - behind) / theta_mid
            nextin = residual[rows, :] - block
            states_out[0][rows, :] = nextin
            states_out[1][rows, :] = (precond[rows, :] - direct) / theta_mid
        elif stage == 4:
            residual, step = states_in
            block = 0.5 * (jump + behind)
            nextin = keep_step * step[rows, :] + new_step * block
            states_out[0][rows, :] = residual[rows, :] + direct
            states_out[1][rows, :] = nextin
        else:
            residual, raw_step, start, step = states_in
            block = jump - new_step * behind
            states_out[0][rows, :] = residual[rows, :] - block
            second = raw_step[rows, :] - new_step * direct
            states_out[1][rows, :] = second + start[rows, :] + step[rows, :]
        if nextin is not None:
            fill_pieces(slot_pieces, side * cap, nextin)
        fill_pieces(out_pieces, side * cap, block)
    copies(parts_out, components_of(own, out_pieces))
    if stage < 5:

        def write(side, block):
            outs[side][...] = block

        apply_local(matrix, codes_row, codes_lanes, slot_pieces, row_pieces, out_pieces, write)


def rows_kernel(codes_lanes, residual, multipliers, modes, residual_out, multipliers_out, modes_out, pieces):
    total = residual.shape[0]
    cap = total // SIDES
    for n, source in enumerate((residual, multipliers, modes)):
        high, low = two_pieces(source[...])
        pieces[:, 256 * n : 256 * n + 128] = high
        pieces[:, 256 * n + 128 : 256 * (n + 1)] = low

    def keep(begin, rows):
        for n, target in enumerate((residual_out, multipliers_out, modes_out)):
            target[begin : begin + cap, :] = halves(rows[:, 256 * n : 256 * (n + 1)])

    to_rows(codes_lanes, pieces, keep)


def last_kernel(residual, modes, gathered, inverse_rows, out):
    coefficients = repeated(exact(inverse_rows[0:GROUP, :], gathered[...]))
    out[...] = residual[...] + three_pass(modes[...], coefficients)


def call(kernel, name, outs, inputs, scratch=(), smem=(), left=(), flops=None, room=58):
    spaces = [pltpu.VMEM] * len(inputs)
    for n in smem:
        spaces[n] = pltpu.SMEM
    for n in left:
        spaces[n] = pl.ANY
    shapes = []
    for shape in outs:
        shapes.append(jax.ShapeDtypeStruct(shape, jnp.float32) if isinstance(shape, tuple) else shape)
    return pl.pallas_call(
        kernel,
        name=name,
        out_shape=shapes,
        in_specs=[pl.BlockSpec(memory_space=space) for space in spaces],
        out_specs=[pl.BlockSpec(memory_space=pltpu.VMEM)] * len(outs),
        scratch_shapes=list(scratch),
        cost_estimate=None
        if flops is None
        else pl.CostEstimate(flops=flops, bytes_accessed=0, transcendentals=0),
        compiler_params=pltpu.CompilerParams(vmem_limit_bytes=room * 1024 * 1024),
    )(*inputs)


def exchange(blocks):
    received = []
    for side, block in enumerate(blocks):
        axis = "sub" if side < 2 else "layer"
        pairs = []
        for i in range(side % 2, lax.axis_size(axis) - 1, 2):
            pairs += [(i, i + 1), (i + 1, i)]
        received.append(lax.ppermute(block, axis, pairs))
    return received


def everywhere(stacked):
    return lax.all_to_all(stacked, ("sub", "layer"), split_axis=0, concat_axis=0, tiled=True)


def per_device(
    local_gap, route_codes, flexibility, dirichlet, rigid_modes, coarse_inverse, rigid_load
):
    gap = local_gap[0, 0]
    flex = flexibility[0, 0]
    schur = dirichlet[0, 0]
    modes = rigid_modes[0, 0]
    mode_count, total = modes.shape
    cap = total // SIDES
    cols = gap.shape[1]
    layers = lax.axis_size("layer")
    wide = lax.axis_size("sub") * layers * PAD
    place = jnp.stack([lax.axis_index("sub"), lax.axis_index("layer")]).astype(jnp.int32)
    pieces = pltpu.VMEM((total, 2 * cols), jnp.bfloat16)
    scratch = [pieces] * 3
    block = [(cap, cols)] * SIDES
    whole = (total, cols)
    weight = 128 * total * total * cols
    parts = (wide, cols)
    brought = [pltpu.VMEM((total, total), jnp.float32), pltpu.SemaphoreType.DMA((SIDES,))]

    shown = call(
        functools.partial(modes_kernel, mode_count),
        "modes_to_slots",
        [(PAD, cap)] * SIDES
        + [(wide, wide + cols), jax.ShapeDtypeStruct((total, 128), jnp.int32), (2 * PAD, total)]
        + [jax.ShapeDtypeStruct((1, total), jnp.int32)],
        [route_codes[0], modes, coarse_inverse, rigid_load, place],
        smem=(4,),
    )
    own, (inverse_load, codes_lanes, own_pieces, codes_row) = shown[:4], shown[4:]
    gathered = everywhere(inverse_load)
    partner = exchange(own)
    shown = call(
        functools.partial(operators_kernel, mode_count),
        "operators_on_modes",
        [(cap // 2, 4 * GROUP)] * SIDES + [(total, 4 * GROUP)],
        [flex, schur, codes_row, codes_lanes, *own, *partner],
        scratch + brought * 2,
        left=(0, 1),
    )
    slabs, slot_modes = shown[:4], shown[4]
    shown = call(
        functools.partial(start_kernel, mode_count, layers),
        "start",
        [(cap + cap // 2, cols)] * SIDES + [whole, (5 * GROUP, wide)],
        [flex, gap, codes_row, codes_lanes, *slabs, gathered, slot_modes, place],
        scratch + brought,
        smem=(10,),
        left=(0,),
    )
    sent, (start, inverse_rows) = shown[:4], shown[4:]
    received = exchange(sent)
    shown = call(
        first_kernel,
        "stage_1",
        block + [whole, parts] + [(2 * cap, 4 * GROUP)] * 2,
        [schur, codes_row, codes_lanes, *received, *sent, own_pieces],
        scratch + brought,
        left=(0,),
    )
    sent, (gap_jump, components, mine, theirs) = shown[:4], shown[4:]

    def stage(number, matrix, states_in, sent, components):
        gathered = everywhere(components)
        received = exchange(sent)
        (jumps,) = call(jump_kernel, "jump", [whole], [*received, *sent], flops=weight)
        inputs = [codes_row, codes_lanes, jumps, mine, theirs]
        inputs += [own_pieces, gathered, inverse_rows, slot_modes, *states_in]
        outs = [whole] * 2 + [parts]
        kernel = functools.partial(stage_kernel, number, (len(states_in), 2))
        name = "stage_%d" % number
        if matrix is None:
            return call(functools.partial(kernel, None), name, outs, inputs, scratch)
        return call(kernel, name, block + outs, [matrix] + inputs, scratch + brought, left=(0,))

    shown = stage(2, flex, [gap_jump], sent, components)
    sent, (precond, residual, components) = shown[:4], shown[4:]
    shown = stage(3, schur, [precond, residual], sent, components)
    sent, (residual, step, components) = shown[:4], shown[4:]
    shown = stage(4, flex, [residual, step], sent, components)
    sent, (residual, raw_step, components) = shown[:4], shown[4:]
    shown = stage(5, None, [residual, raw_step, start, step], sent, components)
    residual, multipliers, components = shown

    gathered = everywhere(components)
    residual, multipliers, row_modes = call(
        rows_kernel,
        "slots_to_rows",
        [whole, whole, (total, 4 * GROUP)],
        [codes_lanes, residual, multipliers, slot_modes],
        [pltpu.VMEM((total, 768), jnp.bfloat16)],
    )
    (residual,) = call(
        last_kernel, "residual", [whole], [residual, row_modes, gathered, inverse_rows]
    )
    return (multipliers[None, None], residual[None, None])


def solution(mesh):
    placed = (
        P("sub", "layer", None, None),
        P("sub", "layer", None),
        P("sub", "layer", None, None),
        P("sub", "layer", None, None),
        P("sub", "layer", None, None),
        P(("sub", "layer"), None),
        P(("sub", "layer"), None),
    )
    return jax.shard_map(
        per_device,
        mesh=mesh,
        in_specs=placed,
        out_specs=(P("sub", "layer", None, None), P("sub", "layer", None, None)),
        check_vma=False,
    )
```

```python
import functools

import jax
import jax.numpy as jnp
from jax import lax
from jax.experimental import pallas as pl
from jax.experimental.pallas import tpu as pltpu
from jax.sharding import PartitionSpec as P

theta_mid = 4.25
delta_half = 3.75
sigma_ratio = theta_mid / delta_half
damping = delta_half / theta_mid
damping_next = 1.0 / (2.0 * sigma_ratio - damping)
keep_step = damping_next * damping
new_step = 2.0 * damping_next / delta_half

GROUP = 32
PAD = 8
SIDES = 4


def exact(a, b, contract=((1,), (0,))):
    return lax.dot_general(
        a,
        b,
        (contract, ((), ())),
        precision=lax.Precision.HIGHEST,
        preferred_element_type=jnp.float32,
    )


def one_pass(a, b):
    return jnp.dot(a, b, preferred_element_type=jnp.float32)


def two_pieces(x):
    high = x.astype(jnp.bfloat16)
    low = (x - high.astype(jnp.float32)).astype(jnp.bfloat16)
    return high, low


def slot_by_row(codes_row, start, rows):
    slots = lax.broadcasted_iota(jnp.int32, (rows, codes_row.shape[1]), 0) + start
    return jnp.where(slots == codes_row, 1.0, 0.0).astype(jnp.bfloat16)


def row_by_slot(codes_lanes, slots):
    rows, lanes = codes_lanes.shape
    lane = lax.broadcasted_iota(jnp.int32, (rows, lanes), 1)
    parts = [
        jnp.where(lane + first == codes_lanes, 1.0, 0.0).astype(jnp.bfloat16)
        for first in range(0, slots, lanes)
    ]
    return jnp.concatenate(parts, axis=1)


def fill_pieces(pieces, start, x):
    high, low = two_pieces(x)
    cols = x.shape[1]
    pieces[pl.ds(start, x.shape[0]), 0:cols] = high
    pieces[pl.ds(start, x.shape[0]), cols : 2 * cols] = low


def to_rows(codes_lanes, slot_pieces, write):
    total = slot_pieces.shape[0]
    chunk = total // SIDES
    for c in range(SIDES):
        pick = row_by_slot(codes_lanes[c * chunk : (c + 1) * chunk, :], total)
        write(c * chunk, one_pass(pick, slot_pieces[...]))


def halves(x):
    cols = x.shape[1] // 2
    return x[:, :cols] + x[:, cols:]


def fetch(matrix, held, arrived):
    chunk = held.shape[0] // SIDES
    pieces = []
    for c in range(SIDES):
        rows = pl.ds(c * chunk, chunk)
        pieces.append(pltpu.make_async_copy(matrix.at[rows], held.at[rows], arrived.at[c]))
        pieces[c].start()
    return pieces, held


def apply_local(fetched, codes_row, codes_lanes, slot_pieces, row_pieces, out_pieces, write, less=None):
    total = slot_pieces.shape[0]
    chunk = total // SIDES

    def keep(start, rows):
        row_pieces[start : start + chunk, :] = rows.astype(jnp.bfloat16)

    to_rows(codes_lanes, slot_pieces, keep)
    apply_rows(fetched, codes_row, row_pieces, out_pieces, write, less)


def apply_rows(fetched, codes_row, row_pieces, out_pieces, write, less=None):
    coming, matrix = fetched
    total = row_pieces.shape[0]
    chunk = total // SIDES
    cols = row_pieces.shape[1] // 2
    for c in range(SIDES):
        coming[c].wait()
        high, low = two_pieces(matrix[c * chunk : (c + 1) * chunk, :])
        product = halves(one_pass(high, row_pieces[...])) + one_pass(low, row_pieces[:, :cols])
        if less is not None:
            product = less[c * chunk : (c + 1) * chunk, :] - product
        fill_pieces(out_pieces, c * chunk, product)
    for side in range(SIDES):
        pick = slot_by_row(codes_row[...], side * chunk, chunk)
        write(side, halves(one_pass(pick, out_pieces[...])))


def three_pass(a, b):
    a_high, a_low = two_pieces(a)
    b_high, b_low = two_pieces(b)
    both = jnp.concatenate([b_high, b_low], axis=1)
    return halves(one_pass(a_high, both)) + one_pass(a_low, b_high)


def copies(ref, block):
    rows = block.shape[0]
    for q in range(ref.shape[0] // rows):
        ref[q * rows : (q + 1) * rows, :] = block


def modes_kernel(mode_count, codes_row, modes, inverse, load, place, *outs):
    total = codes_row.shape[1]
    cap = total // SIDES
    codes = codes_row[...]
    heading = codes // cap
    even = jnp.where(heading < 2, 1 - lax.rem(place[0], 2), 1 - lax.rem(place[1], 2))
    turn = jnp.where(heading < SIDES, even * (1 - 2 * (heading % 2)), 0)
    codes = codes + turn * cap
    outs[SIDES + 3][...] = codes
    codes = jnp.broadcast_to(codes, (128, total)).astype(jnp.float32)
    codes_lanes = jnp.transpose(codes).astype(jnp.int32)
    x = jnp.concatenate(
        [modes[...], jnp.zeros((PAD - mode_count, total), jnp.float32)], axis=0
    )
    high = x.astype(jnp.bfloat16).astype(jnp.float32)
    middle = (x - high).astype(jnp.bfloat16).astype(jnp.float32)
    low = x - high - middle
    pieces = jnp.concatenate([high, middle, low, jnp.zeros_like(low)], axis=0).astype(jnp.bfloat16)
    moved = one_pass(pieces, row_by_slot(codes_lanes, total))
    upper, lower = moved[0:PAD], moved[PAD : 2 * PAD]
    moved = upper + lower + moved[2 * PAD : 3 * PAD]
    for side in range(SIDES):
        outs[side][...] = moved[:, side * cap : (side + 1) * cap]
    coarse = inverse.shape[1]
    padded = coarse // mode_count * PAD
    old = lax.broadcasted_iota(jnp.int32, (coarse, padded), 0)
    new = lax.broadcasted_iota(jnp.int32, (coarse, padded), 1)
    spread = jnp.where((old // mode_count) * PAD + old % mode_count == new, 1.0, 0.0)
    blank = jnp.zeros((PAD - mode_count, coarse), jnp.float32)
    wide = exact(jnp.concatenate([inverse[...], blank], axis=0), spread)
    blank = jnp.zeros((PAD - mode_count, load.shape[1]), jnp.float32)
    loads = jnp.concatenate([load[...], blank], axis=0)
    copies(outs[SIDES], jnp.concatenate([wide, loads], axis=1))
    outs[SIDES + 1][...] = codes_lanes
    outs[SIDES + 2][...] = jnp.concatenate([upper, lower], axis=0)


def around(i, j):
    right, up = 1 - 2 * (i % 2), 1 - 2 * (j % 2)
    return [(i, j), (i + right, j), (i - right, j), (i, j + up), (i, j - up)]


def mode_blocks(own, partner):
    cap = own[0].shape[1]
    rows = []
    for side in range(SIDES):
        column = [own[side][...]]
        for other in range(SIDES):
            if other == side:
                column.append(-partner[side][...])
            else:
                column.append(jnp.zeros((PAD, cap), jnp.float32))
        rows.append(jnp.concatenate(column, axis=0))
    return rows


def lane_spread(mode_count, lanes):
    shape = (PAD * (SIDES + 1), lanes)
    old = lax.broadcasted_iota(jnp.int32, shape, 0)
    new = lax.broadcasted_iota(jnp.int32, shape, 1)
    spot = (old // PAD) * mode_count + old % PAD
    match = (spot == new % GROUP) & (old % PAD < mode_count)
    return jnp.where(match, 1.0, 0.0)


def operators_kernel(mode_count, flex, schur, codes_row, codes_lanes, *refs):
    own, partner = refs[0:4], refs[4:8]
    outs = refs[8:12]
    modes_out = refs[12]
    slot_pieces, row_pieces, out_pieces = refs[13:16]
    schur = fetch(schur, refs[16], refs[17])
    flex = fetch(flex, refs[18], refs[19])
    total = codes_lanes.shape[0]
    cap = total // SIDES
    half = cap // 2
    lanes = 4 * GROUP
    spread = lane_spread(mode_count, lanes)
    for side, block in enumerate(mode_blocks(own, partner)):
        placed = exact(block, spread, ((0,), (0,)))
        first = lax.broadcasted_iota(jnp.int32, placed.shape, 1) < GROUP
        modes_out[side * cap : (side + 1) * cap, :] = jnp.where(first, placed, 0.0)
        fill_pieces(slot_pieces, side * cap, placed)
    group = lax.broadcasted_iota(jnp.int32, (half, lanes), 1) // GROUP

    def write_schur(side, block):
        outs[side][...] = jnp.where(group == 0, block[:half], block[half:])

    def write_flex(side, block):
        mine = jnp.where(group == 2, block[:half], block[half:])
        outs[side][...] = jnp.where(group < 2, outs[side][...], mine)

    apply_local(schur, codes_row, codes_lanes, slot_pieces, row_pieces, out_pieces, write_schur)
    apply_rows(flex, codes_row, row_pieces, out_pieces, write_flex)


def start_kernel(mode_count, layers, flex, gap, codes_row, codes_lanes, *refs):
    slabs = refs[0:4]
    gathered, modes, place_ref = refs[4:7]
    outs = refs[7:11]
    start_out, inverse_out = refs[11:13]
    slot_pieces, row_pieces, out_pieces = refs[13:16]
    flex = fetch(flex, refs[16], refs[17])
    cap = codes_lanes.shape[0] // SIDES
    wide = gathered.shape[0]
    spread = lane_spread(mode_count, GROUP)
    for n, centre in enumerate(around(place_ref[0], place_ref[1])):
        rows = []
        for i, j in around(*centre):
            first = jnp.clip(i * layers + j, 0, wide // PAD - 1) * PAD
            rows.append(gathered[pl.ds(pl.multiple_of(first, PAD), PAD), 0:wide])
        table = jnp.concatenate(rows, axis=0)
        inverse_out[n * GROUP : (n + 1) * GROUP, :] = exact(spread, table, ((0,), (0,)))
    coefficients = repeated(exact(inverse_out[0:GROUP, :], gathered[:, wide:]))
    start = three_pass(modes[...], coefficients)
    start_out[...] = start
    fill_pieces(slot_pieces, 0, start)

    def write(side, block):
        outs[side][0:cap, :] = block
        outs[side][cap:, :] = slabs[side][...]

    apply_local(flex, codes_row, codes_lanes, slot_pieces, row_pieces, out_pieces, write, gap)


def repeated(x):
    return jnp.concatenate([x] * 4, axis=0)


def components_of(own_pieces, block_pieces):
    both = one_pass(own_pieces[...].astype(jnp.bfloat16), block_pieces[...])
    cols = both.shape[1] // 2
    return halves(both[0:PAD]) + both[PAD:, :cols]


def grouped(slab, first):
    group = lax.broadcasted_iota(jnp.int32, slab.shape, 1) // GROUP
    upper = jnp.where(group == first, slab, 0.0)
    lower = jnp.where(group == first + 1, slab, 0.0)
    return jnp.concatenate([upper, lower], axis=0)


def lagged(side, first, mine, theirs, coefficients):
    left = jnp.concatenate([grouped(mine, first), grouped(theirs, first)], axis=1)
    near = coefficients[(side + 1) * GROUP : (side + 2) * GROUP]
    return three_pass(left, jnp.concatenate([repeated(coefficients[0:GROUP]), repeated(-near)], axis=0))


def first_kernel(*refs):
    received, sent, own = refs[0:4], refs[4:8], refs[8]
    gap_out, parts_out, mine_out, theirs_out, pieces_out = refs[9:14]
    cap = gap_out.shape[0] // SIDES
    half = mine_out.shape[0] // SIDES
    for side in range(SIDES):
        block = sent[side][0:cap, :] - received[side][0:cap, :]
        gap_out[side * cap : (side + 1) * cap, :] = block
        fill_pieces(pieces_out, side * cap, block)
        mine_out[side * half : (side + 1) * half, :] = sent[side][cap:, :]
        theirs_out[side * half : (side + 1) * half, :] = received[side][cap:, :]
    copies(parts_out, components_of(own, pieces_out))


def product_kernel(matrix, codes_row, codes_lanes, slot_pieces, *refs):
    outs = refs[0:4]
    row_pieces, out_pieces = refs[4:6]
    matrix = fetch(matrix, refs[6], refs[7])

    def write(side, block):
        outs[side][...] = block

    apply_local(matrix, codes_row, codes_lanes, slot_pieces, row_pieces, out_pieces, write)


def stage_kernel(stage, counts, *refs):
    refs = list(refs)

    def take(count):
        taken = refs[:count]
        del refs[:count]
        return taken

    received, sent = take(4), take(4)
    mine, theirs, own, gathered, inverse_rows, modes = take(6)
    states_in = take(counts[0])
    states_out = take(counts[1])
    (parts_out,) = take(1)
    pieces_out = take(1)[0] if stage < 5 else None
    (block_pieces,) = take(1)
    total = modes.shape[0]
    cap = total // SIDES
    coefficients = exact(inverse_rows[...], gathered[...])
    direct_all = three_pass(modes[...], repeated(coefficients[0:GROUP]))
    half = mine.shape[0] // SIDES
    for side in range(SIDES):
        rows = slice(side * cap, (side + 1) * cap)
        jump = sent[side][...] - received[side][...]
        slab = slice(side * half, (side + 1) * half)
        first = 0 if stage in (2, 4) else 2
        behind = lagged(side, first, mine[slab, :], theirs[slab, :], coefficients)
        direct = direct_all[rows, :]
        nextin = None
        if stage == 2:
            (gap,) = states_in
            block = 0.5 * (jump - behind)
            nextin = block
            states_out[0][rows, :] = block
            states_out[1][rows, :] = gap[rows, :] - direct
        elif stage == 3:
            precond, residual = states_in
            block = (jump - behind) / theta_mid
            nextin = residual[rows, :] - block
            states_out[0][rows, :] = nextin
            states_out[1][rows, :] = (precond[rows, :] - direct) / theta_mid
        elif stage == 4:
            residual, step = states_in
            block = 0.5 * (jump + behind)
            nextin = keep_step * step[rows, :] + new_step * block
            states_out[0][rows, :] = residual[rows, :] + direct
            states_out[1][rows, :] = nextin
        else:
            residual, raw_step, start, step = states_in
            block = jump - new_step * behind
            states_out[0][rows, :] = residual[rows, :] - block
            second = raw_step[rows, :] - new_step * direct
            states_out[1][rows, :] = second + start[rows, :] + step[rows, :]
        if nextin is not None:
            fill_pieces(pieces_out, side * cap, nextin)
        fill_pieces(block_pieces, side * cap, block)
    copies(parts_out, components_of(own, block_pieces))


def rows_kernel(codes_lanes, residual, multipliers, modes, residual_out, multipliers_out, modes_out, pieces):
    total = residual.shape[0]
    cap = total // SIDES
    for n, source in enumerate((residual, multipliers, modes)):
        high, low = two_pieces(source[...])
        pieces[:, 256 * n : 256 * n + 128] = high
        pieces[:, 256 * n + 128 : 256 * (n + 1)] = low

    def keep(begin, rows):
        for n, target in enumerate((residual_out, multipliers_out, modes_out)):
            target[begin : begin + cap, :] = halves(rows[:, 256 * n : 256 * (n + 1)])

    to_rows(codes_lanes, pieces, keep)


def last_kernel(residual, modes, gathered, inverse_rows, out):
    coefficients = repeated(exact(inverse_rows[0:GROUP, :], gathered[...]))
    out[...] = residual[...] + three_pass(modes[...], coefficients)


def call(kernel, name, outs, inputs, scratch=(), smem=(), left=(), flops=None, room=58):
    spaces = [pltpu.VMEM] * len(inputs)
    for n in smem:
        spaces[n] = pltpu.SMEM
    for n in left:
        spaces[n] = pl.ANY
    shapes = []
    for shape in outs:
        shapes.append(jax.ShapeDtypeStruct(shape, jnp.float32) if isinstance(shape, tuple) else shape)
    return pl.pallas_call(
        kernel,
        name=name,
        out_shape=shapes,
        in_specs=[pl.BlockSpec(memory_space=space) for space in spaces],
        out_specs=[pl.BlockSpec(memory_space=pltpu.VMEM)] * len(outs),
        scratch_shapes=list(scratch),
        cost_estimate=None
        if flops is None
        else pl.CostEstimate(flops=flops, bytes_accessed=8 * inputs[0].size, transcendentals=0),
        compiler_params=pltpu.CompilerParams(vmem_limit_bytes=room * 1024 * 1024),
    )(*inputs)


def exchange(blocks):
    received = []
    for side, block in enumerate(blocks):
        axis = "sub" if side < 2 else "layer"
        pairs = []
        for i in range(side % 2, lax.axis_size(axis) - 1, 2):
            pairs += [(i, i + 1), (i + 1, i)]
        received.append(lax.ppermute(block, axis, pairs))
    return received


def everywhere(stacked):
    return lax.all_to_all(stacked, ("sub", "layer"), split_axis=0, concat_axis=0, tiled=True)


def per_device(
    local_gap, route_codes, flexibility, dirichlet, rigid_modes, coarse_inverse, rigid_load
):
    gap = local_gap[0, 0]
    flex = flexibility[0, 0]
    schur = dirichlet[0, 0]
    modes = rigid_modes[0, 0]
    mode_count, total = modes.shape
    cap = total // SIDES
    cols = gap.shape[1]
    layers = lax.axis_size("layer")
    wide = lax.axis_size("sub") * layers * PAD
    place = jnp.stack([lax.axis_index("sub"), lax.axis_index("layer")]).astype(jnp.int32)
    pieces = pltpu.VMEM((total, 2 * cols), jnp.bfloat16)
    scratch = [pieces] * 3
    block = [(cap, cols)] * SIDES
    whole = (total, cols)
    parts = (wide, cols)
    brought = [pltpu.VMEM((total, total), jnp.float32), pltpu.SemaphoreType.DMA((SIDES,))]

    shown = call(
        functools.partial(modes_kernel, mode_count),
        "modes_to_slots",
        [(PAD, cap)] * SIDES
        + [(wide, wide + cols), jax.ShapeDtypeStruct((total, 128), jnp.int32), (2 * PAD, total)]
        + [jax.ShapeDtypeStruct((1, total), jnp.int32)],
        [route_codes[0], modes, coarse_inverse, rigid_load, place],
        smem=(4,),
    )
    own, (inverse_load, codes_lanes, own_pieces, codes_row) = shown[:4], shown[4:]
    gathered = everywhere(inverse_load)
    partner = exchange(own)
    shown = call(
        functools.partial(operators_kernel, mode_count),
        "operators_on_modes",
        [(cap // 2, 4 * GROUP)] * SIDES + [(total, 4 * GROUP)],
        [flex, schur, codes_row, codes_lanes, *own, *partner],
        scratch + brought * 2,
        left=(0, 1),
    )
    slabs, slot_modes = shown[:4], shown[4]
    shown = call(
        functools.partial(start_kernel, mode_count, layers),
        "start",
        [(cap + cap // 2, cols)] * SIDES + [whole, (5 * GROUP, wide)],
        [flex, gap, codes_row, codes_lanes, *slabs, gathered, slot_modes, place],
        scratch + brought,
        smem=(10,),
        left=(0,),
    )
    sent, (start, inverse_rows) = shown[:4], shown[4:]
    received = exchange(sent)
    in_pieces = jax.ShapeDtypeStruct((total, 2 * cols), jnp.bfloat16)
    gap_jump, components, mine, theirs, ready = call(
        first_kernel,
        "stage_1",
        [whole, parts, (2 * cap, 4 * GROUP), (2 * cap, 4 * GROUP), in_pieces],
        [*received, *sent, own_pieces],
    )

    def product(matrix, name, ready):
        return call(
            product_kernel,
            name,
            block,
            [matrix, codes_row, codes_lanes, ready],
            [pieces] * 2 + brought,
            left=(0,),
            flops=16 * total * total * cols,
        )

    def stage(number, states_in, sent, received, components):
        inputs = [*received, *sent, mine, theirs, own_pieces, components, inverse_rows, slot_modes]
        outs = [whole] * 2 + [parts]
        if number < 5:
            outs = outs + [in_pieces]
        kernel = functools.partial(stage_kernel, number, (len(states_in), 2))
        return call(kernel, "stage_%d" % number, outs, inputs + states_in, [pieces])

    components = everywhere(components)
    sent = product(schur, "product_1", ready)
    received = exchange(sent)
    shown = stage(2, [gap_jump], sent, received, components)
    precond, residual, components, ready = shown
    components = everywhere(components)
    sent = product(flex, "product_2", ready)
    received = exchange(sent)
    shown = stage(3, [precond, residual], sent, received, components)
    residual, step, components, ready = shown
    components = everywhere(components)
    sent = product(schur, "product_3", ready)
    received = exchange(sent)
    shown = stage(4, [residual, step], sent, received, components)
    residual, raw_step, components, ready = shown
    components = everywhere(components)
    sent = product(flex, "product_4", ready)
    received = exchange(sent)
    shown = stage(5, [residual, raw_step, start, step], sent, received, components)
    residual, multipliers, components = shown

    gathered = everywhere(components)
    residual, multipliers, row_modes = call(
        rows_kernel,
        "slots_to_rows",
        [whole, whole, (total, 4 * GROUP)],
        [codes_lanes, residual, multipliers, slot_modes],
        [pltpu.VMEM((total, 768), jnp.bfloat16)],
    )
    (residual,) = call(
        last_kernel, "residual", [whole], [residual, row_modes, gathered, inverse_rows]
    )
    return (multipliers[None, None], residual[None, None])


def solution(mesh):
    placed = (
        P("sub", "layer", None, None),
        P("sub", "layer", None),
        P("sub", "layer", None, None),
        P("sub", "layer", None, None),
        P("sub", "layer", None, None),
        P(("sub", "layer"), None),
        P(("sub", "layer"), None),
    )
    return jax.shard_map(
        per_device,
        mesh=mesh,
        in_specs=placed,
        out_specs=(P("sub", "layer", None, None), P("sub", "layer", None, None)),
        check_vma=False,
    )
```

```python
import functools

import jax
import jax.numpy as jnp
from jax import lax
from jax.experimental import pallas as pl
from jax.experimental.pallas import tpu as pltpu
from jax.sharding import PartitionSpec as P

theta_mid = 4.25
delta_half = 3.75
sigma_ratio = theta_mid / delta_half
damping = delta_half / theta_mid
damping_next = 1.0 / (2.0 * sigma_ratio - damping)
keep_step = damping_next * damping
new_step = 2.0 * damping_next / delta_half

GROUP = 32
PAD = 8
SIDES = 4


def exact(a, b, contract=((1,), (0,))):
    return lax.dot_general(
        a,
        b,
        (contract, ((), ())),
        precision=lax.Precision.HIGHEST,
        preferred_element_type=jnp.float32,
    )


def one_pass(a, b):
    return jnp.dot(a, b, preferred_element_type=jnp.float32)


def two_pieces(x):
    high = x.astype(jnp.bfloat16)
    low = (x - high.astype(jnp.float32)).astype(jnp.bfloat16)
    return high, low


def slot_by_row(codes_row, start, rows):
    slots = lax.broadcasted_iota(jnp.int32, (rows, codes_row.shape[1]), 0) + start
    return jnp.where(slots == codes_row, 1.0, 0.0).astype(jnp.bfloat16)


def row_by_slot(codes_lanes, slots):
    rows, lanes = codes_lanes.shape
    lane = lax.broadcasted_iota(jnp.int32, (rows, lanes), 1)
    parts = [
        jnp.where(lane + first == codes_lanes, 1.0, 0.0).astype(jnp.bfloat16)
        for first in range(0, slots, lanes)
    ]
    return jnp.concatenate(parts, axis=1)


def fill_pieces(pieces, start, x):
    high, low = two_pieces(x)
    cols = x.shape[1]
    pieces[pl.ds(start, x.shape[0]), 0:cols] = high
    pieces[pl.ds(start, x.shape[0]), cols : 2 * cols] = low


def to_rows(codes_lanes, slot_pieces, write):
    total = slot_pieces.shape[0]
    chunk = total // SIDES
    for c in range(SIDES):
        pick = row_by_slot(codes_lanes[c * chunk : (c + 1) * chunk, :], total)
        write(c * chunk, one_pass(pick, slot_pieces[...]))


def halves(x):
    cols = x.shape[1] // 2
    return x[:, :cols] + x[:, cols:]


def fetch(matrix, held, arrived):
    chunk = held.shape[0] // SIDES
    pieces = []
    for c in range(SIDES):
        rows = pl.ds(c * chunk, chunk)
        pieces.append(pltpu.make_async_copy(matrix.at[rows], held.at[rows], arrived.at[c]))
        pieces[c].start()
    return pieces, held


def apply_local(fetched, codes_row, codes_lanes, slot_pieces, row_pieces, out_pieces, write, less=None):
    total = slot_pieces.shape[0]
    chunk = total // SIDES

    def keep(start, rows):
        row_pieces[start : start + chunk, :] = rows.astype(jnp.bfloat16)

    to_rows(codes_lanes, slot_pieces, keep)
    apply_rows(fetched, codes_row, row_pieces, out_pieces, write, less)


def apply_rows(fetched, codes_row, row_pieces, out_pieces, write, less=None):
    coming, matrix = fetched
    total = row_pieces.shape[0]
    chunk = total // SIDES
    cols = row_pieces.shape[1] // 2
    for c in range(SIDES):
        coming[c].wait()
        high, low = two_pieces(matrix[c * chunk : (c + 1) * chunk, :])
        product = halves(one_pass(high, row_pieces[...])) + one_pass(low, row_pieces[:, :cols])
        if less is not None:
            product = less[c * chunk : (c + 1) * chunk, :] - product
        fill_pieces(out_pieces, c * chunk, product)
    for side in range(SIDES):
        pick = slot_by_row(codes_row[...], side * chunk, chunk)
        write(side, halves(one_pass(pick, out_pieces[...])))


def three_pass(a, b):
    a_high, a_low = two_pieces(a)
    b_high, b_low = two_pieces(b)
    both = jnp.concatenate([b_high, b_low], axis=1)
    return halves(one_pass(a_high, both)) + one_pass(a_low, b_high)


def copies(ref, block):
    rows = block.shape[0]
    for q in range(ref.shape[0] // rows):
        ref[q * rows : (q + 1) * rows, :] = block


def modes_kernel(mode_count, codes_row, modes, inverse, load, place, *outs):
    total = codes_row.shape[1]
    cap = total // SIDES
    codes = codes_row[...]
    heading = codes // cap
    even = jnp.where(heading < 2, 1 - lax.rem(place[0], 2), 1 - lax.rem(place[1], 2))
    turn = jnp.where(heading < SIDES, even * (1 - 2 * (heading % 2)), 0)
    codes = codes + turn * cap
    outs[SIDES + 3][...] = codes
    codes = jnp.broadcast_to(codes, (128, total)).astype(jnp.float32)
    codes_lanes = jnp.transpose(codes).astype(jnp.int32)
    x = jnp.concatenate(
        [modes[:, 0, :], jnp.zeros((PAD - mode_count, total), jnp.float32)], axis=0
    )
    high = x.astype(jnp.bfloat16).astype(jnp.float32)
    middle = (x - high).astype(jnp.bfloat16).astype(jnp.float32)
    low = x - high - middle
    pieces = jnp.concatenate([high, middle, low, jnp.zeros_like(low)], axis=0).astype(jnp.bfloat16)
    moved = one_pass(pieces, row_by_slot(codes_lanes, total))
    upper, lower = moved[0:PAD], moved[PAD : 2 * PAD]
    moved = upper + lower + moved[2 * PAD : 3 * PAD]
    for side in range(SIDES):
        outs[side][...] = moved[:, side * cap : (side + 1) * cap]
    coarse = inverse.shape[1]
    padded = coarse // mode_count * PAD
    old = lax.broadcasted_iota(jnp.int32, (coarse, padded), 0)
    new = lax.broadcasted_iota(jnp.int32, (coarse, padded), 1)
    spread = jnp.where((old // mode_count) * PAD + old % mode_count == new, 1.0, 0.0)
    blank = jnp.zeros((PAD - mode_count, coarse), jnp.float32)
    wide = exact(jnp.concatenate([inverse[...], blank], axis=0), spread)
    blank = jnp.zeros((PAD - mode_count, load.shape[1]), jnp.float32)
    loads = jnp.concatenate([load[...], blank], axis=0)
    copies(outs[SIDES], jnp.concatenate([wide, loads], axis=1))
    outs[SIDES + 1][...] = codes_lanes
    outs[SIDES + 2][...] = jnp.concatenate([upper, lower], axis=0)


def around(i, j):
    right, up = 1 - 2 * (i % 2), 1 - 2 * (j % 2)
    return [(i, j), (i + right, j), (i - right, j), (i, j + up), (i, j - up)]


def mode_blocks(own, partner):
    cap = own[0].shape[1]
    rows = []
    for side in range(SIDES):
        column = [own[side][...]]
        for other in range(SIDES):
            if other == side:
                column.append(-partner[side][...])
            else:
                column.append(jnp.zeros((PAD, cap), jnp.float32))
        rows.append(jnp.concatenate(column, axis=0))
    return rows


def lane_spread(mode_count, lanes):
    shape = (PAD * (SIDES + 1), lanes)
    old = lax.broadcasted_iota(jnp.int32, shape, 0)
    new = lax.broadcasted_iota(jnp.int32, shape, 1)
    spot = (old // PAD) * mode_count + old % PAD
    match = (spot == new % GROUP) & (old % PAD < mode_count)
    return jnp.where(match, 1.0, 0.0)


def operators_kernel(mode_count, flex, schur, codes_row, codes_lanes, *refs):
    own, partner = refs[0:4], refs[4:8]
    outs = refs[8:12]
    modes_out = refs[12]
    slot_pieces, row_pieces, out_pieces = refs[13:16]
    schur = fetch(schur, refs[16], refs[17])
    flex = fetch(flex, refs[18], refs[19])
    total = codes_lanes.shape[0]
    cap = total // SIDES
    half = cap // 2
    lanes = 4 * GROUP
    spread = lane_spread(mode_count, lanes)
    for side, block in enumerate(mode_blocks(own, partner)):
        placed = exact(block, spread, ((0,), (0,)))
        first = lax.broadcasted_iota(jnp.int32, placed.shape, 1) < GROUP
        modes_out[side * cap : (side + 1) * cap, :] = jnp.where(first, placed, 0.0)
        fill_pieces(slot_pieces, side * cap, placed)
    group = lax.broadcasted_iota(jnp.int32, (half, lanes), 1) // GROUP

    def write_schur(side, block):
        outs[side][...] = jnp.where(group == 0, block[:half], block[half:])

    def write_flex(side, block):
        mine = jnp.where(group == 2, block[:half], block[half:])
        outs[side][...] = jnp.where(group < 2, outs[side][...], mine)

    apply_local(schur, codes_row, codes_lanes, slot_pieces, row_pieces, out_pieces, write_schur)
    apply_rows(flex, codes_row, row_pieces, out_pieces, write_flex)


def start_kernel(mode_count, layers, flex, gap, codes_row, codes_lanes, *refs):
    slabs = refs[0:4]
    gathered, modes, place_ref = refs[4:7]
    outs = refs[7:11]
    start_out, inverse_out = refs[11:13]
    slot_pieces, row_pieces, out_pieces = refs[13:16]
    flex = fetch(flex, refs[16], refs[17])
    cap = codes_lanes.shape[0] // SIDES
    wide = gathered.shape[0]
    spread = lane_spread(mode_count, GROUP)
    for n, centre in enumerate(around(place_ref[0], place_ref[1])):
        rows = []
        for i, j in around(*centre):
            first = jnp.clip(i * layers + j, 0, wide // PAD - 1) * PAD
            rows.append(gathered[pl.ds(pl.multiple_of(first, PAD), PAD), 0:wide])
        table = jnp.concatenate(rows, axis=0)
        inverse_out[n * GROUP : (n + 1) * GROUP, :] = exact(spread, table, ((0,), (0,)))
    coefficients = repeated(exact(inverse_out[0:GROUP, :], gathered[:, wide:]))
    start = three_pass(modes[...], coefficients)
    start_out[...] = start
    fill_pieces(slot_pieces, 0, start)

    def write(side, block):
        outs[side][0:cap, :] = block
        outs[side][cap:, :] = slabs[side][...]

    apply_local(flex, codes_row, codes_lanes, slot_pieces, row_pieces, out_pieces, write, gap)


def repeated(x):
    return jnp.concatenate([x] * 4, axis=0)


def components_of(own_pieces, block_pieces):
    both = one_pass(own_pieces[...].astype(jnp.bfloat16), block_pieces[...])
    cols = both.shape[1] // 2
    return halves(both[0:PAD]) + both[PAD:, :cols]


def grouped(slab, first):
    group = lax.broadcasted_iota(jnp.int32, slab.shape, 1) // GROUP
    upper = jnp.where(group == first, slab, 0.0)
    lower = jnp.where(group == first + 1, slab, 0.0)
    return jnp.concatenate([upper, lower], axis=0)


def lagged(side, first, mine, theirs, coefficients):
    left = jnp.concatenate([grouped(mine, first), grouped(theirs, first)], axis=1)
    near = coefficients[(side + 1) * GROUP : (side + 2) * GROUP]
    return three_pass(left, jnp.concatenate([repeated(coefficients[0:GROUP]), repeated(-near)], axis=0))


def first_kernel(schur, codes_row, codes_lanes, *refs):
    received, sent, own = refs[0:4], refs[4:8], refs[8]
    outs = refs[9:13]
    gap_out, parts_out, mine_out, theirs_out = refs[13:17]
    slot_pieces, row_pieces, out_pieces = refs[17:20]
    schur = fetch(schur, refs[20], refs[21])
    half = sent[0].shape[0] - codes_lanes.shape[0] // SIDES
    cap = codes_lanes.shape[0] // SIDES
    for side in range(SIDES):
        block = sent[side][0:cap, :] - received[side][0:cap, :]
        gap_out[side * cap : (side + 1) * cap, :] = block
        fill_pieces(slot_pieces, side * cap, block)
        mine_out[side * half : (side + 1) * half, :] = sent[side][cap:, :]
        theirs_out[side * half : (side + 1) * half, :] = received[side][cap:, :]
    copies(parts_out, components_of(own, slot_pieces))

    def write(side, block):
        outs[side][...] = block

    apply_local(schur, codes_row, codes_lanes, slot_pieces, row_pieces, out_pieces, write)


def stage_kernel(stage, matrix, codes_row, codes_lanes, *refs):
    refs = list(refs)

    def take(count):
        taken = refs[:count]
        del refs[:count]
        return taken

    received, sent = take(4), take(4)
    mine, theirs, own, gathered, inverse_rows = take(5)
    (state_in,) = take(1) if stage > 2 else [None]
    outs = take(4) if stage < 5 else []
    state_out, parts_out = take(2)
    slot_pieces, row_pieces, out_pieces = take(3)
    if stage < 5:
        matrix = fetch(matrix, *take(2))
    total = codes_lanes.shape[0]
    cap = total // SIDES
    half = mine.shape[0] // SIDES
    coefficients = exact(inverse_rows[...], gathered[...])
    for side in range(SIDES):
        rows = slice(side * cap, (side + 1) * cap)
        slab = slice(side * half, (side + 1) * half)
        jump = sent[side][...] - received[side][...]
        first = 0 if stage in (2, 4) else 2
        behind = lagged(side, first, mine[slab, :], theirs[slab, :], coefficients)
        if stage == 2:
            block = 0.5 * (jump - behind)
            state = block
        elif stage == 3:
            block = (jump - behind) / theta_mid
            state = state_in[rows, :] - block
        elif stage == 4:
            block = 0.5 * (jump + behind)
            state = keep_step * state_in[rows, :] + new_step * block
        else:
            block = jump - new_step * behind
            state = state_in[rows, :] - block
        state_out[rows, :] = state
        if stage < 5:
            fill_pieces(slot_pieces, side * cap, state)
        fill_pieces(out_pieces, side * cap, block)
    copies(parts_out, components_of(own, out_pieces))
    if stage < 5:

        def write(side, block):
            outs[side][...] = block

        apply_local(matrix, codes_row, codes_lanes, slot_pieces, row_pieces, out_pieces, write)


def direct_of(modes, gathered, inverse_rows):
    coefficients = exact(inverse_rows[0:GROUP, :], gathered[...])
    return three_pass(modes[...], repeated(coefficients))


def update_kernel(stage, state, modes, gathered, inverse_rows, after, out):
    direct = direct_of(modes, gathered, inverse_rows)
    if stage == 2:
        out[...] = state[...] - direct
    elif stage == 3:
        out[...] = (state[...] - direct) / theta_mid
    else:
        out[...] = state[...] + direct


def rows_kernel(codes_lanes, residual, raw_step, start, step, modes, gathered, inverse_rows, *refs):
    targets, pieces = refs[0:3], refs[3]
    total, cols = residual.shape
    cap = total // SIDES
    direct = direct_of(modes, gathered, inverse_rows)
    multipliers = raw_step[...] - new_step * direct + start[...] + step[...]
    for n, source in enumerate((residual[...], multipliers, modes[...])):
        high, low = two_pieces(source)
        pieces[:, 2 * n * cols : (2 * n + 1) * cols] = high
        pieces[:, (2 * n + 1) * cols : (2 * n + 2) * cols] = low

    def keep(begin, rows):
        for n, target in enumerate(targets):
            target[begin : begin + cap, :] = halves(rows[:, 2 * n * cols : (2 * n + 2) * cols])

    to_rows(codes_lanes, pieces, keep)


def last_kernel(residual, modes, gathered, inverse_rows, out):
    coefficients = repeated(exact(inverse_rows[0:GROUP, :], gathered[...]))
    out[...] = residual[...] + three_pass(modes[...], coefficients)


def call(kernel, name, outs, inputs, scratch=(), smem=(), left=(), flops=None, room=58):
    spaces = [pltpu.VMEM] * len(inputs)
    for n in smem:
        spaces[n] = pltpu.SMEM
    for n in left:
        spaces[n] = pl.ANY
    shapes = []
    for shape in outs:
        shapes.append(jax.ShapeDtypeStruct(shape, jnp.float32) if isinstance(shape, tuple) else shape)
    return pl.pallas_call(
        kernel,
        name=name,
        out_shape=shapes,
        in_specs=[pl.BlockSpec(memory_space=space) for space in spaces],
        out_specs=[pl.BlockSpec(memory_space=pltpu.VMEM)] * len(outs),
        scratch_shapes=list(scratch),
        cost_estimate=None
        if flops is None
        else pl.CostEstimate(flops=flops, bytes_accessed=16 * inputs[0].size, transcendentals=0),
        compiler_params=pltpu.CompilerParams(vmem_limit_bytes=room * 1024 * 1024),
    )(*inputs)


def exchange(blocks):
    received = []
    for side, block in enumerate(blocks):
        axis = "sub" if side < 2 else "layer"
        pairs = []
        for i in range(side % 2, lax.axis_size(axis) - 1, 2):
            pairs += [(i, i + 1), (i + 1, i)]
        received.append(lax.ppermute(block, axis, pairs))
    return received


def everywhere(stacked):
    return lax.all_to_all(stacked, ("sub", "layer"), split_axis=0, concat_axis=0, tiled=True)


def per_device(
    local_gap, route_codes, flexibility, dirichlet, rigid_modes, coarse_inverse, rigid_load
):
    gap = local_gap[0, 0]
    flex = flexibility[0, 0]
    schur = dirichlet[0, 0]
    mode_count, total = rigid_modes.shape[2:]
    modes = rigid_modes.reshape(mode_count, 1, total)
    cap = total // SIDES
    cols = gap.shape[1]
    layers = lax.axis_size("layer")
    wide = lax.axis_size("sub") * layers * PAD
    place = jnp.stack([lax.axis_index("sub"), lax.axis_index("layer")]).astype(jnp.int32)
    pieces = pltpu.VMEM((total, 2 * cols), jnp.bfloat16)
    scratch = [pieces] * 3
    block = [(cap, cols)] * SIDES
    whole = (total, cols)
    parts = (wide, cols)
    brought = [pltpu.VMEM((total, total), jnp.float32), pltpu.SemaphoreType.DMA((SIDES,))]

    shown = call(
        functools.partial(modes_kernel, mode_count),
        "modes_to_slots",
        [(PAD, cap)] * SIDES
        + [(wide, wide + cols), jax.ShapeDtypeStruct((total, 128), jnp.int32), (2 * PAD, total)]
        + [jax.ShapeDtypeStruct((1, total), jnp.int32)],
        [route_codes[0], modes, coarse_inverse, rigid_load, place],
        smem=(4,),
    )
    own, (inverse_load, codes_lanes, own_pieces, codes_row) = shown[:4], shown[4:]
    gathered = everywhere(inverse_load)
    partner = exchange(own)
    shown = call(
        functools.partial(operators_kernel, mode_count),
        "operators_on_modes",
        [(cap // 2, 4 * GROUP)] * SIDES + [(total, 4 * GROUP)],
        [flex, schur, codes_row, codes_lanes, *own, *partner],
        scratch + brought * 2,
        left=(0, 1),
    )
    slabs, slot_modes = shown[:4], shown[4]
    shown = call(
        functools.partial(start_kernel, mode_count, layers),
        "start",
        [(cap + cap // 2, cols)] * SIDES + [whole, (5 * GROUP, wide)],
        [flex, gap, codes_row, codes_lanes, *slabs, gathered, slot_modes, place],
        scratch + brought,
        smem=(10,),
        left=(0,),
    )
    sent, (start, inverse_rows) = shown[:4], shown[4:]
    received = exchange(sent)
    shown = call(
        first_kernel,
        "stage_1",
        block + [whole, parts] + [(2 * cap, 4 * GROUP)] * 2,
        [schur, codes_row, codes_lanes, *received, *sent, own_pieces],
        scratch + brought,
        left=(0,),
    )
    sent, (gap_jump, components, mine, theirs) = shown[:4], shown[4:]

    def stage(number, matrix, states_in, sent, components):
        gathered = everywhere(components)
        received = exchange(sent)
        inputs = [codes_row, codes_lanes, *received, *sent, mine, theirs]
        inputs += [own_pieces, gathered, inverse_rows, *states_in]
        outs = [whole, parts]
        kernel = functools.partial(stage_kernel, number)
        name = "stage_%d" % number
        if matrix is None:
            shown = call(functools.partial(kernel, None), name, outs, inputs, scratch)
        else:
            inputs = [matrix] + inputs
            shown = call(kernel, name, block + outs, inputs, scratch + brought, left=(0,))
        return gathered, shown[:-2], *shown[-2:]

    def update(number, state, gathered, after):
        (out,) = call(
            functools.partial(update_kernel, number),
            "update_%d" % number,
            [whole],
            [state, slot_modes, gathered, inverse_rows, after],
            left=(4,),
            flops=8 * total * cols * cols,
        )
        return out

    gathered, sent, precond, components = stage(2, flex, [], sent, components)
    residual = update(2, gap_jump, gathered, components)
    gathered, sent, residual, components = stage(3, schur, [residual], sent, components)
    step = update(3, precond, gathered, components)
    gathered, sent, raw_step, components = stage(4, flex, [step], sent, components)
    residual = update(4, residual, gathered, components)
    gathered, _, residual, components = stage(5, None, [residual], sent, components)
    last_gathered = everywhere(components)
    residual, multipliers, row_modes = call(
        rows_kernel,
        "slots_to_rows",
        [whole, whole, (total, 4 * GROUP)],
        [codes_lanes, residual, raw_step, start, step, slot_modes, gathered, inverse_rows],
        [pltpu.VMEM((total, 6 * cols), jnp.bfloat16)],
    )
    gathered = last_gathered
    (residual,) = call(
        last_kernel, "residual", [whole], [residual, row_modes, gathered, inverse_rows]
    )
    return (multipliers[None, None], residual[None, None])


def solution(mesh):
    placed = (
        P("sub", "layer", None, None),
        P("sub", "layer", None),
        P("sub", "layer", None, None),
        P("sub", "layer", None, None),
        P("sub", "layer", None, None),
        P(("sub", "layer"), None),
        P(("sub", "layer"), None),
    )
    return jax.shard_map(
        per_device,
        mesh=mesh,
        in_specs=placed,
        out_specs=(P("sub", "layer", None, None), P("sub", "layer", None, None)),
        check_vma=False,
    )
```

```python
import functools

import jax
import jax.numpy as jnp
from jax import lax
from jax.experimental import pallas as pl
from jax.experimental.pallas import tpu as pltpu
from jax.sharding import PartitionSpec as P

theta_mid = 4.25
delta_half = 3.75
sigma_ratio = theta_mid / delta_half
damping = delta_half / theta_mid
damping_next = 1.0 / (2.0 * sigma_ratio - damping)
keep_step = damping_next * damping
new_step = 2.0 * damping_next / delta_half

GROUP = 32
PAD = 8
SIDES = 4


def exact(a, b, contract=((1,), (0,))):
    return lax.dot_general(
        a,
        b,
        (contract, ((), ())),
        precision=lax.Precision.HIGHEST,
        preferred_element_type=jnp.float32,
    )


def one_pass(a, b):
    return jnp.dot(a, b, preferred_element_type=jnp.float32)


def two_pieces(x):
    high = x.astype(jnp.bfloat16)
    low = (x - high.astype(jnp.float32)).astype(jnp.bfloat16)
    return high, low


def slot_by_row(codes_row, start, rows):
    slots = lax.broadcasted_iota(jnp.int32, (rows, codes_row.shape[1]), 0) + start
    return jnp.where(slots == codes_row, 1.0, 0.0).astype(jnp.bfloat16)


def row_by_slot(codes_lanes, slots):
    rows, lanes = codes_lanes.shape
    lane = lax.broadcasted_iota(jnp.int32, (rows, lanes), 1)
    parts = [
        jnp.where(lane + first == codes_lanes, 1.0, 0.0).astype(jnp.bfloat16)
        for first in range(0, slots, lanes)
    ]
    return jnp.concatenate(parts, axis=1)


def fill_pieces(pieces, start, x):
    high, low = two_pieces(x)
    cols = x.shape[1]
    pieces[pl.ds(start, x.shape[0]), 0:cols] = high
    pieces[pl.ds(start, x.shape[0]), cols : 2 * cols] = low


def to_rows(codes_lanes, slot_pieces, write):
    total = slot_pieces.shape[0]
    chunk = total // SIDES
    for c in range(SIDES):
        pick = row_by_slot(codes_lanes[c * chunk : (c + 1) * chunk, :], total)
        write(c * chunk, one_pass(pick, slot_pieces[...]))


def halves(x):
    cols = x.shape[1] // 2
    return x[:, :cols] + x[:, cols:]


def fetch(matrix, held, arrived):
    chunk = held.shape[0] // SIDES
    pieces = []
    for c in range(SIDES):
        rows = pl.ds(c * chunk, chunk)
        pieces.append(pltpu.make_async_copy(matrix.at[rows], held.at[rows], arrived.at[c]))
        pieces[c].start()
    return pieces, held


def apply_local(fetched, codes_row, codes_lanes, slot_pieces, row_pieces, out_pieces, write, less=None):
    total = slot_pieces.shape[0]
    chunk = total // SIDES

    def keep(start, rows):
        row_pieces[start : start + chunk, :] = rows.astype(jnp.bfloat16)

    to_rows(codes_lanes, slot_pieces, keep)
    apply_rows(fetched, codes_row, row_pieces, out_pieces, write, less)


def apply_rows(fetched, codes_row, row_pieces, out_pieces, write, less=None):
    coming, matrix = fetched
    total = row_pieces.shape[0]
    chunk = total // SIDES
    cols = row_pieces.shape[1] // 2
    for c in range(SIDES):
        coming[c].wait()
        high, low = two_pieces(matrix[c * chunk : (c + 1) * chunk, :])
        product = halves(one_pass(high, row_pieces[...])) + one_pass(low, row_pieces[:, :cols])
        if less is not None:
            product = less[c * chunk : (c + 1) * chunk, :] - product
        fill_pieces(out_pieces, c * chunk, product)
    for side in range(SIDES):
        pick = slot_by_row(codes_row[...], side * chunk, chunk)
        write(side, halves(one_pass(pick, out_pieces[...])))


def three_pass(a, b):
    a_high, a_low = two_pieces(a)
    b_high, b_low = two_pieces(b)
    both = jnp.concatenate([b_high, b_low], axis=1)
    return halves(one_pass(a_high, both)) + one_pass(a_low, b_high)


def copies(ref, block):
    rows = block.shape[0]
    for q in range(ref.shape[0] // rows):
        ref[q * rows : (q + 1) * rows, :] = block


def modes_kernel(mode_count, codes_row, modes, inverse, load, *outs):
    total = codes_row.shape[1]
    cap = total // SIDES
    codes = codes_row[...]
    heading = codes // cap
    i, j = lax.axis_index("sub"), lax.axis_index("layer")
    even = jnp.where(heading < 2, 1 - lax.rem(i, 2), 1 - lax.rem(j, 2))
    turn = jnp.where(heading < SIDES, even * (1 - 2 * (heading % 2)), 0)
    codes = codes + turn * cap
    outs[SIDES + 3][...] = codes
    codes = jnp.broadcast_to(codes, (128, total)).astype(jnp.float32)
    codes_lanes = jnp.transpose(codes).astype(jnp.int32)
    x = jnp.concatenate(
        [modes[:, 0, :], jnp.zeros((PAD - mode_count, total), jnp.float32)], axis=0
    )
    high = x.astype(jnp.bfloat16).astype(jnp.float32)
    middle = (x - high).astype(jnp.bfloat16).astype(jnp.float32)
    low = x - high - middle
    pieces = jnp.concatenate([high, middle, low, jnp.zeros_like(low)], axis=0).astype(jnp.bfloat16)
    moved = one_pass(pieces, row_by_slot(codes_lanes, total))
    upper, lower = moved[0:PAD], moved[PAD : 2 * PAD]
    moved = upper + lower + moved[2 * PAD : 3 * PAD]
    for side in range(SIDES):
        outs[side][...] = moved[:, side * cap : (side + 1) * cap]
    coarse = inverse.shape[1]
    padded = coarse // mode_count * PAD
    old = lax.broadcasted_iota(jnp.int32, (coarse, padded), 0)
    new = lax.broadcasted_iota(jnp.int32, (coarse, padded), 1)
    spread = jnp.where((old // mode_count) * PAD + old % mode_count == new, 1.0, 0.0)
    blank = jnp.zeros((PAD - mode_count, coarse), jnp.float32)
    wide = exact(jnp.concatenate([inverse[...], blank], axis=0), spread)
    blank = jnp.zeros((PAD - mode_count, load.shape[1]), jnp.float32)
    loads = jnp.concatenate([load[...], blank], axis=0)
    copies(outs[SIDES], jnp.concatenate([wide, loads], axis=1))
    outs[SIDES + 1][...] = codes_lanes
    outs[SIDES + 2][...] = jnp.concatenate([upper, lower], axis=0)


def around(i, j):
    right, up = 1 - 2 * (i % 2), 1 - 2 * (j % 2)
    return [(i, j), (i + right, j), (i - right, j), (i, j + up), (i, j - up)]


def mode_blocks(own, partner):
    cap = own[0].shape[1]
    rows = []
    for side in range(SIDES):
        column = [own[side][...]]
        for other in range(SIDES):
            if other == side:
                column.append(-partner[side][...])
            else:
                column.append(jnp.zeros((PAD, cap), jnp.float32))
        rows.append(jnp.concatenate(column, axis=0))
    return rows


def lane_spread(mode_count, lanes):
    shape = (PAD * (SIDES + 1), lanes)
    old = lax.broadcasted_iota(jnp.int32, shape, 0)
    new = lax.broadcasted_iota(jnp.int32, shape, 1)
    spot = (old // PAD) * mode_count + old % PAD
    match = (spot == new % GROUP) & (old % PAD < mode_count)
    return jnp.where(match, 1.0, 0.0)


def operators_kernel(mode_count, flex, schur, codes_row, codes_lanes, *refs):
    own, partner = refs[0:4], refs[4:8]
    outs = refs[8:12]
    modes_out = refs[12]
    slot_pieces, row_pieces, out_pieces = refs[13:16]
    schur = fetch(schur, refs[16], refs[17])
    flex = fetch(flex, refs[18], refs[19])
    total = codes_lanes.shape[0]
    cap = total // SIDES
    half = cap // 2
    lanes = 4 * GROUP
    spread = lane_spread(mode_count, lanes)
    for side, block in enumerate(mode_blocks(own, partner)):
        placed = exact(block, spread, ((0,), (0,)))
        first = lax.broadcasted_iota(jnp.int32, placed.shape, 1) < GROUP
        modes_out[side * cap : (side + 1) * cap, :] = jnp.where(first, placed, 0.0)
        fill_pieces(slot_pieces, side * cap, placed)
    group = lax.broadcasted_iota(jnp.int32, (half, lanes), 1) // GROUP

    def write_schur(side, block):
        outs[side][...] = jnp.where(group == 0, block[:half], block[half:])

    def write_flex(side, block):
        mine = jnp.where(group == 2, block[:half], block[half:])
        outs[side][...] = jnp.where(group < 2, outs[side][...], mine)

    apply_local(schur, codes_row, codes_lanes, slot_pieces, row_pieces, out_pieces, write_schur)
    apply_rows(flex, codes_row, row_pieces, out_pieces, write_flex)


def start_kernel(mode_count, layers, flex, gap, codes_row, codes_lanes, *refs):
    slabs = refs[0:4]
    gathered, modes = refs[4:6]
    outs = refs[6:10]
    start_out, inverse_out = refs[10:12]
    slot_pieces, row_pieces, out_pieces = refs[12:15]
    flex = fetch(flex, refs[15], refs[16])
    cap = codes_lanes.shape[0] // SIDES
    wide = gathered.shape[0]
    spread = lane_spread(mode_count, GROUP)
    for n, centre in enumerate(around(lax.axis_index("sub"), lax.axis_index("layer"))):
        rows = []
        for i, j in around(*centre):
            first = jnp.clip(i * layers + j, 0, wide // PAD - 1) * PAD
            rows.append(gathered[pl.ds(pl.multiple_of(first, PAD), PAD), 0:wide])
        table = jnp.concatenate(rows, axis=0)
        inverse_out[n * GROUP : (n + 1) * GROUP, :] = exact(spread, table, ((0,), (0,)))
    coefficients = repeated(exact(inverse_out[0:GROUP, :], gathered[:, wide:]))
    start = three_pass(modes[...], coefficients)
    start_out[...] = start
    fill_pieces(slot_pieces, 0, start)

    def write(side, block):
        outs[side][0:cap, :] = block
        outs[side][cap:, :] = slabs[side][...]

    apply_local(flex, codes_row, codes_lanes, slot_pieces, row_pieces, out_pieces, write, gap)


def repeated(x):
    return jnp.concatenate([x] * 4, axis=0)


def components_of(own_pieces, block_pieces):
    both = one_pass(own_pieces[...].astype(jnp.bfloat16), block_pieces[...])
    cols = both.shape[1] // 2
    return halves(both[0:PAD]) + both[PAD:, :cols]


def grouped(slab, first):
    group = lax.broadcasted_iota(jnp.int32, slab.shape, 1) // GROUP
    upper = jnp.where(group == first, slab, 0.0)
    lower = jnp.where(group == first + 1, slab, 0.0)
    return jnp.concatenate([upper, lower], axis=0)


def lagged(side, first, mine, theirs, coefficients):
    left = jnp.concatenate([grouped(mine, first), grouped(theirs, first)], axis=1)
    near = coefficients[(side + 1) * GROUP : (side + 2) * GROUP]
    return three_pass(left, jnp.concatenate([repeated(coefficients[0:GROUP]), repeated(-near)], axis=0))


def first_kernel(schur, codes_row, codes_lanes, *refs):
    received, sent, own = refs[0:4], refs[4:8], refs[8]
    outs = refs[9:13]
    gap_out, parts_out, mine_out, theirs_out = refs[13:17]
    slot_pieces, row_pieces, out_pieces = refs[17:20]
    schur = fetch(schur, refs[20], refs[21])
    half = sent[0].shape[0] - codes_lanes.shape[0] // SIDES
    cap = codes_lanes.shape[0] // SIDES
    for side in range(SIDES):
        block = sent[side][0:cap, :] - received[side][0:cap, :]
        gap_out[side * cap : (side + 1) * cap, :] = block
        fill_pieces(slot_pieces, side * cap, block)
        mine_out[side * half : (side + 1) * half, :] = sent[side][cap:, :]
        theirs_out[side * half : (side + 1) * half, :] = received[side][cap:, :]
    copies(parts_out, components_of(own, slot_pieces))

    def write(side, block):
        outs[side][...] = block

    apply_local(schur, codes_row, codes_lanes, slot_pieces, row_pieces, out_pieces, write)


def stage_kernel(stage, matrix, codes_row, codes_lanes, *refs):
    refs = list(refs)

    def take(count):
        taken = refs[:count]
        del refs[:count]
        return taken

    received, sent = take(4), take(4)
    mine, theirs, own, gathered, inverse_rows = take(5)
    (state_in,) = take(1) if stage > 2 else [None]
    outs = take(4) if stage < 5 else []
    state_out, parts_out = take(2)
    slot_pieces, row_pieces, out_pieces = take(3)
    if stage < 5:
        matrix = fetch(matrix, *take(2))
    total = codes_lanes.shape[0]
    cap = total // SIDES
    half = mine.shape[0] // SIDES
    coefficients = exact(inverse_rows[...], gathered[...])
    for side in range(SIDES):
        rows = slice(side * cap, (side + 1) * cap)
        slab = slice(side * half, (side + 1) * half)
        jump = sent[side][...] - received[side][...]
        first = 0 if stage in (2, 4) else 2
        behind = lagged(side, first, mine[slab, :], theirs[slab, :], coefficients)
        if stage == 2:
            block = 0.5 * (jump - behind)
            state = block
        elif stage == 3:
            block = (jump - behind) / theta_mid
            state = state_in[rows, :] - block
        elif stage == 4:
            block = 0.5 * (jump + behind)
            state = keep_step * state_in[rows, :] + new_step * block
        else:
            block = jump - new_step * behind
            state = state_in[rows, :] - block
        state_out[rows, :] = state
        if stage < 5:
            fill_pieces(slot_pieces, side * cap, state)
        fill_pieces(out_pieces, side * cap, block)
    copies(parts_out, components_of(own, out_pieces))
    if stage < 5:

        def write(side, block):
            outs[side][...] = block

        apply_local(matrix, codes_row, codes_lanes, slot_pieces, row_pieces, out_pieces, write)


def direct_of(modes, gathered, inverse_rows):
    coefficients = exact(inverse_rows[0:GROUP, :], gathered[...])
    return three_pass(modes[...], repeated(coefficients))


def update_kernel(stage, state, modes, gathered, inverse_rows, after, out):
    direct = direct_of(modes, gathered, inverse_rows)
    if stage == 2:
        out[...] = state[...] - direct
    elif stage == 3:
        out[...] = (state[...] - direct) / theta_mid
    else:
        out[...] = state[...] + direct


def rows_kernel(codes_lanes, residual, raw_step, start, step, modes, gathered, inverse_rows, *refs):
    targets, pieces = refs[0:3], refs[3]
    total, cols = residual.shape
    cap = total // SIDES
    direct = direct_of(modes, gathered, inverse_rows)
    multipliers = raw_step[...] - new_step * direct + start[...] + step[...]
    for n, source in enumerate((residual[...], multipliers, modes[...])):
        high, low = two_pieces(source)
        pieces[:, 2 * n * cols : (2 * n + 1) * cols] = high
        pieces[:, (2 * n + 1) * cols : (2 * n + 2) * cols] = low

    def keep(begin, rows):
        for n, target in enumerate(targets):
            target[begin : begin + cap, :] = halves(rows[:, 2 * n * cols : (2 * n + 2) * cols])

    to_rows(codes_lanes, pieces, keep)


def last_kernel(residual, modes, gathered, inverse_rows, out):
    coefficients = repeated(exact(inverse_rows[0:GROUP, :], gathered[...]))
    out[...] = residual[...] + three_pass(modes[...], coefficients)


def call(kernel, name, outs, inputs, scratch=(), smem=(), left=(), flops=None, room=58):
    spaces = [pltpu.VMEM] * len(inputs)
    for n in smem:
        spaces[n] = pltpu.SMEM
    for n in left:
        spaces[n] = pl.ANY
    shapes = []
    for shape in outs:
        shapes.append(jax.ShapeDtypeStruct(shape, jnp.float32) if isinstance(shape, tuple) else shape)
    return pl.pallas_call(
        kernel,
        name=name,
        out_shape=shapes,
        in_specs=[pl.BlockSpec(memory_space=space) for space in spaces],
        out_specs=[pl.BlockSpec(memory_space=pltpu.VMEM)] * len(outs),
        scratch_shapes=list(scratch),
        cost_estimate=None
        if flops is None
        else pl.CostEstimate(flops=flops, bytes_accessed=16 * inputs[0].size, transcendentals=0),
        compiler_params=pltpu.CompilerParams(vmem_limit_bytes=room * 1024 * 1024),
    )(*inputs)


def exchange(blocks):
    received = []
    for side, block in enumerate(blocks):
        axis = "sub" if side < 2 else "layer"
        pairs = []
        for i in range(side % 2, lax.axis_size(axis) - 1, 2):
            pairs += [(i, i + 1), (i + 1, i)]
        received.append(lax.ppermute(block, axis, pairs))
    return received


def everywhere(stacked):
    return lax.all_to_all(stacked, ("sub", "layer"), split_axis=0, concat_axis=0, tiled=True)


def per_device(
    local_gap, route_codes, flexibility, dirichlet, rigid_modes, coarse_inverse, rigid_load
):
    gap = local_gap[0, 0]
    flex = flexibility[0, 0]
    schur = dirichlet[0, 0]
    mode_count, total = rigid_modes.shape[2:]
    modes = rigid_modes.reshape(mode_count, 1, total)
    cap = total // SIDES
    cols = gap.shape[1]
    layers = lax.axis_size("layer")
    wide = lax.axis_size("sub") * layers * PAD
    pieces = pltpu.VMEM((total, 2 * cols), jnp.bfloat16)
    scratch = [pieces] * 3
    block = [(cap, cols)] * SIDES
    whole = (total, cols)
    parts = (wide, cols)
    brought = [pltpu.VMEM((total, total), jnp.float32), pltpu.SemaphoreType.DMA((SIDES,))]

    shown = call(
        functools.partial(modes_kernel, mode_count),
        "modes_to_slots",
        [(PAD, cap)] * SIDES
        + [(wide, wide + cols), jax.ShapeDtypeStruct((total, 128), jnp.int32), (2 * PAD, total)]
        + [jax.ShapeDtypeStruct((1, total), jnp.int32)],
        [route_codes[0], modes, coarse_inverse, rigid_load],
    )
    own, (inverse_load, codes_lanes, own_pieces, codes_row) = shown[:4], shown[4:]
    gathered = everywhere(inverse_load)
    partner = exchange(own)
    shown = call(
        functools.partial(operators_kernel, mode_count),
        "operators_on_modes",
        [(cap // 2, 4 * GROUP)] * SIDES + [(total, 4 * GROUP)],
        [flex, schur, codes_row, codes_lanes, *own, *partner],
        scratch + brought * 2,
        left=(0, 1),
    )
    slabs, slot_modes = shown[:4], shown[4]
    shown = call(
        functools.partial(start_kernel, mode_count, layers),
        "start",
        [(cap + cap // 2, cols)] * SIDES + [whole, (5 * GROUP, wide)],
        [flex, gap, codes_row, codes_lanes, *slabs, gathered, slot_modes],
        scratch + brought,
        left=(0,),
    )
    sent, (start, inverse_rows) = shown[:4], shown[4:]
    received = exchange(sent)
    shown = call(
        first_kernel,
        "stage_1",
        block + [whole, parts] + [(2 * cap, 4 * GROUP)] * 2,
        [schur, codes_row, codes_lanes, *received, *sent, own_pieces],
        scratch + brought,
        left=(0,),
    )
    sent, (gap_jump, components, mine, theirs) = shown[:4], shown[4:]

    def stage(number, matrix, states_in, sent, components):
        gathered = everywhere(components)
        received = exchange(sent)
        inputs = [codes_row, codes_lanes, *received, *sent, mine, theirs]
        inputs += [own_pieces, gathered, inverse_rows, *states_in]
        outs = [whole, parts]
        kernel = functools.partial(stage_kernel, number)
        name = "stage_%d" % number
        if matrix is None:
            shown = call(functools.partial(kernel, None), name, outs, inputs, scratch)
        else:
            inputs = [matrix] + inputs
            shown = call(kernel, name, block + outs, inputs, scratch + brought, left=(0,))
        return gathered, shown[:-2], *shown[-2:]

    def update(number, state, gathered, after):
        (out,) = call(
            functools.partial(update_kernel, number),
            "update_%d" % number,
            [whole],
            [state, slot_modes, gathered, inverse_rows, after],
            left=(4,),
            flops=8 * total * cols * cols,
        )
        return out

    gathered, sent, precond, components = stage(2, flex, [], sent, components)
    residual = update(2, gap_jump, gathered, components)
    gathered, sent, residual, components = stage(3, schur, [residual], sent, components)
    step = update(3, precond, gathered, components)
    gathered, sent, raw_step, components = stage(4, flex, [step], sent, components)
    residual = update(4, residual, gathered, components)
    gathered, _, residual, components = stage(5, None, [residual], sent, components)
    last_gathered = everywhere(components)
    residual, multipliers, row_modes = call(
        rows_kernel,
        "slots_to_rows",
        [whole, whole, (total, 4 * GROUP)],
        [codes_lanes, residual, raw_step, start, step, slot_modes, gathered, inverse_rows],
        [pltpu.VMEM((total, 6 * cols), jnp.bfloat16)],
    )
    gathered = last_gathered
    (residual,) = call(
        last_kernel,
        "residual",
        [whole],
        [residual, row_modes, gathered, inverse_rows],
        room=12,
    )
    return (multipliers[None, None], residual[None, None])


def solution(mesh):
    placed = (
        P("sub", "layer", None, None),
        P("sub", "layer", None),
        P("sub", "layer", None, None),
        P("sub", "layer", None, None),
        P("sub", "layer", None, None),
        P(("sub", "layer"), None),
        P(("sub", "layer"), None),
    )
    return jax.shard_map(
        per_device,
        mesh=mesh,
        in_specs=placed,
        out_specs=(P("sub", "layer", None, None), P("sub", "layer", None, None)),
        check_vma=False,
    )
```

```python
import functools

import jax
import jax.numpy as jnp
from jax import lax
from jax.experimental import pallas as pl
from jax.experimental.pallas import tpu as pltpu
from jax.sharding import PartitionSpec as P

theta_mid = 4.25
delta_half = 3.75
sigma_ratio = theta_mid / delta_half
damping = delta_half / theta_mid
damping_next = 1.0 / (2.0 * sigma_ratio - damping)
keep_step = damping_next * damping
new_step = 2.0 * damping_next / delta_half

GROUP = 32
PAD = 8
SIDES = 4


def exact(a, b, contract=((1,), (0,))):
    return lax.dot_general(
        a,
        b,
        (contract, ((), ())),
        precision=lax.Precision.HIGHEST,
        preferred_element_type=jnp.float32,
    )


def one_pass(a, b):
    return jnp.dot(a, b, preferred_element_type=jnp.float32)


def two_pieces(x):
    high = x.astype(jnp.bfloat16)
    low = (x - high.astype(jnp.float32)).astype(jnp.bfloat16)
    return high, low


def slot_by_row(codes_row, start, rows):
    slots = lax.broadcasted_iota(jnp.int32, (rows, codes_row.shape[1]), 0) + start
    return jnp.where(slots == codes_row, 1.0, 0.0).astype(jnp.bfloat16)


def row_by_slot(codes_lanes, slots):
    rows, lanes = codes_lanes.shape
    lane = lax.broadcasted_iota(jnp.int32, (rows, lanes), 1)
    parts = [
        jnp.where(lane + first == codes_lanes, 1.0, 0.0).astype(jnp.bfloat16)
        for first in range(0, slots, lanes)
    ]
    return jnp.concatenate(parts, axis=1)


def fill_pieces(pieces, start, x):
    high, low = two_pieces(x)
    cols = x.shape[1]
    pieces[pl.ds(start, x.shape[0]), 0:cols] = high
    pieces[pl.ds(start, x.shape[0]), cols : 2 * cols] = low


def to_rows(codes_lanes, slot_pieces, write):
    total = slot_pieces.shape[0]
    chunk = total // SIDES
    for c in range(SIDES):
        pick = row_by_slot(codes_lanes[c * chunk : (c + 1) * chunk, :], total)
        write(c * chunk, one_pass(pick, slot_pieces[...]))


def halves(x):
    cols = x.shape[1] // 2
    return x[:, :cols] + x[:, cols:]


def fetch(matrix, held, arrived):
    chunk = held.shape[0] // SIDES
    pieces = []
    for c in range(SIDES):
        rows = pl.ds(c * chunk, chunk)
        pieces.append(pltpu.make_async_copy(matrix.at[rows], held.at[rows], arrived.at[c]))
        pieces[c].start()
    return pieces, held


def apply_local(fetched, codes_row, codes_lanes, slot_pieces, row_pieces, out_pieces, write, less=None):
    total = slot_pieces.shape[0]
    chunk = total // SIDES

    def keep(start, rows):
        row_pieces[start : start + chunk, :] = rows.astype(jnp.bfloat16)

    to_rows(codes_lanes, slot_pieces, keep)
    apply_rows(fetched, codes_row, row_pieces, out_pieces, write, less)


def apply_rows(fetched, codes_row, row_pieces, out_pieces, write, less=None):
    coming, matrix = fetched
    total = row_pieces.shape[0]
    chunk = total // SIDES
    cols = row_pieces.shape[1] // 2
    for c in range(SIDES):
        coming[c].wait()
        high, low = two_pieces(matrix[c * chunk : (c + 1) * chunk, :])
        product = halves(one_pass(high, row_pieces[...])) + one_pass(low, row_pieces[:, :cols])
        if less is not None:
            product = less[c * chunk : (c + 1) * chunk, :] - product
        fill_pieces(out_pieces, c * chunk, product)
    for side in range(SIDES):
        pick = slot_by_row(codes_row[...], side * chunk, chunk)
        write(side, halves(one_pass(pick, out_pieces[...])))


def three_pass(a, b):
    a_high, a_low = two_pieces(a)
    b_high, b_low = two_pieces(b)
    both = jnp.concatenate([b_high, b_low], axis=1)
    return halves(one_pass(a_high, both)) + one_pass(a_low, b_high)


def copies(ref, block):
    rows = block.shape[0]
    for q in range(ref.shape[0] // rows):
        ref[q * rows : (q + 1) * rows, :] = block


def modes_kernel(mode_count, codes_row, modes, inverse, load, *outs):
    total = codes_row.shape[1]
    cap = total // SIDES
    codes = codes_row[...]
    heading = codes // cap
    i, j = lax.axis_index("sub"), lax.axis_index("layer")
    even = jnp.where(heading < 2, 1 - lax.rem(i, 2), 1 - lax.rem(j, 2))
    turn = jnp.where(heading < SIDES, even * (1 - 2 * (heading % 2)), 0)
    codes = codes + turn * cap
    outs[SIDES + 3][...] = codes
    codes = jnp.broadcast_to(codes, (128, total)).astype(jnp.float32)
    codes_lanes = jnp.transpose(codes).astype(jnp.int32)
    x = jnp.concatenate(
        [modes[:, 0, :], jnp.zeros((PAD - mode_count, total), jnp.float32)], axis=0
    )
    high = x.astype(jnp.bfloat16).astype(jnp.float32)
    middle = (x - high).astype(jnp.bfloat16).astype(jnp.float32)
    low = x - high - middle
    pieces = jnp.concatenate([high, middle, low, jnp.zeros_like(low)], axis=0).astype(jnp.bfloat16)
    moved = one_pass(pieces, row_by_slot(codes_lanes, total))
    upper, lower = moved[0:PAD], moved[PAD : 2 * PAD]
    moved = upper + lower + moved[2 * PAD : 3 * PAD]
    for side in range(SIDES):
        outs[side][...] = moved[:, side * cap : (side + 1) * cap]
    coarse = inverse.shape[1]
    padded = coarse // mode_count * PAD
    old = lax.broadcasted_iota(jnp.int32, (coarse, padded), 0)
    new = lax.broadcasted_iota(jnp.int32, (coarse, padded), 1)
    spread = jnp.where((old // mode_count) * PAD + old % mode_count == new, 1.0, 0.0)
    blank = jnp.zeros((PAD - mode_count, coarse), jnp.float32)
    wide = exact(jnp.concatenate([inverse[...], blank], axis=0), spread)
    blank = jnp.zeros((PAD - mode_count, load.shape[1]), jnp.float32)
    loads = jnp.concatenate([load[...], blank], axis=0)
    copies(outs[SIDES], jnp.concatenate([wide, loads], axis=1))
    outs[SIDES + 1][...] = codes_lanes
    outs[SIDES + 2][...] = jnp.concatenate([upper, lower], axis=0)


def around(i, j):
    right, up = 1 - 2 * (i % 2), 1 - 2 * (j % 2)
    return [(i, j), (i + right, j), (i - right, j), (i, j + up), (i, j - up)]


def mode_blocks(own, partner):
    cap = own[0].shape[1]
    rows = []
    for side in range(SIDES):
        column = [own[side][...]]
        for other in range(SIDES):
            if other == side:
                column.append(-partner[side][...])
            else:
                column.append(jnp.zeros((PAD, cap), jnp.float32))
        rows.append(jnp.concatenate(column, axis=0))
    return rows


def lane_spread(mode_count, lanes):
    shape = (PAD * (SIDES + 1), lanes)
    old = lax.broadcasted_iota(jnp.int32, shape, 0)
    new = lax.broadcasted_iota(jnp.int32, shape, 1)
    spot = (old // PAD) * mode_count + old % PAD
    match = (spot == new % GROUP) & (old % PAD < mode_count)
    return jnp.where(match, 1.0, 0.0)


def operators_kernel(mode_count, flex, schur, codes_row, codes_lanes, *refs):
    own, partner = refs[0:4], refs[4:8]
    outs = refs[8:12]
    modes_out = refs[12]
    slot_pieces, row_pieces, out_pieces = refs[13:16]
    schur = fetch(schur, refs[16], refs[17])
    flex = fetch(flex, refs[18], refs[19])
    total = codes_lanes.shape[0]
    cap = total // SIDES
    half = cap // 2
    lanes = 4 * GROUP
    spread = lane_spread(mode_count, lanes)
    for side, block in enumerate(mode_blocks(own, partner)):
        placed = exact(block, spread, ((0,), (0,)))
        first = lax.broadcasted_iota(jnp.int32, placed.shape, 1) < GROUP
        modes_out[side * cap : (side + 1) * cap, :] = jnp.where(first, placed, 0.0)
        fill_pieces(slot_pieces, side * cap, placed)
    group = lax.broadcasted_iota(jnp.int32, (half, lanes), 1) // GROUP

    def write_schur(side, block):
        outs[side][...] = jnp.where(group == 0, block[:half], block[half:])

    def write_flex(side, block):
        mine = jnp.where(group == 2, block[:half], block[half:])
        outs[side][...] = jnp.where(group < 2, outs[side][...], mine)

    apply_local(schur, codes_row, codes_lanes, slot_pieces, row_pieces, out_pieces, write_schur)
    apply_rows(flex, codes_row, row_pieces, out_pieces, write_flex)


def start_kernel(mode_count, layers, flex, gap, codes_row, codes_lanes, *refs):
    slabs = refs[0:4]
    gathered, modes = refs[4:6]
    outs = refs[6:10]
    start_out, inverse_out = refs[10:12]
    slot_pieces, row_pieces, out_pieces = refs[12:15]
    flex = fetch(flex, refs[15], refs[16])
    cap = codes_lanes.shape[0] // SIDES
    wide = gathered.shape[0]
    spread = lane_spread(mode_count, GROUP)
    for n, centre in enumerate(around(lax.axis_index("sub"), lax.axis_index("layer"))):
        rows = []
        for i, j in around(*centre):
            first = jnp.clip(i * layers + j, 0, wide // PAD - 1) * PAD
            rows.append(gathered[pl.ds(pl.multiple_of(first, PAD), PAD), 0:wide])
        table = jnp.concatenate(rows, axis=0)
        inverse_out[n * GROUP : (n + 1) * GROUP, :] = exact(spread, table, ((0,), (0,)))
    coefficients = repeated(exact(inverse_out[0:GROUP, :], gathered[:, wide:]))
    start = three_pass(modes[...], coefficients)
    start_out[...] = start
    fill_pieces(slot_pieces, 0, start)

    def write(side, block):
        outs[side][0:cap, :] = block
        outs[side][cap:, :] = slabs[side][...]

    apply_local(flex, codes_row, codes_lanes, slot_pieces, row_pieces, out_pieces, write, gap)


def repeated(x):
    return jnp.concatenate([x] * 4, axis=0)


def components_of(own_pieces, block_pieces):
    both = one_pass(own_pieces[...].astype(jnp.bfloat16), block_pieces[...])
    cols = both.shape[1] // 2
    return halves(both[0:PAD]) + both[PAD:, :cols]


def grouped(slab, first):
    group = lax.broadcasted_iota(jnp.int32, slab.shape, 1) // GROUP
    upper = jnp.where(group == first, slab, 0.0)
    lower = jnp.where(group == first + 1, slab, 0.0)
    return jnp.concatenate([upper, lower], axis=0)


def lagged(side, first, mine, theirs, coefficients):
    left = jnp.concatenate([grouped(mine, first), grouped(theirs, first)], axis=1)
    near = coefficients[(side + 1) * GROUP : (side + 2) * GROUP]
    return three_pass(left, jnp.concatenate([repeated(coefficients[0:GROUP]), repeated(-near)], axis=0))


def first_kernel(schur, codes_row, codes_lanes, *refs):
    received, sent, own = refs[0:4], refs[4:8], refs[8]
    outs = refs[9:13]
    gap_out, parts_out, mine_out, theirs_out = refs[13:17]
    slot_pieces, row_pieces, out_pieces = refs[17:20]
    schur = fetch(schur, refs[20], refs[21])
    half = sent[0].shape[0] - codes_lanes.shape[0] // SIDES
    cap = codes_lanes.shape[0] // SIDES
    for side in range(SIDES):
        block = sent[side][0:cap, :] - received[side][0:cap, :]
        gap_out[side * cap : (side + 1) * cap, :] = block
        fill_pieces(slot_pieces, side * cap, block)
        mine_out[side * half : (side + 1) * half, :] = sent[side][cap:, :]
        theirs_out[side * half : (side + 1) * half, :] = received[side][cap:, :]
    copies(parts_out, components_of(own, slot_pieces))

    def write(side, block):
        outs[side][...] = block

    apply_local(schur, codes_row, codes_lanes, slot_pieces, row_pieces, out_pieces, write)


def stage_kernel(stage, matrix, codes_row, codes_lanes, *refs):
    refs = list(refs)

    def take(count):
        taken = refs[:count]
        del refs[:count]
        return taken

    received, sent = take(4), take(4)
    mine, theirs, own, gathered, inverse_rows = take(5)
    (state_in,) = take(1) if stage > 2 else [None]
    outs = take(4) if stage < 5 else []
    state_out, parts_out = take(2)
    slot_pieces, row_pieces, out_pieces = take(3)
    if stage < 5:
        matrix = fetch(matrix, *take(2))
    total = codes_lanes.shape[0]
    cap = total // SIDES
    half = mine.shape[0] // SIDES
    coefficients = exact(inverse_rows[...], gathered[...])
    for side in range(SIDES):
        rows = slice(side * cap, (side + 1) * cap)
        slab = slice(side * half, (side + 1) * half)
        jump = sent[side][...] - received[side][...]
        first = 0 if stage in (2, 4) else 2
        behind = lagged(side, first, mine[slab, :], theirs[slab, :], coefficients)
        if stage == 2:
            block = 0.5 * (jump - behind)
            state = block
        elif stage == 3:
            block = (jump - behind) / theta_mid
            state = state_in[rows, :] - block
        elif stage == 4:
            block = 0.5 * (jump + behind)
            state = keep_step * state_in[rows, :] + new_step * block
        else:
            block = jump - new_step * behind
            state = state_in[rows, :] - block
        state_out[rows, :] = state
        if stage < 5:
            fill_pieces(slot_pieces, side * cap, state)
        fill_pieces(out_pieces, side * cap, block)
    copies(parts_out, components_of(own, out_pieces))
    if stage < 5:

        def write(side, block):
            outs[side][...] = block

        apply_local(matrix, codes_row, codes_lanes, slot_pieces, row_pieces, out_pieces, write)


def direct_of(modes, gathered, inverse_rows):
    coefficients = exact(inverse_rows[0:GROUP, :], gathered[...])
    return three_pass(modes[...], repeated(coefficients))


def update_kernel(stage, state, modes, gathered, inverse_rows, after, out):
    direct = direct_of(modes, gathered, inverse_rows)
    if stage == 2:
        out[...] = state[...] - direct
    elif stage == 3:
        out[...] = (state[...] - direct) / theta_mid
    else:
        out[...] = state[...] + direct


def rows_kernel(codes_lanes, residual, raw_step, start, step, modes, gathered, inverse_rows, *refs):
    targets, pieces = refs[0:3], refs[3]
    total, cols = residual.shape
    cap = total // SIDES
    direct = direct_of(modes, gathered, inverse_rows)
    multipliers = raw_step[...] - new_step * direct + start[...] + step[...]
    for n, source in enumerate((residual[...], multipliers, modes[...])):
        high, low = two_pieces(source)
        pieces[:, 2 * n * cols : (2 * n + 1) * cols] = high
        pieces[:, (2 * n + 1) * cols : (2 * n + 2) * cols] = low

    def chunk(c, carry):
        here = pl.ds(pl.multiple_of(c * cap, 16), cap)
        rows = one_pass(row_by_slot(codes_lanes[here, :], total), pieces[...])
        for n, target in enumerate(targets):
            target[here, :] = halves(rows[:, 2 * n * cols : (2 * n + 2) * cols])
        return carry

    lax.fori_loop(0, SIDES, chunk, 0)


def last_kernel(residual, modes, gathered, inverse_rows, out):
    coefficients = repeated(exact(inverse_rows[0:GROUP, :], gathered[...]))
    out[...] = residual[...] + three_pass(modes[...], coefficients)


def call(kernel, name, outs, inputs, scratch=(), smem=(), left=(), flops=None, room=58):
    spaces = [pltpu.VMEM] * len(inputs)
    for n in smem:
        spaces[n] = pltpu.SMEM
    for n in left:
        spaces[n] = pl.ANY
    shapes = []
    for shape in outs:
        shapes.append(jax.ShapeDtypeStruct(shape, jnp.float32) if isinstance(shape, tuple) else shape)
    return pl.pallas_call(
        kernel,
        name=name,
        out_shape=shapes,
        in_specs=[pl.BlockSpec(memory_space=space) for space in spaces],
        out_specs=[pl.BlockSpec(memory_space=pltpu.VMEM)] * len(outs),
        scratch_shapes=list(scratch),
        cost_estimate=None
        if flops is None
        else pl.CostEstimate(flops=flops, bytes_accessed=16 * inputs[0].size, transcendentals=0),
        compiler_params=pltpu.CompilerParams(vmem_limit_bytes=room * 1024 * 1024),
    )(*inputs)


def exchange(blocks):
    received = []
    for side, block in enumerate(blocks):
        axis = "sub" if side < 2 else "layer"
        pairs = []
        for i in range(side % 2, lax.axis_size(axis) - 1, 2):
            pairs += [(i, i + 1), (i + 1, i)]
        received.append(lax.ppermute(block, axis, pairs))
    return received


def everywhere(stacked):
    return lax.all_to_all(stacked, ("sub", "layer"), split_axis=0, concat_axis=0, tiled=True)


def per_device(
    local_gap, route_codes, flexibility, dirichlet, rigid_modes, coarse_inverse, rigid_load
):
    gap = local_gap[0, 0]
    flex = flexibility[0, 0]
    schur = dirichlet[0, 0]
    mode_count, total = rigid_modes.shape[2:]
    modes = rigid_modes.reshape(mode_count, 1, total)
    cap = total // SIDES
    cols = gap.shape[1]
    layers = lax.axis_size("layer")
    wide = lax.axis_size("sub") * layers * PAD
    pieces = pltpu.VMEM((total, 2 * cols), jnp.bfloat16)
    scratch = [pieces] * 3
    block = [(cap, cols)] * SIDES
    whole = (total, cols)
    parts = (wide, cols)
    brought = [pltpu.VMEM((total, total), jnp.float32), pltpu.SemaphoreType.DMA((SIDES,))]

    shown = call(
        functools.partial(modes_kernel, mode_count),
        "modes_to_slots",
        [(PAD, cap)] * SIDES
        + [(wide, wide + cols), jax.ShapeDtypeStruct((total, 128), jnp.int32), (2 * PAD, total)]
        + [jax.ShapeDtypeStruct((1, total), jnp.int32)],
        [route_codes[0], modes, coarse_inverse, rigid_load],
    )
    own, (inverse_load, codes_lanes, own_pieces, codes_row) = shown[:4], shown[4:]
    gathered = everywhere(inverse_load)
    partner = exchange(own)
    shown = call(
        functools.partial(operators_kernel, mode_count),
        "operators_on_modes",
        [(cap // 2, 4 * GROUP)] * SIDES + [(total, 4 * GROUP)],
        [flex, schur, codes_row, codes_lanes, *own, *partner],
        scratch + brought * 2,
        left=(0, 1),
    )
    slabs, slot_modes = shown[:4], shown[4]
    shown = call(
        functools.partial(start_kernel, mode_count, layers),
        "start",
        [(cap + cap // 2, cols)] * SIDES + [whole, (5 * GROUP, wide)],
        [flex, gap, codes_row, codes_lanes, *slabs, gathered, slot_modes],
        scratch + brought,
        left=(0,),
    )
    sent, (start, inverse_rows) = shown[:4], shown[4:]
    received = exchange(sent)
    shown = call(
        first_kernel,
        "stage_1",
        block + [whole, parts] + [(2 * cap, 4 * GROUP)] * 2,
        [schur, codes_row, codes_lanes, *received, *sent, own_pieces],
        scratch + brought,
        left=(0,),
    )
    sent, (gap_jump, components, mine, theirs) = shown[:4], shown[4:]

    def stage(number, matrix, states_in, sent, components):
        gathered = everywhere(components)
        received = exchange(sent)
        inputs = [codes_row, codes_lanes, *received, *sent, mine, theirs]
        inputs += [own_pieces, gathered, inverse_rows, *states_in]
        outs = [whole, parts]
        kernel = functools.partial(stage_kernel, number)
        name = "stage_%d" % number
        if matrix is None:
            shown = call(functools.partial(kernel, None), name, outs, inputs, scratch)
        else:
            inputs = [matrix] + inputs
            shown = call(kernel, name, block + outs, inputs, scratch + brought, left=(0,))
        return gathered, shown[:-2], *shown[-2:]

    def update(number, state, gathered, after):
        (out,) = call(
            functools.partial(update_kernel, number),
            "update_%d" % number,
            [whole],
            [state, slot_modes, gathered, inverse_rows, after],
            left=(4,),
            flops=8 * total * cols * cols,
        )
        return out

    gathered, sent, precond, components = stage(2, flex, [], sent, components)
    residual = update(2, gap_jump, gathered, components)
    gathered, sent, residual, components = stage(3, schur, [residual], sent, components)
    step = update(3, precond, gathered, components)
    gathered, sent, raw_step, components = stage(4, flex, [step], sent, components)
    residual = update(4, residual, gathered, components)
    gathered, _, residual, components = stage(5, None, [residual], sent, components)
    last_gathered = everywhere(components)
    residual, multipliers, row_modes = call(
        rows_kernel,
        "slots_to_rows",
        [whole, whole, (total, 4 * GROUP)],
        [codes_lanes, residual, raw_step, start, step, slot_modes, gathered, inverse_rows],
        [pltpu.VMEM((total, 6 * cols), jnp.bfloat16)],
    )
    gathered = last_gathered
    (residual,) = call(
        last_kernel,
        "residual",
        [whole],
        [residual, row_modes, gathered, inverse_rows],
        room=12,
    )
    return (multipliers[None, None], residual[None, None])


def solution(mesh):
    placed = (
        P("sub", "layer", None, None),
        P("sub", "layer", None),
        P("sub", "layer", None, None),
        P("sub", "layer", None, None),
        P("sub", "layer", None, None),
        P(("sub", "layer"), None),
        P(("sub", "layer"), None),
    )
    return jax.shard_map(
        per_device,
        mesh=mesh,
        in_specs=placed,
        out_specs=(P("sub", "layer", None, None), P("sub", "layer", None, None)),
        check_vma=False,
    )
```

```python
import functools

import jax
import jax.numpy as jnp
from jax import lax
from jax.experimental import pallas as pl
from jax.experimental.pallas import tpu as pltpu
from jax.sharding import PartitionSpec as P

theta_mid = 4.25
delta_half = 3.75
sigma_ratio = theta_mid / delta_half
damping = delta_half / theta_mid
damping_next = 1.0 / (2.0 * sigma_ratio - damping)
keep_step = damping_next * damping
new_step = 2.0 * damping_next / delta_half

GROUP = 32
PAD = 8
SIDES = 4


def exact(a, b, contract=((1,), (0,))):
    return lax.dot_general(
        a,
        b,
        (contract, ((), ())),
        precision=lax.Precision.HIGHEST,
        preferred_element_type=jnp.float32,
    )


def one_pass(a, b):
    return jnp.dot(a, b, preferred_element_type=jnp.float32)


def two_pieces(x):
    high = x.astype(jnp.bfloat16)
    low = (x - high.astype(jnp.float32)).astype(jnp.bfloat16)
    return high, low


def slot_by_row(codes_row, start, rows):
    slots = lax.broadcasted_iota(jnp.int32, (rows, codes_row.shape[1]), 0) + start
    return jnp.where(slots == codes_row, 1.0, 0.0).astype(jnp.bfloat16)


def row_by_slot(codes_lanes, slots):
    rows, lanes = codes_lanes.shape
    lane = lax.broadcasted_iota(jnp.int32, (rows, lanes), 1)
    parts = [
        jnp.where(lane + first == codes_lanes, 1.0, 0.0).astype(jnp.bfloat16)
        for first in range(0, slots, lanes)
    ]
    return jnp.concatenate(parts, axis=1)


def fill_pieces(pieces, start, x):
    high, low = two_pieces(x)
    cols = x.shape[1]
    pieces[pl.ds(start, x.shape[0]), 0:cols] = high
    pieces[pl.ds(start, x.shape[0]), cols : 2 * cols] = low


def to_rows(codes_lanes, slot_pieces, write):
    total = slot_pieces.shape[0]
    chunk = total // SIDES
    for c in range(SIDES):
        pick = row_by_slot(codes_lanes[c * chunk : (c + 1) * chunk, :], total)
        write(c * chunk, one_pass(pick, slot_pieces[...]))


def halves(x):
    cols = x.shape[1] // 2
    return x[:, :cols] + x[:, cols:]


def fetch(matrix, held, arrived):
    chunk = held.shape[0] // SIDES
    pieces = []
    for c in range(SIDES):
        rows = pl.ds(c * chunk, chunk)
        pieces.append(pltpu.make_async_copy(matrix.at[rows], held.at[rows], arrived.at[c]))
        pieces[c].start()
    return pieces, held


def apply_local(fetched, codes_row, codes_lanes, slot_pieces, row_pieces, out_pieces, write, less=None):
    total = slot_pieces.shape[0]
    chunk = total // SIDES

    def keep(start, rows):
        row_pieces[start : start + chunk, :] = rows.astype(jnp.bfloat16)

    to_rows(codes_lanes, slot_pieces, keep)
    apply_rows(fetched, codes_row, row_pieces, out_pieces, write, less)


def apply_rows(fetched, codes_row, row_pieces, out_pieces, write, less=None):
    coming, matrix = fetched
    total = row_pieces.shape[0]
    chunk = total // SIDES
    cols = row_pieces.shape[1] // 2
    for c in range(SIDES):
        coming[c].wait()
        high, low = two_pieces(matrix[c * chunk : (c + 1) * chunk, :])
        product = halves(one_pass(high, row_pieces[...])) + one_pass(low, row_pieces[:, :cols])
        if less is not None:
            product = less[c * chunk : (c + 1) * chunk, :] - product
        fill_pieces(out_pieces, c * chunk, product)
    for side in range(SIDES):
        pick = slot_by_row(codes_row[...], side * chunk, chunk)
        write(side, halves(one_pass(pick, out_pieces[...])))


def three_pass(a, b):
    a_high, a_low = two_pieces(a)
    b_high, b_low = two_pieces(b)
    both = jnp.concatenate([b_high, b_low], axis=1)
    return halves(one_pass(a_high, both)) + one_pass(a_low, b_high)


def copies(ref, block):
    rows = block.shape[0]
    for q in range(ref.shape[0] // rows):
        ref[q * rows : (q + 1) * rows, :] = block


def modes_kernel(mode_count, codes_row, modes, inverse, load, *outs):
    total = codes_row.shape[1]
    cap = total // SIDES
    codes = codes_row[...]
    heading = codes // cap
    i, j = lax.axis_index("sub"), lax.axis_index("layer")
    even = jnp.where(heading < 2, 1 - lax.rem(i, 2), 1 - lax.rem(j, 2))
    turn = jnp.where(heading < SIDES, even * (1 - 2 * (heading % 2)), 0)
    codes = codes + turn * cap
    outs[SIDES + 3][...] = codes
    codes = jnp.broadcast_to(codes, (128, total)).astype(jnp.float32)
    codes_lanes = jnp.transpose(codes).astype(jnp.int32)
    x = jnp.concatenate(
        [modes[:, 0, :], jnp.zeros((PAD - mode_count, total), jnp.float32)], axis=0
    )
    high = x.astype(jnp.bfloat16).astype(jnp.float32)
    middle = (x - high).astype(jnp.bfloat16).astype(jnp.float32)
    low = x - high - middle
    pieces = jnp.concatenate([high, middle, low, jnp.zeros_like(low)], axis=0).astype(jnp.bfloat16)
    moved = one_pass(pieces, row_by_slot(codes_lanes, total))
    upper, lower = moved[0:PAD], moved[PAD : 2 * PAD]
    moved = upper + lower + moved[2 * PAD : 3 * PAD]
    for side in range(SIDES):
        outs[side][...] = moved[:, side * cap : (side + 1) * cap]
    coarse = inverse.shape[1]
    padded = coarse // mode_count * PAD
    old = lax.broadcasted_iota(jnp.int32, (coarse, padded), 0)
    new = lax.broadcasted_iota(jnp.int32, (coarse, padded), 1)
    spread = jnp.where((old // mode_count) * PAD + old % mode_count == new, 1.0, 0.0)
    blank = jnp.zeros((PAD - mode_count, coarse), jnp.float32)
    wide = exact(jnp.concatenate([inverse[...], blank], axis=0), spread)
    blank = jnp.zeros((PAD - mode_count, load.shape[1]), jnp.float32)
    loads = jnp.concatenate([load[...], blank], axis=0)
    copies(outs[SIDES], jnp.concatenate([wide, loads], axis=1))
    outs[SIDES + 1][...] = codes_lanes
    outs[SIDES + 2][...] = jnp.concatenate([upper, lower], axis=0)


def around(i, j):
    right, up = 1 - 2 * (i % 2), 1 - 2 * (j % 2)
    return [(i, j), (i + right, j), (i - right, j), (i, j + up), (i, j - up)]


def mode_blocks(own, partner):
    cap = own[0].shape[1]
    rows = []
    for side in range(SIDES):
        column = [own[side][...]]
        for other in range(SIDES):
            if other == side:
                column.append(-partner[side][...])
            else:
                column.append(jnp.zeros((PAD, cap), jnp.float32))
        rows.append(jnp.concatenate(column, axis=0))
    return rows


def lane_spread(mode_count, lanes):
    shape = (PAD * (SIDES + 1), lanes)
    old = lax.broadcasted_iota(jnp.int32, shape, 0)
    new = lax.broadcasted_iota(jnp.int32, shape, 1)
    spot = (old // PAD) * mode_count + old % PAD
    match = (spot == new % GROUP) & (old % PAD < mode_count)
    return jnp.where(match, 1.0, 0.0)


def operators_kernel(mode_count, flex, schur, codes_row, codes_lanes, *refs):
    own, partner = refs[0:4], refs[4:8]
    outs = refs[8:12]
    modes_out = refs[12]
    slot_pieces, row_pieces, out_pieces = refs[13:16]
    schur = fetch(schur, refs[16], refs[17])
    flex = fetch(flex, refs[18], refs[19])
    total = codes_lanes.shape[0]
    cap = total // SIDES
    half = cap // 2
    lanes = 4 * GROUP
    spread = lane_spread(mode_count, lanes)
    for side, block in enumerate(mode_blocks(own, partner)):
        placed = exact(block, spread, ((0,), (0,)))
        first = lax.broadcasted_iota(jnp.int32, placed.shape, 1) < GROUP
        modes_out[side * cap : (side + 1) * cap, :] = jnp.where(first, placed, 0.0)
        fill_pieces(slot_pieces, side * cap, placed)
    group = lax.broadcasted_iota(jnp.int32, (half, lanes), 1) // GROUP

    def write_schur(side, block):
        outs[side][...] = jnp.where(group == 0, block[:half], block[half:])

    def write_flex(side, block):
        mine = jnp.where(group == 2, block[:half], block[half:])
        outs[side][...] = jnp.where(group < 2, outs[side][...], mine)

    apply_local(schur, codes_row, codes_lanes, slot_pieces, row_pieces, out_pieces, write_schur)
    apply_rows(flex, codes_row, row_pieces, out_pieces, write_flex)


def start_kernel(mode_count, layers, flex, gap, codes_row, codes_lanes, *refs):
    slabs = refs[0:4]
    gathered, modes = refs[4:6]
    outs = refs[6:10]
    start_out, inverse_out = refs[10:12]
    slot_pieces, row_pieces, out_pieces = refs[12:15]
    flex = fetch(flex, refs[15], refs[16])
    cap = codes_lanes.shape[0] // SIDES
    wide = gathered.shape[0]
    spread = lane_spread(mode_count, GROUP)
    for n, centre in enumerate(around(lax.axis_index("sub"), lax.axis_index("layer"))):
        rows = []
        for i, j in around(*centre):
            first = jnp.clip(i * layers + j, 0, wide // PAD - 1) * PAD
            rows.append(gathered[pl.ds(pl.multiple_of(first, PAD), PAD), 0:wide])
        table = jnp.concatenate(rows, axis=0)
        inverse_out[n * GROUP : (n + 1) * GROUP, :] = exact(spread, table, ((0,), (0,)))
    coefficients = repeated(exact(inverse_out[0:GROUP, :], gathered[:, wide:]))
    start = three_pass(modes[...], coefficients)
    start_out[...] = start
    fill_pieces(slot_pieces, 0, start)

    def write(side, block):
        outs[side][0:cap, :] = block
        outs[side][cap:, :] = slabs[side][...]

    apply_local(flex, codes_row, codes_lanes, slot_pieces, row_pieces, out_pieces, write, gap)


def repeated(x):
    return jnp.concatenate([x] * 4, axis=0)


def components_of(own_pieces, block_pieces):
    both = one_pass(own_pieces[...].astype(jnp.bfloat16), block_pieces[...])
    cols = both.shape[1] // 2
    return halves(both[0:PAD]) + both[PAD:, :cols]


def grouped(slab, first):
    group = lax.broadcasted_iota(jnp.int32, slab.shape, 1) // GROUP
    upper = jnp.where(group == first, slab, 0.0)
    lower = jnp.where(group == first + 1, slab, 0.0)
    return jnp.concatenate([upper, lower], axis=0)


def lagged(side, first, mine, theirs, coefficients):
    left = jnp.concatenate([grouped(mine, first), grouped(theirs, first)], axis=1)
    near = coefficients[(side + 1) * GROUP : (side + 2) * GROUP]
    return three_pass(left, jnp.concatenate([repeated(coefficients[0:GROUP]), repeated(-near)], axis=0))


def first_kernel(schur, codes_row, codes_lanes, *refs):
    received, sent, own = refs[0:4], refs[4:8], refs[8]
    outs = refs[9:13]
    gap_out, parts_out, mine_out, theirs_out = refs[13:17]
    slot_pieces, row_pieces, out_pieces = refs[17:20]
    schur = fetch(schur, refs[20], refs[21])
    half = sent[0].shape[0] - codes_lanes.shape[0] // SIDES
    cap = codes_lanes.shape[0] // SIDES
    for side in range(SIDES):
        block = sent[side][0:cap, :] - received[side][0:cap, :]
        gap_out[side * cap : (side + 1) * cap, :] = block
        fill_pieces(slot_pieces, side * cap, block)
        mine_out[side * half : (side + 1) * half, :] = sent[side][cap:, :]
        theirs_out[side * half : (side + 1) * half, :] = received[side][cap:, :]
    copies(parts_out, components_of(own, slot_pieces))

    def write(side, block):
        outs[side][...] = block

    apply_local(schur, codes_row, codes_lanes, slot_pieces, row_pieces, out_pieces, write)


def stage_kernel(stage, matrix, codes_row, codes_lanes, *refs):
    refs = list(refs)

    def take(count):
        taken = refs[:count]
        del refs[:count]
        return taken

    received, sent = take(4), take(4)
    mine, theirs, own, gathered, inverse_rows = take(5)
    (state_in,) = take(1) if stage > 2 else [None]
    outs = take(4) if stage < 5 else []
    state_out, parts_out = take(2)
    slot_pieces, row_pieces, out_pieces = take(3)
    if stage < 5:
        matrix = fetch(matrix, *take(2))
    total = codes_lanes.shape[0]
    cap = total // SIDES
    half = mine.shape[0] // SIDES
    coefficients = three_pass(inverse_rows[...], gathered[...])
    for side in range(SIDES):
        rows = slice(side * cap, (side + 1) * cap)
        slab = slice(side * half, (side + 1) * half)
        jump = sent[side][...] - received[side][...]
        first = 0 if stage in (2, 4) else 2
        behind = lagged(side, first, mine[slab, :], theirs[slab, :], coefficients)
        if stage == 2:
            block = 0.5 * (jump - behind)
            state = block
        elif stage == 3:
            block = (jump - behind) / theta_mid
            state = state_in[rows, :] - block
        elif stage == 4:
            block = 0.5 * (jump + behind)
            state = keep_step * state_in[rows, :] + new_step * block
        else:
            block = jump - new_step * behind
            state = state_in[rows, :] - block
        state_out[rows, :] = state
        if stage < 5:
            fill_pieces(slot_pieces, side * cap, state)
        fill_pieces(out_pieces, side * cap, block)
    copies(parts_out, components_of(own, out_pieces))
    if stage < 5:

        def write(side, block):
            outs[side][...] = block

        apply_local(matrix, codes_row, codes_lanes, slot_pieces, row_pieces, out_pieces, write)


def direct_of(modes, gathered, inverse_rows):
    coefficients = three_pass(inverse_rows[0:GROUP, :], gathered[...])
    return three_pass(modes[...], repeated(coefficients))


def update_kernel(stage, state, modes, gathered, inverse_rows, after, out):
    direct = direct_of(modes, gathered, inverse_rows)
    if stage == 2:
        out[...] = state[...] - direct
    elif stage == 3:
        out[...] = (state[...] - direct) / theta_mid
    else:
        out[...] = state[...] + direct


def rows_kernel(codes_lanes, residual, raw_step, start, step, modes, gathered, inverse_rows, *refs):
    targets, pieces = refs[0:3], refs[3]
    total, cols = residual.shape
    cap = total // SIDES
    direct = direct_of(modes, gathered, inverse_rows)
    multipliers = raw_step[...] - new_step * direct + start[...] + step[...]
    for n, source in enumerate((residual[...], multipliers, modes[...])):
        high, low = two_pieces(source)
        pieces[:, 2 * n * cols : (2 * n + 1) * cols] = high
        pieces[:, (2 * n + 1) * cols : (2 * n + 2) * cols] = low

    def chunk(c, carry):
        here = pl.ds(pl.multiple_of(c * cap, 16), cap)
        rows = one_pass(row_by_slot(codes_lanes[here, :], total), pieces[...])
        for n, target in enumerate(targets):
            target[here, :] = halves(rows[:, 2 * n * cols : (2 * n + 2) * cols])
        return carry

    lax.fori_loop(0, SIDES, chunk, 0)


def last_kernel(residual, modes, gathered, inverse_rows, out):
    coefficients = repeated(three_pass(inverse_rows[0:GROUP, :], gathered[...]))
    out[...] = residual[...] + three_pass(modes[...], coefficients)


def call(kernel, name, outs, inputs, scratch=(), smem=(), left=(), flops=None, room=58):
    spaces = [pltpu.VMEM] * len(inputs)
    for n in smem:
        spaces[n] = pltpu.SMEM
    for n in left:
        spaces[n] = pl.ANY
    shapes = []
    for shape in outs:
        shapes.append(jax.ShapeDtypeStruct(shape, jnp.float32) if isinstance(shape, tuple) else shape)
    return pl.pallas_call(
        kernel,
        name=name,
        out_shape=shapes,
        in_specs=[pl.BlockSpec(memory_space=space) for space in spaces],
        out_specs=[pl.BlockSpec(memory_space=pltpu.VMEM)] * len(outs),
        scratch_shapes=list(scratch),
        cost_estimate=None
        if flops is None
        else pl.CostEstimate(flops=flops, bytes_accessed=16 * inputs[0].size, transcendentals=0),
        compiler_params=pltpu.CompilerParams(vmem_limit_bytes=room * 1024 * 1024),
    )(*inputs)


def exchange(blocks):
    received = []
    for side, block in enumerate(blocks):
        axis = "sub" if side < 2 else "layer"
        pairs = []
        for i in range(side % 2, lax.axis_size(axis) - 1, 2):
            pairs += [(i, i + 1), (i + 1, i)]
        received.append(lax.ppermute(block, axis, pairs))
    return received


def everywhere(stacked):
    return lax.all_to_all(stacked, ("sub", "layer"), split_axis=0, concat_axis=0, tiled=True)


def per_device(
    local_gap, route_codes, flexibility, dirichlet, rigid_modes, coarse_inverse, rigid_load
):
    gap = local_gap[0, 0]
    flex = flexibility[0, 0]
    schur = dirichlet[0, 0]
    mode_count, total = rigid_modes.shape[2:]
    modes = rigid_modes.reshape(mode_count, 1, total)
    cap = total // SIDES
    cols = gap.shape[1]
    layers = lax.axis_size("layer")
    wide = lax.axis_size("sub") * layers * PAD
    pieces = pltpu.VMEM((total, 2 * cols), jnp.bfloat16)
    scratch = [pieces] * 3
    block = [(cap, cols)] * SIDES
    whole = (total, cols)
    parts = (wide, cols)
    brought = [pltpu.VMEM((total, total), jnp.float32), pltpu.SemaphoreType.DMA((SIDES,))]

    shown = call(
        functools.partial(modes_kernel, mode_count),
        "modes_to_slots",
        [(PAD, cap)] * SIDES
        + [(wide, wide + cols), jax.ShapeDtypeStruct((total, 128), jnp.int32), (2 * PAD, total)]
        + [jax.ShapeDtypeStruct((1, total), jnp.int32)],
        [route_codes[0], modes, coarse_inverse, rigid_load],
    )
    own, (inverse_load, codes_lanes, own_pieces, codes_row) = shown[:4], shown[4:]
    gathered = everywhere(inverse_load)
    partner = exchange(own)
    shown = call(
        functools.partial(operators_kernel, mode_count),
        "operators_on_modes",
        [(cap // 2, 4 * GROUP)] * SIDES + [(total, 4 * GROUP)],
        [flex, schur, codes_row, codes_lanes, *own, *partner],
        scratch + brought * 2,
        left=(0, 1),
    )
    slabs, slot_modes = shown[:4], shown[4]
    shown = call(
        functools.partial(start_kernel, mode_count, layers),
        "start",
        [(cap + cap // 2, cols)] * SIDES + [whole, (5 * GROUP, wide)],
        [flex, gap, codes_row, codes_lanes, *slabs, gathered, slot_modes],
        scratch + brought,
        left=(0,),
    )
    sent, (start, inverse_rows) = shown[:4], shown[4:]
    received = exchange(sent)
    shown = call(
        first_kernel,
        "stage_1",
        block + [whole, parts] + [(2 * cap, 4 * GROUP)] * 2,
        [schur, codes_row, codes_lanes, *received, *sent, own_pieces],
        scratch + brought,
        left=(0,),
    )
    sent, (gap_jump, components, mine, theirs) = shown[:4], shown[4:]

    def stage(number, matrix, states_in, sent, components):
        gathered = everywhere(components)
        received = exchange(sent)
        inputs = [codes_row, codes_lanes, *received, *sent, mine, theirs]
        inputs += [own_pieces, gathered, inverse_rows, *states_in]
        outs = [whole, parts]
        kernel = functools.partial(stage_kernel, number)
        name = "stage_%d" % number
        if matrix is None:
            shown = call(functools.partial(kernel, None), name, outs, inputs, scratch)
        else:
            inputs = [matrix] + inputs
            shown = call(kernel, name, block + outs, inputs, scratch + brought, left=(0,))
        return gathered, shown[:-2], *shown[-2:]

    def update(number, state, gathered, after):
        (out,) = call(
            functools.partial(update_kernel, number),
            "update_%d" % number,
            [whole],
            [state, slot_modes, gathered, inverse_rows, after],
            left=(4,),
            flops=8 * total * cols * cols,
        )
        return out

    gathered, sent, precond, components = stage(2, flex, [], sent, components)
    residual = update(2, gap_jump, gathered, components)
    gathered, sent, residual, components = stage(3, schur, [residual], sent, components)
    step = update(3, precond, gathered, components)
    gathered, sent, raw_step, components = stage(4, flex, [step], sent, components)
    residual = update(4, residual, gathered, components)
    gathered, _, residual, components = stage(5, None, [residual], sent, components)
    last_gathered = everywhere(components)
    residual, multipliers, row_modes = call(
        rows_kernel,
        "slots_to_rows",
        [whole, whole, (total, 4 * GROUP)],
        [codes_lanes, residual, raw_step, start, step, slot_modes, gathered, inverse_rows],
        [pltpu.VMEM((total, 6 * cols), jnp.bfloat16)],
    )
    gathered = last_gathered
    (residual,) = call(
        last_kernel,
        "residual",
        [whole],
        [residual, row_modes, gathered, inverse_rows],
    )
    return (multipliers[None, None], residual[None, None])


def solution(mesh):
    placed = (
        P("sub", "layer", None, None),
        P("sub", "layer", None),
        P("sub", "layer", None, None),
        P("sub", "layer", None, None),
        P("sub", "layer", None, None),
        P(("sub", "layer"), None),
        P(("sub", "layer"), None),
    )
    return jax.shard_map(
        per_device,
        mesh=mesh,
        in_specs=placed,
        out_specs=(P("sub", "layer", None, None), P("sub", "layer", None, None)),
        check_vma=False,
    )
```
